32 devices in a mesh: context: 4 (over y, core), experts: 8 (over z, x).
Axes of the slice: x: 2, y: 2, z: 4, core: 2. Of those that a mesh axis runs over, the one named last changes fastest.
Arguments:
- tokens: bfloat16 [4096, 2048], P(('context', 'experts')), may hold values from -6 to 6
- attn_gain: bfloat16 [2048], P(('context', 'experts')), may hold values from 0.5 to 1.5
- query_key_value_weight: bfloat16 [2048, 3072], P(('context', 'experts')), may hold values from -0.125 to 0.125
- out_weight: bfloat16 [2048, 2048], P(('context', 'experts')), may hold values from -3 to 3
- ffn_gain: bfloat16 [2048], P(('context', 'experts')), may hold values from 0.5 to 1.5
- router_weight: bfloat16 [2048, 16], P(('context', 'experts')), may hold values from -0.0625 to 0.0625
- shared_gate: bfloat16 [2048, 2816], P(('context', 'experts')), may hold values from -0.125 to 0.125
- shared_up: bfloat16 [2048, 2816], P(('context', 'experts')), may hold values from -0.125 to 0.125
- shared_down: bfloat16 [2816, 2048], P(('context', 'experts')), may hold values from -0.109375 to 0.109375
- routed_gate_weight: bfloat16 [16, 2048, 1408], P('experts'), may hold values from -0.125 to 0.125
- routed_up_weight: bfloat16 [16, 2048, 1408], P('experts'), may hold values from -0.125 to 0.125
- routed_down_weight: bfloat16 [16, 1408, 2048], P('experts'), may hold values from -0.875 to 0.875
- routes: int32 [4096, 6], P(('context', 'experts')), may hold values from 0 to 15, all different within a row; in each aligned block of 128 rows (0 to 127, 128 to 255, ...) at most 64 rows name the same one
- cotangent: bfloat16 [4096, 2048], P(('context', 'experts')), may hold values from -6 to 6
Outputs:
- layer_out: bfloat16 [4096, 2048], P(('context', 'experts'))
- tokens_grad: float32 [4096, 2048], P(('context', 'experts'))
- attn_gain_grad: float32 [2048], P(('context', 'experts'))
- qkv_weight_grad: float32 [2048, 3072], P(('context', 'experts'))
- out_weight_grad: float32 [2048, 2048], P(('context', 'experts'))
- ffn_gain_grad: float32 [2048], P(('context', 'experts'))
- router_weight_grad: float32 [2048, 16], P(('context', 'experts'))
- shared_gate_grad: float32 [2048, 2816], P(('context', 'experts'))
- shared_up_grad: float32 [2048, 2816], P(('context', 'experts'))
- shared_down_grad: float32 [2816, 2048], P(('context', 'experts'))
- expert_gate_grad: float32 [16, 2048, 1408], P('experts', 'context')
- expert_up_grad: float32 [16, 2048, 1408], P('experts', 'context')
- expert_down_grad: float32 [16, 1408, 2048], P('experts', None, 'context')
The draws below stay inside these ranges and needn't reach their ends.
Inputs may be any that keep to these rules, and one draw needn't show every extreme that they name: `routes`: each token names 6 different experts. In the 128 rows of one device no expert is named by more than 64 rows, a bound that some block reaches.
All inputs are finite; a program needn't handle non-finite values.
Results may differ from the reference program's by a relative error of at most 0.025.
Values may be sent and summed in bfloat16 or wider, within the bound.
No kernel may reach another device: no remote copies, remote signals or barrier semaphores. Data moves between devices by JAX's collectives and lax.ppermute only.
A program may use at most 512 MiB of HBM per device.

```python
import math
import jax
import jax.numpy as jnp
import numpy as np
from jax import lax

MODEL_DIM = 2048
QUERY_HEADS = 16
KEY_VALUE_HEADS = 4
HEAD_DIM = 128
EFF = 1408
SFF = 2816
TOP = 6
TOK_DEV = 128
EXPERTS = 16
SEQ = 4096
CAP = 64


def block_scale(key, shape, pieces, smallest, top_value):
    def one(dim, parts):
        heights = jax.random.uniform(jax.random.fold_in(jax.random.fold_in(key, 6), dim), (parts,), jnp.float32, smallest / len(pieces), top_value / len(pieces))
        return jnp.repeat(jnp.exp(heights), shape[dim] // parts).reshape((-1,) + (1,) * (len(shape) - dim - 1))

    factor_of = one(*pieces[0])
    for cut in pieces[1:]:
        factor_of = factor_of * one(*cut)
    return factor_of


def shared_out(stream_key, own, number, rows, number_of, top, limit, slope):
    sequence = jax.random.permutation(stream_key, number_of)
    crowded, usual = shares(number_of, rows * top, limit, slope, True), shares(number_of, rows * top, limit, slope, False)
    places = jnp.arange(number_of)

    def named(tallies, offset_by):
        used = int((tallies > 0).sum())
        fixed = max(1, used // 4)
        passed = fixed + (places - fixed + offset_by * (used - fixed)) % max(1, number_of - fixed)
        return jnp.zeros((number_of,), jnp.int32).at[sequence[jnp.where(places < fixed, places, passed)]].set(jnp.asarray(tallies, jnp.int32))

    tallies = jnp.where(number % 4 == 0, named(crowded, number // 4), named(usual, number - number // 4 - 1))
    mixed = jax.random.permutation(jax.random.fold_in(own, 3), number_of)
    source_of, taker = mixed[0:number_of // 2 * 2:2], mixed[1:number_of // 2 * 2:2]
    margin = jnp.minimum(tallies[source_of] - 1, limit - tallies[taker]) // 2
    margin = jnp.where((source_of == sequence[0]) | (taker == sequence[0]) | (tallies[taker] == 0), 0, jnp.maximum(margin, 0))
    passed = jax.random.randint(jax.random.fold_in(own, 4), (number_of // 2,), 0, 1 << 20) % (margin + 1)
    tallies = tallies.at[source_of].add(-passed).at[taker].add(passed)
    members = jnp.searchsorted(jnp.cumsum(tallies), jnp.arange(rows * top), side="right").astype(jnp.int32)
    grid = members.reshape(top, rows).T
    grid = grid[jax.random.permutation(jax.random.fold_in(own, 1), rows)]
    offset_by = jax.random.randint(jax.random.fold_in(own, 2), (rows, 1), 0, top)
    return jnp.take_along_axis(grid, (jnp.arange(top)[None, :] + offset_by) % top, axis=1)


def shares(number_of, total, most, lean, full):
    weights = [(1 << 20) // math.isqrt(standing ** lean) + 1 for standing in range(1, number_of + 1)]
    largest = most if full else min(most, max(-(-total // number_of), total * weights[0] // sum(weights)))
    least = 1 if total - largest >= number_of - 1 else 0
    given, spare = [largest] + [least] * (number_of - 1), total - largest - least * (number_of - 1)
    while spare > 0:
        candidates = [i for i in range(1, number_of) if given[i] < largest] or [i for i in range(1, number_of) if given[i] < most]
        whole, remaining = sum([weights[i] for i in candidates]), spare
        for i in candidates:
            more = min(most - given[i], max(1, remaining * weights[i] // whole), spare)
            given[i] = given[i] + more
            spare = spare - more
    return np.array(given)


def scatter_about(own_key, shape, width, most, split=(), held_as=jnp.bfloat16):
    entries = jax.random.normal(own_key, shape, jnp.float32) * width
    if len(split) > 0:
        entries = block_scale(own_key, shape, split, -0.22, 0.18) * entries
    return jnp.clip(entries, min=-most, max=most).astype(held_as)


def setup_inputs(seed: int = 0) -> dict:
    streams_of = jax.random.split(jax.random.key(seed), 15)
    tokens = scatter_about(streams_of[0], (SEQ, MODEL_DIM), 1.0, 6.0, ((0, 32),))
    attn_gain = jnp.clip(1.0 + 0.1 * jax.random.normal(streams_of[1], (MODEL_DIM,), jnp.float32), 0.5, 1.5).astype(jnp.bfloat16)
    query_key_value_weight = scatter_about(streams_of[2], (MODEL_DIM, (QUERY_HEADS + 2 * KEY_VALUE_HEADS) * HEAD_DIM), MODEL_DIM ** -0.5, 0.125, ((0, 32),))
    out_weight = scatter_about(streams_of[3], (QUERY_HEADS * HEAD_DIM, MODEL_DIM), ((SEQ // 8) ** 0.5 * (QUERY_HEADS * HEAD_DIM) ** -0.5), 3.0, ((0, 32),))
    ffn_gain = jnp.clip(1.0 + 0.1 * jax.random.normal(streams_of[4], (MODEL_DIM,), jnp.float32), 0.5, 1.5).astype(jnp.bfloat16)
    router_weight = scatter_about(streams_of[5], (MODEL_DIM, EXPERTS), (4 * MODEL_DIM) ** -0.5, 0.0625, ((0, 32),))
    shared_gate = scatter_about(streams_of[6], (MODEL_DIM, SFF), MODEL_DIM ** -0.5, 0.125, ((0, 32),))
    shared_up = scatter_about(streams_of[7], (MODEL_DIM, SFF), MODEL_DIM ** -0.5, 0.125, ((0, 32),))
    shared_down = scatter_about(streams_of[8], (SFF, MODEL_DIM), SFF ** -0.5, 0.109375, ((0, 32),))
    routed_gate_weight = scatter_about(streams_of[9], (EXPERTS, MODEL_DIM, EFF), MODEL_DIM ** -0.5, 0.125, ((0, 8),))
    routed_up_weight = scatter_about(streams_of[10], (EXPERTS, MODEL_DIM, EFF), MODEL_DIM ** -0.5, 0.125, ((0, 8),))
    routed_down_weight = scatter_about(streams_of[11], (EXPERTS, EFF, MODEL_DIM), (EFF // 32) ** -0.5, 0.875, ((0, 8),))
    routes_keys = jax.random.split(jax.random.fold_in(streams_of[12], 1), SEQ // TOK_DEV)
    routes_turns = jax.random.permutation(jax.random.fold_in(streams_of[12], 3), SEQ // TOK_DEV)
    routes = jax.vmap(lambda own, number: shared_out(jax.random.fold_in(streams_of[12], 2), own, number, TOK_DEV, EXPERTS, TOP, CAP, 1))(routes_keys, routes_turns).reshape((SEQ, TOP))
    cotangent = scatter_about(streams_of[13], (SEQ, MODEL_DIM), 1.0, 6.0, ((0, 32),))
    return dict(tokens=tokens, attn_gain=attn_gain, query_key_value_weight=query_key_value_weight, out_weight=out_weight, ffn_gain=ffn_gain, router_weight=router_weight, shared_gate=shared_gate, shared_up=shared_up, shared_down=shared_down, routed_gate_weight=routed_gate_weight, routed_up_weight=routed_up_weight, routed_down_weight=routed_down_weight, routes=routes, cotangent=cotangent)


@jax.custom_vjp
def lower_precision(v):
    return lax.optimization_barrier(v.astype(jnp.bfloat16)).astype(jnp.float32)

@jax.custom_vjp
def low_back(v):
    return v

def low_keep(v):
    return (lower_precision(v), None)

def low_pass(kept, grad):
    return (grad,)

def back_keep(v):
    return (v, None)

def back_low(kept, grad):
    return (lower_precision(grad),)
lower_precision.defvjp(low_keep, low_pass)
low_back.defvjp(back_keep, back_low)
EPSILON = 1e-06
THETA = 10000.0
NEG_LARGE = -1e+30

def matmul(left, right):
    return jnp.dot(left, right, precision=lax.Precision.HIGHEST, preferred_element_type=jnp.float32)

def rms_scale(values):
    return lax.rsqrt(lax.optimization_barrier(jnp.mean(values * values, axis=-1, keepdims=True)) + EPSILON)

def rotate_halves(values, token_position, direction):
    half_width = values.shape[-1] // 2
    frequency = THETA ** (-jnp.arange(half_width, dtype=jnp.float32) * 2.0 / values.shape[-1])
    angles = token_position[:, None] * frequency[None, :]
    cosine = jnp.cos(angles)[:, None, :]
    sine_part = direction * jnp.sin(angles)[:, None, :]
    first = values[..., :half_width]
    second = values[..., half_width:]
    return jnp.concatenate([first * cosine - second * sine_part, second * cosine + first * sine_part], axis=-1)

def attend(query_rows, key_row_set, value_row_set):
    sequence_length = query_rows.shape[0]
    query_group_width = QUERY_HEADS // KEY_VALUE_HEADS
    block_row_span = math.gcd(sequence_length, 512)
    query_group_count = query_rows.reshape(sequence_length // block_row_span, block_row_span, KEY_VALUE_HEADS, query_group_width, HEAD_DIM)
    block_starts = jnp.arange(sequence_length // block_row_span, dtype=jnp.int32) * block_row_span
    key_pos = jnp.arange(sequence_length, dtype=jnp.int32)
    score_scale = HEAD_DIM ** (-0.5)

    def one_block(packed):
        query_block, block_start = packed
        scores = jnp.einsum('ikgh,jkh->kgij', query_block, key_row_set, precision=lax.Precision.HIGHEST) * score_scale
        scores = low_back(scores)
        query_pos = block_start + jnp.arange(block_row_span, dtype=jnp.int32)
        visible = query_pos[:, None] >= key_pos[None, :]
        scores = jnp.where(visible, scores, NEG_LARGE)
        weights = lower_precision(jax.nn.softmax(scores, axis=-1))
        return jnp.einsum('kgij,jkh->ikgh', weights, value_row_set, precision=lax.Precision.HIGHEST)
    result = lax.map(jax.checkpoint(one_block), (query_group_count, block_starts))
    return result.reshape(sequence_length, QUERY_HEADS * HEAD_DIM)

def experts_out(normed, routes, weight_gate, weight_up, weight_down):
    sequence_length = normed.shape[0]
    block_count = sequence_length // TOK_DEV
    flat_ids = routes.reshape(block_count, TOK_DEV * TOP)
    onehot = (flat_ids[:, :, None] == jnp.arange(EXPERTS, dtype=jnp.int32)[None, None, :]).astype(jnp.int32)
    slot_index = lax.optimization_barrier(jnp.sum((jnp.cumsum(onehot, axis=1) - onehot) * onehot, axis=2))
    rows_per = block_count * CAP
    where_to = flat_ids * rows_per + jnp.arange(block_count, dtype=jnp.int32)[:, None] * CAP + slot_index
    token_ids = (jnp.arange(sequence_length * TOP, dtype=jnp.int32) // TOP).reshape(block_count, TOK_DEV * TOP)
    source = jnp.full((EXPERTS * rows_per,), sequence_length, jnp.int32).at[where_to.reshape(-1)].set(token_ids.reshape(-1))
    padded = jnp.concatenate([normed, jnp.zeros((1, normed.shape[1]), normed.dtype)], axis=0)

    def one_expert(packed):
        gate_mat, up_mat, down_mat, source_rows = packed
        expert_row_set = padded[source_rows]
        gate_pre = low_back(matmul(expert_row_set, gate_mat))
        up_pre = low_back(matmul(expert_row_set, up_mat))
        activated_rows = lower_precision(jax.nn.silu(gate_pre) * up_pre)
        return lower_precision(low_back(matmul(activated_rows, down_mat)))
    result = lax.map(jax.checkpoint(one_expert), (weight_gate, weight_up, weight_down, source.reshape(EXPERTS, rows_per)))
    return (result.reshape(EXPERTS * rows_per, normed.shape[1]), where_to.reshape(sequence_length, TOP))

def forward(inputs, attn_gain, query_key_value_weight, out_weight, ffn_gain, router_weight, shared_gate, shared_up, shared_down, routed_gate_weight, routed_up_weight, routed_down_weight, routes):
    sequence_length = inputs.shape[0]
    token_position = jnp.arange(sequence_length, dtype=jnp.float32)
    query_width = QUERY_HEADS * HEAD_DIM
    key_width = KEY_VALUE_HEADS * HEAD_DIM
    normed_one = lower_precision(inputs * rms_scale(inputs) * attn_gain)
    projected_rows = low_back(matmul(normed_one, query_key_value_weight))
    query_rows = lower_precision(rotate_halves(projected_rows[:, :query_width].reshape(sequence_length, QUERY_HEADS, HEAD_DIM), token_position, 1.0))
    key_row_set = lower_precision(rotate_halves(projected_rows[:, query_width:query_width + key_width].reshape(sequence_length, KEY_VALUE_HEADS, HEAD_DIM), token_position, 1.0))
    value_row_set = lower_precision(projected_rows[:, query_width + key_width:].reshape(sequence_length, KEY_VALUE_HEADS, HEAD_DIM))
    attended = lower_precision(low_back(attend(query_rows, key_row_set, value_row_set)))
    middle = inputs + low_back(matmul(attended, out_weight))
    normed_two = lower_precision(middle * rms_scale(middle) * ffn_gain)
    router_probs = jax.nn.softmax(low_back(matmul(normed_two, router_weight)), axis=-1)
    gate_values = jnp.take_along_axis(router_probs, routes, axis=1)
    shared_act = lower_precision(jax.nn.silu(low_back(matmul(normed_two, shared_gate))) * low_back(matmul(normed_two, shared_up)))
    mixed = low_back(matmul(shared_act, shared_down))
    result, where_to = experts_out(normed_two, routes, routed_gate_weight, routed_up_weight, routed_down_weight)
    for column in range(TOP):
        mixed = mixed + gate_values[:, column:column + 1] * result[where_to[:, column]]
    return middle + mixed

def reference(tokens, attn_gain, query_key_value_weight, out_weight, ffn_gain, router_weight, shared_gate, shared_up, shared_down, routed_gate_weight, routed_up_weight, routed_down_weight, routes, cotangent):
    floats = [array.astype(jnp.float32) for array in (tokens, attn_gain, query_key_value_weight, out_weight, ffn_gain, router_weight, shared_gate, shared_up, shared_down, routed_gate_weight, routed_up_weight, routed_down_weight)]

    def layer_fn(*weights):
        return forward(*weights, routes)
    layer_out, pull_back = jax.vjp(layer_fn, *floats)
    grads = pull_back(cotangent.astype(jnp.float32))
    return (layer_out.astype(jnp.bfloat16), grads[0], grads[1], grads[2], grads[3], grads[4], grads[5], grads[6], grads[7], grads[8], grads[9], grads[10], grads[11])
```

```python
import functools
import math

import jax
import jax.numpy as jnp
from jax import lax
from jax.experimental import pallas as pl
from jax.experimental.pallas import tpu as pltpu
from jax.sharding import PartitionSpec as P

QUERY_HEADS = 16
KEY_VALUE_HEADS = 4
HEAD_DIM = 128
TOP = 6


EPSILON = 1e-06
THETA = 10000.0
NEG_LARGE = -1e30


def rms_scale(values):
    return lax.rsqrt(jnp.mean(values * values, axis=-1, keepdims=True) + EPSILON)


def norm_back(values, row_scale, gain_values, grad_out):
    weighted = grad_out * gain_values
    gain_grad = jnp.sum(grad_out * values * row_scale, axis=0)
    inner_mean = jnp.mean(weighted * values, axis=-1, keepdims=True)
    return (
        row_scale * weighted - values * row_scale * row_scale * row_scale * inner_mean,
        gain_grad,
    )


def inner_rows(left, right):
    return lax.dot_general(
        left, right, (((0,), (0,)), ((), ())), preferred_element_type=jnp.float32
    )


def dot_last(left, right):
    return lax.dot_general(
        left, right, (((1,), (1,)), ((), ())), preferred_element_type=jnp.float32
    )


def ring_pairs(count):
    order = [i for i in range(count) if i % 2 == 0] + [i for i in reversed(range(count)) if i % 2 == 1]
    right = [(order[i], order[(i + 1) % count]) for i in range(count)]
    left = [(order[i], order[(i - 1) % count]) for i in range(count)]
    return right, left


def ring_place(index, count):
    return jnp.where(index % 2 == 0, index // 2, count - 1 - index // 2)


def ring_index(place, count):
    place = (place + 2 * count) % count
    return jnp.where(place < count // 2, 2 * place, 2 * (count - 1 - place) + 1)


class RingGather:
    def __init__(self, block):
        self.count = lax.axis_size("experts")
        self.right, self.left = ring_pairs(self.count)
        self.half = block.shape[0] // 2
        self.block = block
        self.ahead = [block]
        self.behind = [block]
        self.far = None

    def step(self):
        if len(self.ahead) < self.count // 2:
            self.behind.append(lax.ppermute(self.behind[-1], "experts", self.right))
            self.ahead.append(lax.ppermute(self.ahead[-1], "experts", self.left))
        else:
            self.far = [
                lax.ppermute(self.behind[-1][: self.half], "experts", self.right),
                lax.ppermute(self.ahead[-1][self.half :], "experts", self.left),
            ]

    def latest(self):
        return self.far if self.far else [self.behind[-1], self.ahead[-1]]

    def replace(self, values):
        if self.far:
            self.far = list(values)
        else:
            self.behind[-1], self.ahead[-1] = values

    def pieces(self):
        return self.ahead + self.far + self.behind[:0:-1]


class RingScatter:
    def __init__(self, whole):
        self.count = lax.axis_size("experts")
        self.right, self.left = ring_pairs(self.count)
        self.whole = whole
        self.rows = whole.shape[0] // self.count
        self.half = self.rows // 2
        self.left_steps = self.count // 2
        self.first = None
        self.second = None

    def own(self, step):
        start = step % self.count * self.rows
        return self.whole[start : start + self.rows].astype(jnp.float32)

    def arrived(self):
        first = self.first.astype(jnp.float32)
        second = self.second.astype(jnp.float32)
        if self.left_steps == self.count // 2 - 1:
            blank = jnp.zeros((self.half, self.whole.shape[1]), jnp.float32)
            first = jnp.concatenate([first, blank], axis=0)
            second = jnp.concatenate([blank, second], axis=0)
        return first, second

    def step(self):
        if self.first is None:
            far = self.own(self.left_steps)
            first, second = far[: self.half], far[self.half :]
        else:
            first, second = self.arrived()
            first = first + self.own(self.left_steps)
            second = second + self.own(-self.left_steps)
        self.first = lax.ppermute(first.astype(jnp.bfloat16), "experts", self.right)
        self.second = lax.ppermute(second.astype(jnp.bfloat16), "experts", self.left)
        self.left_steps -= 1

    def latest(self):
        return [self.first, self.second]

    def replace(self, values):
        self.first, self.second = values

    def total(self):
        first, second = self.arrived()
        return first + second + self.own(0)


def meet(rings, *values):
    held, values = lax.optimization_barrier(([ring.latest() for ring in rings], values))
    for ring, value in zip(rings, held):
        ring.replace(value)
    return values


def ring_order(values):
    count = lax.axis_size("experts")
    place = ring_place(lax.axis_index("experts"), count)
    return jnp.concatenate(
        [
            lax.dynamic_slice_in_dim(values, ring_index(place + step, count), 1, 0)
            for step in range(count)
        ],
        axis=0,
    )


def flip_pairs(count, bit):
    return [(i, i ^ bit) for i in range(count)]


def flip_gather(block, axis):
    count = lax.axis_size(axis)
    index = lax.axis_index(axis)
    whole = block[None]
    bit = 1
    while bit < count:
        received = lax.ppermute(whole, axis, flip_pairs(count, bit))
        whole = jnp.where(
            (index // bit) % 2 == 0,
            jnp.concatenate([whole, received], axis=0),
            jnp.concatenate([received, whole], axis=0),
        )
        bit *= 2
    return whole


def flip_scatter(values, axis):
    count = lax.axis_size(axis)
    index = lax.axis_index(axis)
    bit = 1
    while bit < count:
        pairs = values.reshape((values.shape[0] // 2, 2) + values.shape[1:])
        mine = (index // bit) % 2
        sent = lax.dynamic_index_in_dim(pairs, 1 - mine, 1, keepdims=False)
        kept = lax.dynamic_index_in_dim(pairs, mine, 1, keepdims=False)
        values = kept + lax.ppermute(sent, axis, flip_pairs(count, bit))
        bit *= 2
    return values[0]


def context_gather(block):
    count = lax.axis_size("context")
    index = lax.axis_index("context")
    whole = block[None]
    bit = count // 2
    while bit >= 1:
        received = lax.ppermute(whole, "context", flip_pairs(count, bit))
        low = (index // bit) % 2 == 0
        whole = jnp.stack(
            [jnp.where(low, whole, received), jnp.where(low, received, whole)], axis=1
        ).reshape((2 * whole.shape[0],) + block.shape)
        bit //= 2
    return whole.reshape(count * block.shape[0], block.shape[1])


def core_parts(piece_of):
    count = lax.axis_size("context")
    index = lax.axis_index("context")
    return {place: piece_of(index ^ (place + 1)) for place in range(count - 2, -1, -2)}


def core_exchange(parts):
    pairs = flip_pairs(lax.axis_size("context"), 1)
    return {
        place: lax.ppermute(part.astype(jnp.bfloat16), "context", pairs)
        for place, part in parts.items()
    }


def core_sums(piece_of, received):
    index = lax.axis_index("context")
    return {
        place // 2: piece_of(index ^ place, part) for place, part in received.items()
    }


def far_sums(pieces):
    count = lax.axis_size("context")
    bit = 2
    while bit < count:
        merged = {}
        for place in sorted(pieces, reverse=True):
            if place % 2 == 0:
                received = lax.ppermute(
                    pieces[place + 1].astype(jnp.bfloat16), "context", flip_pairs(count, bit)
                )
                merged[place // 2] = pieces[place] + received.astype(jnp.float32)
        pieces = merged
        bit *= 2
    return pieces[0]


def block_sums(values, received):
    def piece_of(target, part):
        return lax.dynamic_index_in_dim(values, target, 0, keepdims=False) + part.astype(jnp.float32)

    return core_sums(piece_of, received)


def block_parts(values):
    return core_parts(lambda target: lax.dynamic_index_in_dim(values, target, 0, keepdims=False))


def to_experts(stacked):
    return lax.all_to_all(stacked, "experts", split_axis=0, concat_axis=0, tiled=True)


VMEM_BYTES = 60 * 1024 * 1024


def kernel_options():
    return dict(
        compiler_params=pltpu.CompilerParams(vmem_limit_bytes=VMEM_BYTES),
        cost_estimate=pl.CostEstimate(flops=1024, bytes_accessed=1024, transcendentals=0),
    )


def in_vmem(count):
    return [pl.BlockSpec(memory_space=pltpu.VMEM)] * count


def in_smem(count):
    return [pl.BlockSpec(memory_space=pltpu.SMEM)] * count


def plain_dot(left, right):
    return jnp.dot(left, right, preferred_element_type=jnp.float32)


def last_dims(left, right):
    return lax.dot_general(
        left, right, (((1,), (1,)), ((), ())), preferred_element_type=jnp.float32
    )


def first_dims(left, right):
    return lax.dot_general(
        left, right, (((0,), (0,)), ((), ())), preferred_element_type=jnp.float32
    )


def project_kernel(piece_count, *refs):
    pieces = refs[:piece_count]
    gain_ref, weight_ref, cosine_ref, sine_ref, normed_ref, query_ref, key_value_ref = refs[piece_count:]
    start = 0
    for piece in pieces:
        rows = piece.shape[0]
        values = piece[...].astype(jnp.float32)
        scale = lax.rsqrt(jnp.mean(values * values, axis=-1, keepdims=True) + EPSILON)
        normed_ref[start : start + rows, :] = (values * scale * gain_ref[...]).astype(jnp.bfloat16)
        start += rows
    step = math.gcd(start, 512)
    query_width = query_ref.shape[1]

    @pl.loop(0, start // step)
    def _(index):
        here = pl.ds(pl.multiple_of(index * step, step), step)
        normed = normed_ref[here, :]
        cosine = cosine_ref[here, :]
        sine = sine_ref[here, :]

        def rotated(offset):
            head = heads[:, offset : offset + HEAD_DIM]
            return (head * cosine + pltpu.roll(head, HEAD_DIM // 2, 1) * sine).astype(jnp.bfloat16)

        heads = plain_dot(normed, weight_ref[:, :query_width])
        for offset in range(0, query_width, HEAD_DIM):
            query_ref[here, offset : offset + HEAD_DIM] = rotated(offset)
        heads = plain_dot(normed, weight_ref[:, query_width:])
        key_value_ref[here, :HEAD_DIM] = rotated(0)
        key_value_ref[here, HEAD_DIM:] = heads[:, HEAD_DIM:].astype(jnp.bfloat16)


def project(pieces, gain, weight, cosine, sine, query_width):
    rows = sum(piece.shape[0] for piece in pieces)
    width = pieces[0].shape[1]
    return pl.pallas_call(
        functools.partial(project_kernel, len(pieces)),
        out_shape=(
            jax.ShapeDtypeStruct((rows, width), jnp.bfloat16),
            jax.ShapeDtypeStruct((rows, query_width), jnp.bfloat16),
            jax.ShapeDtypeStruct((rows, weight.shape[1] - query_width), jnp.bfloat16),
        ),
        in_specs=in_vmem(len(pieces) + 4),
        out_specs=tuple(in_vmem(3)),
        **kernel_options(),
    )(*pieces, gain, weight, cosine, sine)


def stack_heads(values):
    heads = values.shape[1] // HEAD_DIM
    return jnp.concatenate(
        [values[:, i * HEAD_DIM : (i + 1) * HEAD_DIM] for i in range(heads)], axis=0
    )


def spread_heads(values, heads):
    rows = values.shape[0] // heads
    return jnp.concatenate([values[i * rows : (i + 1) * rows] for i in range(heads)], axis=1)


def stack_lanes(values):
    return jnp.concatenate([values[i : i + 1] for i in range(values.shape[0])], axis=1)


def visible_keys(shape, key_start, query_start, query_tile):
    key_pos = key_start + lax.broadcasted_iota(jnp.int32, shape, 0)
    query_pos = query_start + lax.rem(lax.broadcasted_iota(jnp.int32, shape, 1), query_tile)
    return query_pos >= key_pos


def ring_slices(order_ref, rows, first, count):
    spread = order_ref.shape[0]
    length = rows // spread
    found = []
    for i in range(count):
        number = first + i
        base = lax.div(number, spread) * rows
        place = order_ref[lax.rem(number, spread)] * length
        found.append(pl.ds(pl.multiple_of(base + place, length), length))
    return found


def forward_kernel(
    query_tile, key_tile, block_ref, order_ref, query_ref, key_value_ref, out_ref, low_ref, ring_ref, total_ref
):
    rows = query_ref.shape[0]
    length = rows // order_ref.shape[0]
    heads = query_ref.shape[1] // HEAD_DIM
    wide = heads * query_tile
    scale = HEAD_DIM ** (-0.5) * math.log2(math.e)

    @pl.loop(0, rows // query_tile)
    def _(index):
        offset = pl.multiple_of(index * query_tile, query_tile)
        places = ring_slices(order_ref, rows, index * (query_tile // length), query_tile // length)
        queries = stack_heads(jnp.concatenate([query_ref[place, :] for place in places], axis=0))
        start = block_ref[0] * rows + offset

        def step(tile, state, masked):
            top, total, summed = state
            here = ring_slices(order_ref, rows, tile * (key_tile // length), key_tile // length)
            keys = jnp.concatenate([key_value_ref[place, :HEAD_DIM] for place in here], axis=0)
            values = jnp.concatenate([key_value_ref[place, HEAD_DIM:] for place in here], axis=0)
            scores = last_dims(keys, queries) * scale
            if masked:
                seen = visible_keys(scores.shape, tile * key_tile, start, query_tile)
                scores = jnp.where(seen, scores, NEG_LARGE)
            new_top = jnp.maximum(top, jnp.max(scores, axis=0, keepdims=True))
            weights = jnp.exp2(scores - new_top)
            rescale = jnp.exp2(top - new_top)
            total = total * rescale + jnp.sum(weights, axis=0, keepdims=True)
            summed = summed * rescale + first_dims(values, weights.astype(jnp.bfloat16))
            return new_top, total, summed

        state = (
            jnp.full((1, wide), NEG_LARGE, jnp.float32),
            jnp.zeros((1, wide), jnp.float32),
            jnp.zeros((HEAD_DIM, wide), jnp.float32),
        )
        full = lax.div(start, key_tile)
        state = lax.fori_loop(0, full, lambda tile, state: step(tile, state, False), state)
        top, total, summed = step(full, state, True)
        result = spread_heads((summed / total).T, heads)
        out_ref[pl.ds(offset, query_tile), :] = result
        low = result.astype(jnp.bfloat16)
        low_ref[pl.ds(offset, query_tile), :] = low
        for i, place in enumerate(places):
            ring_ref[place, :] = low[i * length : (i + 1) * length]
        log_total = top + jnp.log2(total)
        for i in range(heads):
            total_ref[i : i + 1, pl.ds(offset, query_tile)] = log_total[
                :, i * query_tile : (i + 1) * query_tile
            ]


def backward_kernel(
    query_tile,
    key_tile,
    block_ref,
    order_ref,
    query_ref,
    key_value_ref,
    out_ref,
    grad_ref,
    total_ref,
    cosine_ref,
    sine_ref,
    query_grad_ref,
    key_value_grad_ref,
):
    rows = query_ref.shape[0]
    length = rows // order_ref.shape[0]
    heads = query_ref.shape[1] // HEAD_DIM
    wide = heads * query_tile
    score_scale = HEAD_DIM ** (-0.5)
    scale = score_scale * math.log2(math.e)

    @pl.loop(0, key_value_ref.shape[0] // key_tile)
    def _(tile):
        key_start = pl.multiple_of(tile * key_tile, key_tile)
        key_value_grad_ref[pl.ds(key_start, key_tile), :] = jnp.zeros(
            (key_tile, 2 * HEAD_DIM), jnp.float32
        )

    @pl.loop(0, rows // query_tile)
    def _(index):
        offset = pl.multiple_of(index * query_tile, query_tile)
        places = ring_slices(order_ref, rows, index * (query_tile // length), query_tile // length)
        queries = stack_heads(jnp.concatenate([query_ref[place, :] for place in places], axis=0))
        grads = stack_heads(grad_ref[pl.ds(offset, query_tile), :])
        outs = stack_heads(out_ref[pl.ds(offset, query_tile), :])
        delta = jnp.sum((grads.astype(jnp.float32) * outs).T, axis=0, keepdims=True)
        log_total = stack_lanes(total_ref[:, pl.ds(offset, query_tile)])
        start = block_ref[0] * rows + offset

        def step(tile, query_grad, masked):
            here = ring_slices(order_ref, rows, tile * (key_tile // length), key_tile // length)
            keys = jnp.concatenate([key_value_ref[place, :HEAD_DIM] for place in here], axis=0)
            values = jnp.concatenate([key_value_ref[place, HEAD_DIM:] for place in here], axis=0)
            weights = jnp.exp2(last_dims(keys, queries) * scale - log_total)
            if masked:
                seen = visible_keys(weights.shape, tile * key_tile, start, query_tile)
                weights = jnp.where(seen, weights, 0.0)
            value_part = plain_dot(weights.astype(jnp.bfloat16), grads)
            score_grad = (weights * (last_dims(values, grads) - delta)).astype(jnp.bfloat16)
            key_part = plain_dot(score_grad, queries) * score_scale
            part = jnp.concatenate([key_part, value_part], axis=1)
            for i, place in enumerate(here):
                key_value_grad_ref[place, :] += part[i * length : (i + 1) * length]
            return query_grad + first_dims(score_grad, keys)

        full = lax.div(start, key_tile)
        query_grad = lax.fori_loop(
            0,
            full,
            lambda tile, state: step(tile, state, False),
            jnp.zeros((wide, HEAD_DIM), jnp.float32),
        )
        query_grad = step(full, query_grad, True) * score_scale
        for i, place in enumerate(places):
            cosine = cosine_ref[place, :]
            sine = sine_ref[place, :]
            for head in range(heads):
                begin = head * query_tile + i * length
                part = query_grad[begin : begin + length]
                turned = part * cosine - pltpu.roll(part, HEAD_DIM // 2, 1) * sine
                query_grad_ref[place, head * HEAD_DIM : (head + 1) * HEAD_DIM] = turned.astype(
                    jnp.bfloat16
                )


def attention_forward(block_index, order, queries, keys):
    rows, wide = queries.shape
    return pl.pallas_call(
        functools.partial(forward_kernel, math.gcd(rows, 256), math.gcd(rows, 512)),
        out_shape=(
            jax.ShapeDtypeStruct((rows, wide), jnp.float32),
            jax.ShapeDtypeStruct((rows, wide), jnp.bfloat16),
            jax.ShapeDtypeStruct((rows, wide), jnp.bfloat16),
            jax.ShapeDtypeStruct((wide // HEAD_DIM, rows), jnp.float32),
        ),
        in_specs=in_smem(2) + in_vmem(2),
        out_specs=tuple(in_vmem(4)),
        **kernel_options(),
    )(block_index.reshape(1), order, queries, keys)


def attention_backward(block_index, order, queries, keys, outs, grads, log_total, cosine, sine):
    rows, wide = queries.shape
    return pl.pallas_call(
        functools.partial(backward_kernel, math.gcd(rows, 256), math.gcd(rows, 512)),
        out_shape=(
            jax.ShapeDtypeStruct((rows, wide), jnp.bfloat16),
            jax.ShapeDtypeStruct((keys.shape[0], 2 * HEAD_DIM), jnp.float32),
        ),
        in_specs=in_smem(2) + in_vmem(7),
        out_specs=tuple(in_vmem(2)),
        **kernel_options(),
    )(block_index.reshape(1), order, queries, keys, outs, grads, log_total, cosine, sine)


def dispatch_kernel(piece_count, experts, *refs):
    pieces = refs[:piece_count]
    chosen_ref, whole_ref, rows_ref = refs[piece_count:]
    start = 0
    for piece in pieces:
        whole_ref[start : start + piece.shape[0], :] = piece[...]
        start += piece.shape[0]
    length = chosen_ref.shape[2]
    capacity = chosen_ref.shape[1] // experts
    for block in range(chosen_ref.shape[0]):
        picked = plain_dot(chosen_ref[block], whole_ref[block * length : (block + 1) * length, :])
        picked = picked.astype(jnp.bfloat16)
        for expert in range(experts):
            rows_ref[expert, block * capacity : (block + 1) * capacity, :] = picked[
                expert * capacity : (expert + 1) * capacity
            ]


def dispatch(pieces, chosen, experts):
    rows = sum(piece.shape[0] for piece in pieces)
    width = pieces[0].shape[1]
    blocks, slots, _ = chosen.shape
    return pl.pallas_call(
        functools.partial(dispatch_kernel, len(pieces), experts),
        out_shape=(
            jax.ShapeDtypeStruct((rows, width), jnp.bfloat16),
            jax.ShapeDtypeStruct((experts, blocks * (slots // experts), width), jnp.bfloat16),
        ),
        in_specs=in_vmem(len(pieces) + 1),
        out_specs=tuple(in_vmem(2)),
        **kernel_options(),
    )(*pieces, chosen)


def column_tiles(width, tile, work):
    whole = width // tile

    @pl.loop(0, whole)
    def _(index):
        work(pl.ds(pl.multiple_of(index * tile, tile), tile))

    if width % tile:
        work(pl.ds(whole * tile, width % tile))


def expert_kernel(
    first_ref,
    rows_ref,
    grad_ref,
    gate_ref,
    weight_gate_ref,
    weight_up_ref,
    weight_down_ref,
    act_ref,
    gate_grad_ref,
    up_grad_ref,
    row_grad_ref,
    score_ref,
):
    hidden = act_ref.shape[2]
    width = rows_ref.shape[2]
    score_ref[...] = jnp.zeros_like(score_ref)

    def hidden_work(here):
        rows = rows_ref[0]
        pre_gate = plain_dot(rows, weight_gate_ref[0, :, here])
        pre_up = plain_dot(rows, weight_up_ref[0, :, here])
        act_grad = last_dims(grad_ref[0], weight_down_ref[0, here, :])
        sigmoid = 1.0 / (1.0 + jnp.exp(-pre_gate))
        silu = pre_gate * sigmoid
        act = (silu * pre_up).astype(jnp.bfloat16)
        act_ref[0, :, here] = act
        score_ref[...] += jnp.sum(act.astype(jnp.float32) * act_grad, axis=1, keepdims=True)
        act_grad = act_grad * gate_ref[0]
        gate_grad_ref[0, :, here] = (
            act_grad * pre_up * sigmoid * (1.0 + pre_gate * (1.0 - sigmoid))
        ).astype(jnp.bfloat16)
        up_grad_ref[0, :, here] = (act_grad * silu).astype(jnp.bfloat16)

    column_tiles(hidden, 256, hidden_work)

    @pl.loop(0, width // 256)
    def _(index):
        here = pl.ds(pl.multiple_of(index * 256, 256), 256)
        row_grad_ref[0, :, here] = (
            last_dims(gate_grad_ref[0], weight_gate_ref[0, here, :])
            + last_dims(up_grad_ref[0], weight_up_ref[0, here, :])
        ).astype(jnp.bfloat16)

    lane = lax.broadcasted_iota(jnp.int32, (score_ref.shape[0], HEAD_DIM), 1)
    own = first_ref[0] + pl.program_id(0)
    row_grad_ref[0, :, width:] = jnp.where(lane == own, score_ref[...], 0.0).astype(jnp.bfloat16)


def expert_pass(first_expert, rows, grads, gates, weight_gate, weight_up, weight_down):
    experts, count, width = rows.shape
    hidden = weight_gate.shape[2]

    def one(*shape):
        return pl.BlockSpec((1,) + shape, lambda expert: (expert, 0, 0))

    def low(*shape):
        return jax.ShapeDtypeStruct((experts,) + shape, jnp.bfloat16)

    return pl.pallas_call(
        expert_kernel,
        grid=(experts,),
        out_shape=(
            low(count, hidden),
            low(count, hidden),
            low(count, hidden),
            low(count, width + HEAD_DIM),
        ),
        in_specs=in_smem(1)
        + [
            one(count, width),
            one(count, width),
            one(count, 1),
            one(width, hidden),
            one(width, hidden),
            one(hidden, width),
        ],
        out_specs=(one(count, hidden), one(count, hidden), one(count, hidden), one(count, width + HEAD_DIM)),
        scratch_shapes=[pltpu.VMEM((count, 1), jnp.float32)],
        **kernel_options(),
    )(first_expert.reshape(1), rows, grads, gates, weight_gate, weight_up, weight_down)


def result_kernel(act_ref, gate_ref, weight_ref, out_ref):
    @pl.loop(0, out_ref.shape[2] // 256)
    def _(index):
        here = pl.ds(pl.multiple_of(index * 256, 256), 256)
        result = plain_dot(act_ref[0], weight_ref[0, :, here]).astype(jnp.bfloat16)
        out_ref[0, :, here] = (result.astype(jnp.float32) * gate_ref[0]).astype(jnp.bfloat16)


def expert_results(act, gates, weight_down):
    experts, count, hidden = act.shape
    width = weight_down.shape[2]

    def one(*shape):
        return pl.BlockSpec((1,) + shape, lambda expert: (expert, 0, 0))

    return pl.pallas_call(
        result_kernel,
        grid=(experts,),
        out_shape=jax.ShapeDtypeStruct((experts, count, width), jnp.bfloat16),
        in_specs=[one(count, hidden), one(count, 1), one(hidden, width)],
        out_specs=one(count, width),
        **kernel_options(),
    )(act, gates, weight_down)


def combine_kernel(turned, chosen_ref, values_ref, left_ref, right_ref, out_ref):
    width = right_ref.shape[0] if turned else right_ref.shape[1]
    experts = values_ref.shape[0]
    length = chosen_ref.shape[1]
    capacity = chosen_ref.shape[2] // experts
    blocks = chosen_ref.shape[0]

    def slots(block, here):
        part = 0.0
        for expert in range(experts):
            part = part + plain_dot(
                chosen_ref[block, :, expert * capacity : (expert + 1) * capacity],
                values_ref[expert, block * capacity : (block + 1) * capacity, here],
            )
        return part

    @pl.loop(0, width // 256)
    def _(index):
        here = pl.ds(pl.multiple_of(index * 256, 256), 256)
        shared = (
            last_dims(left_ref[...], right_ref[here, :])
            if turned
            else plain_dot(left_ref[...], right_ref[:, here])
        )
        for block in range(blocks):
            rows = slice(block * length, (block + 1) * length)
            out_ref[rows, here] = (shared[rows] + slots(block, here)).astype(jnp.bfloat16)

    if out_ref.shape[1] > width:
        for block in range(blocks):
            out_ref[block * length : (block + 1) * length, width:] = slots(
                block, slice(width, out_ref.shape[1])
            ).astype(jnp.bfloat16)


def combine(chosen, values, left, right, turned):
    blocks, length, slots = chosen.shape
    experts, _, wide = values.shape
    capacity = slots // experts
    some = math.gcd(blocks, 4)
    return pl.pallas_call(
        functools.partial(combine_kernel, turned),
        grid=(blocks // some,),
        out_shape=jax.ShapeDtypeStruct((blocks * length, wide), jnp.bfloat16),
        in_specs=[
            pl.BlockSpec((some, length, slots), lambda i: (i, 0, 0)),
            pl.BlockSpec((experts, some * capacity, wide), lambda i: (0, i, 0)),
            pl.BlockSpec((some * length, left.shape[1]), lambda i: (i, 0)),
            pl.BlockSpec(right.shape, lambda i: (0, 0)),
        ],
        out_specs=pl.BlockSpec((some * length, wide), lambda i: (i, 0)),
        **kernel_options(),
    )(chosen, values, left, right)


def shared_kernel(normed_ref, grad_ref, weight_ref, down_ref, act_ref, both_ref):
    hidden = act_ref.shape[1]
    pre_gate = plain_dot(normed_ref[...], weight_ref[:, :hidden])
    pre_up = plain_dot(normed_ref[...], weight_ref[:, hidden:])
    act_grad = last_dims(grad_ref[...], down_ref[...])
    sigmoid = 1.0 / (1.0 + jnp.exp(-pre_gate))
    silu = pre_gate * sigmoid
    act_ref[...] = (silu * pre_up).astype(jnp.bfloat16)
    both_ref[:, :hidden] = (
        act_grad * pre_up * sigmoid * (1.0 + pre_gate * (1.0 - sigmoid))
    ).astype(jnp.bfloat16)
    both_ref[:, hidden:] = (act_grad * silu).astype(jnp.bfloat16)


def shared_pass(normed, grads, weight, down):
    rows, width = normed.shape
    hidden = down.shape[0]
    some = math.gcd(rows, 256)

    def part(columns):
        return pl.BlockSpec((some, columns), lambda i: (i, 0))

    return pl.pallas_call(
        shared_kernel,
        grid=(rows // some,),
        out_shape=(
            jax.ShapeDtypeStruct((rows, hidden), jnp.bfloat16),
            jax.ShapeDtypeStruct((rows, 2 * hidden), jnp.bfloat16),
        ),
        in_specs=[
            part(width),
            part(width),
            pl.BlockSpec(weight.shape, lambda i: (0, 0)),
            pl.BlockSpec(down.shape, lambda i: (0, 0)),
        ],
        out_specs=(part(hidden), part(2 * hidden)),
        **kernel_options(),
    )(normed, grads, weight, down)


def piece_kernel(scaled, added, target_ref, left_ref, right_ref, *refs):
    right = right_ref[0]
    if scaled:
        right = (right.astype(jnp.float32) * refs[0][0]).astype(jnp.bfloat16)
    total = first_dims(left_ref[0], right)
    if added:
        total = total + refs[-2][0].astype(jnp.float32)
    refs[-1][0] = total.astype(jnp.bfloat16)


def weight_piece(target, left, right, parts, cut_left, gates=None, received=None):
    experts, count, left_width = left.shape
    right_width = right.shape[2]
    left_width, right_width = (
        (left_width // parts, right_width) if cut_left else (left_width, right_width // parts)
    )

    def spec(columns, cut):
        if cut:
            return pl.BlockSpec((1, count, columns), lambda e, t: (e, 0, t[0]))
        return pl.BlockSpec((1, count, columns), lambda e, t: (e, 0, 0))

    whole = pl.BlockSpec((1, left_width, right_width), lambda e, t: (e, 0, 0))
    operands = [left, right]
    specs = [spec(left_width, cut_left), spec(right_width, not cut_left)]
    if gates is not None:
        operands.append(gates)
        specs.append(pl.BlockSpec((1, count, 1), lambda e, t: (e, 0, 0)))
    if received is not None:
        operands.append(received)
        specs.append(whole)
    return pl.pallas_call(
        functools.partial(piece_kernel, gates is not None, received is not None),
        grid_spec=pltpu.PrefetchScalarGridSpec(
            num_scalar_prefetch=1, grid=(experts,), in_specs=specs, out_specs=whole
        ),
        out_shape=jax.ShapeDtypeStruct((experts, left_width, right_width), jnp.bfloat16),
        **kernel_options(),
    )(target.reshape(1), *operands)


def weight_sum_kernel(piece_count, left_ref, *refs):
    pieces = refs[:piece_count]
    out_ref = refs[piece_count]

    @pl.loop(0, out_ref.shape[1] // 256)
    def _(index):
        here = pl.ds(pl.multiple_of(index * 256, 256), 256)
        right = jnp.concatenate([piece[:, here] for piece in pieces], axis=0)
        out_ref[:, here] = first_dims(left_ref[...], right).astype(jnp.bfloat16)


def weight_sum(left, pieces):
    return pl.pallas_call(
        functools.partial(weight_sum_kernel, len(pieces)),
        out_shape=jax.ShapeDtypeStruct((left.shape[1], pieces[0].shape[1]), jnp.bfloat16),
        in_specs=in_vmem(len(pieces) + 1),
        out_specs=pl.BlockSpec(memory_space=pltpu.VMEM),
        **kernel_options(),
    )(left, *pieces)


def body(
    tokens,
    attn_gain,
    query_key_value_weight,
    out_weight,
    ffn_gain,
    router_weight,
    shared_gate,
    shared_up,
    shared_down,
    routed_gate_weight,
    routed_up_weight,
    routed_down_weight,
    routes,
    cotangent,
):
    f32 = jnp.float32
    bf16 = jnp.bfloat16
    both = ("context", "experts")
    context_count = lax.axis_size("context")
    spread = lax.axis_size("experts")
    context_index = lax.axis_index("context")
    expert_index = lax.axis_index("experts")
    token_count, width = tokens.shape
    local_experts = routed_gate_weight.shape[0]
    experts_all = local_experts * spread
    rows = token_count * spread
    weight_rows = query_key_value_weight.shape[0]
    query_width = QUERY_HEADS * HEAD_DIM
    key_width = KEY_VALUE_HEADS * HEAD_DIM
    repeat_times = spread // KEY_VALUE_HEADS
    head_share = QUERY_HEADS // spread
    own_width = head_share * HEAD_DIM
    block_width = width // context_count

    def key_columns(weight):
        heads = weight.reshape(weight_rows, KEY_VALUE_HEADS, HEAD_DIM)
        return jnp.repeat(heads, repeat_times, axis=1)

    qkv_send = jnp.concatenate(
        [
            query_key_value_weight[:, :query_width].reshape(weight_rows, spread, own_width),
            key_columns(query_key_value_weight[:, query_width : query_width + key_width]),
            key_columns(query_key_value_weight[:, query_width + key_width :]),
        ],
        axis=2,
    ).transpose(1, 0, 2)
    hidden_piece = shared_down.shape[0]
    hidden_own = hidden_piece * context_count
    hidden_wide = -(-hidden_own // HEAD_DIM) * HEAD_DIM

    def hidden_columns(weight):
        own_columns = (
            weight.reshape(weight_rows, context_count, spread, hidden_piece)
            .transpose(2, 0, 1, 3)
            .reshape(spread, weight_rows, hidden_own)
        )
        return jnp.pad(own_columns, ((0, 0), (0, 0), (0, hidden_wide - hidden_own)))

    shared_send = jnp.concatenate([hidden_columns(shared_gate), hidden_columns(shared_up)], axis=2)

    token_ring = RingGather(tokens)
    token_ring.step()
    qkv_rows = to_experts(qkv_send).reshape(spread * weight_rows, -1)
    small = jnp.concatenate([attn_gain[None], ffn_gain[None], router_weight.T], axis=0)
    small = flip_gather(small, "experts")
    qkv_rows, small = meet([token_ring], qkv_rows, small)
    token_ring.step()
    small = flip_gather(small, "context").transpose(2, 0, 1, 3).reshape(-1, width)
    gain_one = small[0].astype(f32)
    gain_two = small[1].astype(f32)
    router_full = small[2:]
    routes_block = flip_gather(routes.T, "experts")
    position = context_index * rows + jnp.arange(rows, dtype=jnp.int32)
    position = ring_order(position.reshape(spread, token_count)).reshape(rows).astype(f32)
    half_width = HEAD_DIM // 2
    frequency = THETA ** (-jnp.arange(half_width, dtype=f32) * 2.0 / HEAD_DIM)
    angles = position[:, None] * frequency[None, :]
    cosine = jnp.cos(angles)
    sine = jnp.sin(angles)
    cosine = jnp.concatenate([cosine, cosine], axis=1)
    sine = jnp.concatenate([-sine, sine], axis=1)
    qkv_own = context_gather(qkv_rows)
    gain_one, cosine, sine = meet([token_ring], gain_one, cosine, sine)
    token_ring.step()
    qkv_own, routes_block = meet([token_ring], qkv_own, routes_block)
    token_ring.step()
    out_weight, shared_send, shared_down, cotangent_late = meet(
        [token_ring], out_weight, shared_send, shared_down, cotangent
    )

    normed_one, query_rows, key_value = project(
        token_ring.pieces(), gain_one[None], qkv_own, cosine, sine, own_width
    )
    out_full = lax.all_gather(out_weight, both, axis=0, tiled=True)
    key_value, cotangent_late = lax.optimization_barrier((key_value, cotangent_late))
    grad_ring = RingGather(cotangent_late)
    grad_ring.step()
    key_value = context_gather(key_value)
    (key_value,) = meet([grad_ring], key_value)
    grad_ring.step()
    place = ring_place(expert_index, spread)
    order = (ring_place(jnp.arange(spread, dtype=jnp.int32), spread) - place + spread) % spread
    attended, attended_low, attended_ring, log_total = attention_forward(
        context_index, order, query_rows, key_value
    )
    (attended_low,) = meet([grad_ring], attended_low)
    grad_ring.step()
    attended_tok = (
        to_experts(attended_low.reshape(spread, token_count, own_width))
        .transpose(1, 0, 2)
        .reshape(token_count, query_width)
    )
    (attended_tok,) = meet([grad_ring], attended_tok)
    grad_ring.step()

    inputs = tokens.astype(f32)
    middle = inputs + jnp.dot(attended_tok, out_full, preferred_element_type=f32)
    (middle,) = meet([grad_ring], middle)
    scale_two = rms_scale(middle)
    normed_two = (middle * scale_two * gain_two).astype(bf16)
    normed_ring = RingGather(normed_two)
    normed_ring.step()

    first_expert = expert_index * local_experts
    own_ids = first_expert + jnp.arange(local_experts, dtype=jnp.int32)
    routes_block = ring_order(routes_block)
    member = jnp.any(routes_block[:, None] == own_ids[None, :, None, None], axis=2)
    counted = member.astype(jnp.int32)
    slot_index = jnp.cumsum(counted, axis=2) - counted
    capacity = token_count * TOP * 4 // (3 * experts_all)
    slot = jnp.arange(capacity, dtype=jnp.int32)
    chosen = member[:, :, None, :] & (slot_index[:, :, None, :] == slot[None, None, :, None])
    chosen_wide = chosen.astype(f32)
    slots = local_experts * capacity
    chosen_low = chosen.astype(bf16).reshape(spread, slots, token_count)
    chosen_back = chosen_low.transpose(0, 2, 1)
    grad_block, grad_rows = dispatch(grad_ring.pieces(), chosen_low, local_experts)
    shared_rows = to_experts(shared_send).reshape(spread * weight_rows, -1)
    shared_rows, grad_block, chosen_back = meet([normed_ring], shared_rows, grad_block, chosen_back)
    normed_ring.step()
    down_own = jnp.pad(context_gather(shared_down), ((0, hidden_wide - hidden_own), (0, 0)))
    (down_own,) = meet([normed_ring], down_own)
    normed_ring.step()
    shared_own = context_gather(shared_rows)
    (shared_own,) = meet([normed_ring], shared_own)
    normed_ring.step()
    meet([normed_ring])
    normed_block, expert_rows = dispatch(normed_ring.pieces(), chosen_low, local_experts)

    router_probs = jax.nn.softmax(dot_last(normed_block, router_full), axis=-1)
    gate_tokens = (
        lax.dynamic_slice_in_dim(router_probs, first_expert, local_experts, 1)
        .reshape(spread, token_count, local_experts)
        .transpose(0, 2, 1)
    )
    gates = jnp.sum(chosen_wide * gate_tokens[:, :, None, :], axis=3)
    gates = gates.transpose(1, 0, 2).reshape(local_experts, spread * capacity, 1)
    act, expert_dg, expert_du, row_grad = expert_pass(
        first_expert,
        expert_rows,
        grad_rows,
        gates,
        routed_gate_weight,
        routed_up_weight,
        routed_down_weight,
    )
    shared_act, shared_both = shared_pass(normed_block, grad_block, shared_own, down_own)
    grad_scatter = RingScatter(combine(chosen_back, row_grad, shared_both, shared_own, True))

    def down_piece(target, received=None):
        return weight_piece(target, act, grad_rows, context_count, False, gates, received)

    def gate_piece(target, received=None):
        return weight_piece(target, expert_rows, expert_dg, context_count, True, None, received)

    def up_piece(target, received=None):
        return weight_piece(target, expert_rows, expert_du, context_count, True, None, received)

    grad_scatter.step()
    down_parts = core_parts(down_piece)
    (down_parts,) = meet([grad_scatter], down_parts)
    grad_scatter.step()
    down_sums = core_sums(down_piece, core_exchange(down_parts))
    gate_parts = core_parts(gate_piece)
    down_sums, gate_parts = meet([grad_scatter], down_sums, gate_parts)
    grad_scatter.step()
    gate_sums = core_sums(gate_piece, core_exchange(gate_parts))
    up_parts = core_parts(up_piece)
    gate_sums, up_parts = meet([grad_scatter], gate_sums, up_parts)
    grad_scatter.step()
    up_sums = core_sums(up_piece, core_exchange(up_parts))
    shared_sum = inner_rows(normed_block, shared_both).astype(bf16)
    shared_sum = shared_sum.reshape(context_count, block_width, -1)
    up_sums, shared_sum = meet([grad_scatter], up_sums, shared_sum)
    gathered = grad_scatter.total()

    prob_grad = gathered[:, width : width + experts_all]
    probs_tok = router_probs[:token_count]
    logit_grad = (
        probs_tok * (prob_grad - jnp.sum(probs_tok * prob_grad, axis=-1, keepdims=True))
    ).astype(bf16)
    normed_grad = gathered[:, :width] + jnp.dot(
        logit_grad, router_full, preferred_element_type=f32
    )
    grad_final = cotangent.astype(f32)
    middle_norm_grad, ffn_gain_part = norm_back(middle, scale_two, gain_two, normed_grad)
    middle_grad = grad_final + middle_norm_grad
    branch_grad = middle_grad.astype(bf16)
    attended_grad = dot_last(branch_grad, out_full).astype(bf16)
    branch_ring = RingGather(branch_grad)
    branch_ring.step()
    grad_heads = to_experts(
        attended_grad.reshape(token_count, spread, own_width).transpose(1, 0, 2)
    ).reshape(rows, own_width)
    weighted_y = expert_results(act, gates, routed_down_weight)
    out_scatter = RingScatter(combine(chosen_back, weighted_y, shared_act, down_own, False))
    shared_received = core_exchange(block_parts(shared_sum))
    shared_down_sum = inner_rows(shared_act, grad_block)[:hidden_own].astype(bf16)
    shared_down_sum = shared_down_sum.reshape(context_count, hidden_piece, width)
    shared_down_received = core_exchange(block_parts(shared_down_sum))
    expert_down_grad = far_sums(down_sums)
    grad_heads, expert_down_grad, shared_received, shared_down_received = meet(
        [branch_ring], grad_heads, expert_down_grad, shared_received, shared_down_received
    )

    branch_ring.step()
    out_scatter.step()
    query_grad, key_value_all = attention_backward(
        context_index,
        order,
        query_rows,
        key_value,
        attended,
        grad_heads,
        log_total,
        cosine,
        sine,
    )
    shared_far = far_sums(block_sums(shared_sum, shared_received))
    key_value_all, shared_far = meet([branch_ring, out_scatter], key_value_all, shared_far)
    branch_ring.step()
    out_scatter.step()
    key_value_all = key_value_all.reshape(context_count, rows, -1)
    key_value_sums = block_sums(key_value_all, core_exchange(block_parts(key_value_all)))
    shared_back = to_experts(shared_far.astype(bf16).reshape(spread, weight_rows, -1))
    (key_value_sums,) = meet([branch_ring, out_scatter], key_value_sums)
    branch_ring.step()
    out_scatter.step()
    key_value_grad = far_sums(key_value_sums)
    shared_down_grad = far_sums(block_sums(shared_down_sum, shared_down_received))
    small_part = jnp.concatenate([ffn_gain_part[None], inner_rows(logit_grad, normed_two)], axis=0)
    small_part = small_part.reshape(-1, context_count, spread, weight_rows).transpose(1, 2, 0, 3)
    small_sum = flip_scatter(small_part, "context")
    key_value_grad, shared_down_grad, small_sum, shared_back = meet(
        [branch_ring, out_scatter], key_value_grad, shared_down_grad, small_sum, shared_back
    )
    expert_gate_grad = far_sums(gate_sums)
    key_grad = key_value_grad[:, :HEAD_DIM]
    turned = jnp.concatenate([key_grad[:, half_width:], key_grad[:, :half_width]], axis=1)
    key_value_pre = jnp.concatenate(
        [key_grad * cosine - turned * sine, key_value_grad[:, HEAD_DIM:]], axis=1
    ).astype(bf16)
    projected_grad = jnp.concatenate([query_grad, key_value_pre], axis=1)
    projected_grad, expert_gate_grad = lax.optimization_barrier((projected_grad, expert_gate_grad))
    input_scatter = RingScatter(dot_last(projected_grad, qkv_own).astype(bf16))
    input_scatter.step()
    out_scatter.step()
    qkv_sum = inner_rows(normed_one, projected_grad).astype(bf16)
    qkv_sum = qkv_sum.reshape(context_count, block_width, -1)
    qkv_received = core_exchange(block_parts(qkv_sum))
    out_sum = weight_sum(attended_ring, branch_ring.pieces())
    out_sum = out_sum.reshape(context_count, own_width // context_count, width)
    out_received = core_exchange(block_parts(out_sum))
    qkv_received, out_received = meet([input_scatter, out_scatter], qkv_received, out_received)
    input_scatter.step()
    qkv_far = far_sums(block_sums(qkv_sum, qkv_received))
    out_own = far_sums(block_sums(out_sum, out_received))
    small_sum = flip_scatter(small_sum, "experts")
    qkv_far, out_own, small_sum = meet([input_scatter], qkv_far, out_own, small_sum)
    ffn_gain_grad = small_sum[0]
    router_weight_grad = small_sum[1:].T
    input_scatter.step()
    qkv_back = to_experts(qkv_far.astype(bf16).reshape(spread, weight_rows, -1))
    out_weight_grad = lax.ppermute(
        out_own.astype(bf16),
        both,
        [
            (i * spread + j, j * context_count + i)
            for i in range(context_count)
            for j in range(spread)
        ],
    ).astype(f32)
    layer_out = (middle + out_scatter.total()[:, :width]).astype(bf16)
    qkv_back, out_weight_grad, layer_out = meet(
        [input_scatter], qkv_back, out_weight_grad, layer_out
    )
    input_scatter.step()

    def hidden_home(values):
        return (
            values.astype(f32)
            .reshape(spread, weight_rows, context_count, hidden_piece)
            .transpose(1, 2, 0, 3)
            .reshape(weight_rows, -1)
        )

    shared_gate_grad = hidden_home(shared_back[:, :, :hidden_own])
    shared_up_grad = hidden_home(shared_back[:, :, hidden_wide : hidden_wide + hidden_own])

    def key_home(values):
        return (
            values.reshape(KEY_VALUE_HEADS, repeat_times, weight_rows, HEAD_DIM)
            .sum(axis=1)
            .transpose(1, 0, 2)
            .reshape(weight_rows, key_width)
        )

    qkv_back = qkv_back.astype(f32)
    qkv_weight_grad = jnp.concatenate(
        [
            qkv_back[:, :, :own_width].transpose(1, 0, 2).reshape(weight_rows, query_width),
            key_home(qkv_back[:, :, own_width : own_width + HEAD_DIM]),
            key_home(qkv_back[:, :, own_width + HEAD_DIM :]),
        ],
        axis=1,
    )
    attn_gain_grad = jnp.sum(
        query_key_value_weight.astype(f32) * qkv_weight_grad, axis=1
    ) / attn_gain.astype(f32)
    expert_up_grad = far_sums(up_sums)
    input_norm_grad, _ = norm_back(inputs, rms_scale(inputs), gain_one, input_scatter.total())
    tokens_grad = middle_grad + input_norm_grad
    return (
        layer_out,
        tokens_grad,
        attn_gain_grad,
        qkv_weight_grad,
        out_weight_grad,
        ffn_gain_grad,
        router_weight_grad,
        shared_gate_grad,
        shared_up_grad,
        shared_down_grad,
        expert_gate_grad,
        expert_up_grad,
        expert_down_grad,
    )


def solution(mesh):
    return jax.shard_map(
        body,
        mesh=mesh,
        in_specs=(
            P(("context", "experts"), None),
            P(("context", "experts")),
            P(("context", "experts"), None),
            P(("context", "experts"), None),
            P(("context", "experts")),
            P(("context", "experts"), None),
            P(("context", "experts"), None),
            P(("context", "experts"), None),
            P(("context", "experts"), None),
            P("experts", None, None),
            P("experts", None, None),
            P("experts", None, None),
            P(("context", "experts"), None),
            P(("context", "experts"), None),
        ),
        out_specs=(
            P(("context", "experts"), None),
            P(("context", "experts"), None),
            P(("context", "experts")),
            P(("context", "experts"), None),
            P(("context", "experts"), None),
            P(("context", "experts")),
            P(("context", "experts"), None),
            P(("context", "experts"), None),
            P(("context", "experts"), None),
            P(("context", "experts"), None),
            P("experts", "context", None),
            P("experts", "context", None),
            P("experts", None, "context"),
        ),
        check_vma=False,
    )
```

```python
import functools
import math

import jax
import jax.numpy as jnp
from jax import lax
from jax.experimental import pallas as pl
from jax.experimental.pallas import tpu as pltpu
from jax.sharding import PartitionSpec as P

QUERY_HEADS = 16
KEY_VALUE_HEADS = 4
HEAD_DIM = 128
TOP = 6


EPSILON = 1e-06
THETA = 10000.0
NEG_LARGE = -1e30
CONTEXT = ("far", "core")


def rms_scale(values):
    return lax.rsqrt(jnp.mean(values * values, axis=-1, keepdims=True) + EPSILON)


def norm_back(values, row_scale, gain_values, grad_out):
    weighted = grad_out * gain_values
    gain_grad = jnp.sum(grad_out * values * row_scale, axis=0)
    inner_mean = jnp.mean(weighted * values, axis=-1, keepdims=True)
    return (
        row_scale * weighted - values * row_scale * row_scale * row_scale * inner_mean,
        gain_grad,
    )


def inner_rows(left, right):
    return lax.dot_general(
        left, right, (((0,), (0,)), ((), ())), preferred_element_type=jnp.float32
    )


def dot_last(left, right):
    return lax.dot_general(
        left, right, (((1,), (1,)), ((), ())), preferred_element_type=jnp.float32
    )


def context_size():
    return lax.axis_size("far") * lax.axis_size("core")


def ring_pairs(count):
    order = [i for i in range(count) if i % 2 == 0] + [i for i in reversed(range(count)) if i % 2 == 1]
    right = [(order[i], order[(i + 1) % count]) for i in range(count)]
    left = [(order[i], order[(i - 1) % count]) for i in range(count)]
    return right, left


def ring_place(index, count):
    return jnp.where(index % 2 == 0, index // 2, count - 1 - index // 2)


def ring_index(place, count):
    place = (place + 2 * count) % count
    return jnp.where(place < count // 2, 2 * place, 2 * (count - 1 - place) + 1)


class RingGather:
    def __init__(self, block):
        self.count = lax.axis_size("experts")
        self.right, self.left = ring_pairs(self.count)
        self.half = block.shape[0] // 2
        self.block = block
        self.ahead = [block]
        self.behind = [block]
        self.far = None

    def step(self):
        if len(self.ahead) < self.count // 2:
            self.behind.append(lax.ppermute(self.behind[-1], "experts", self.right))
            self.ahead.append(lax.ppermute(self.ahead[-1], "experts", self.left))
        else:
            self.far = [
                lax.ppermute(self.behind[-1][: self.half], "experts", self.right),
                lax.ppermute(self.ahead[-1][self.half :], "experts", self.left),
            ]

    def latest(self):
        return self.far if self.far else [self.behind[-1], self.ahead[-1]]

    def replace(self, values):
        if self.far:
            self.far = list(values)
        else:
            self.behind[-1], self.ahead[-1] = values

    def pieces(self):
        return self.ahead + self.far + self.behind[:0:-1]


class RingScatter:
    def __init__(self, whole):
        self.count = lax.axis_size("experts")
        self.right, self.left = ring_pairs(self.count)
        self.whole = whole
        self.rows = whole.shape[0] // self.count
        self.half = self.rows // 2
        self.left_steps = self.count // 2
        self.first = None
        self.second = None

    def own(self, step):
        start = step % self.count * self.rows
        return self.whole[start : start + self.rows].astype(jnp.float32)

    def arrived(self):
        first = self.first.astype(jnp.float32)
        second = self.second.astype(jnp.float32)
        if self.left_steps == self.count // 2 - 1:
            blank = jnp.zeros((self.half, self.whole.shape[1]), jnp.float32)
            first = jnp.concatenate([first, blank], axis=0)
            second = jnp.concatenate([blank, second], axis=0)
        return first, second

    def step(self):
        if self.first is None:
            far = self.own(self.left_steps)
            first, second = far[: self.half], far[self.half :]
        else:
            first, second = self.arrived()
            first = first + self.own(self.left_steps)
            second = second + self.own(-self.left_steps)
        self.first = lax.ppermute(first.astype(jnp.bfloat16), "experts", self.right)
        self.second = lax.ppermute(second.astype(jnp.bfloat16), "experts", self.left)
        self.left_steps -= 1

    def latest(self):
        return [self.first, self.second]

    def replace(self, values):
        self.first, self.second = values

    def total(self):
        first, second = self.arrived()
        return first + second + self.own(0)


def meet(rings, *values):
    held, values = lax.optimization_barrier(([ring.latest() for ring in rings], values))
    for ring, value in zip(rings, held):
        ring.replace(value)
    return values


def ring_order(values):
    count = lax.axis_size("experts")
    place = ring_place(lax.axis_index("experts"), count)
    return jnp.concatenate(
        [
            lax.dynamic_slice_in_dim(values, ring_index(place + step, count), 1, 0)
            for step in range(count)
        ],
        axis=0,
    )


def flip_pairs(count, bit):
    return [(i, i ^ bit) for i in range(count)]


def flip_double(whole, axis):
    bit = whole.shape[0]
    received = lax.ppermute(whole, axis, flip_pairs(lax.axis_size(axis), bit))
    return jnp.where(
        (lax.axis_index(axis) // bit) % 2 == 0,
        jnp.concatenate([whole, received], axis=0),
        jnp.concatenate([received, whole], axis=0),
    )


def flip_gather(block, axis):
    whole = block[None]
    while whole.shape[0] < lax.axis_size(axis):
        whole = flip_double(whole, axis)
    return whole


def flip_half(values, axis, bit, dimension):
    shape = values.shape
    pairs = values.reshape(shape[:dimension] + (shape[dimension] // 2, 2) + shape[dimension + 1 :])
    mine = (lax.axis_index(axis) // bit) % 2
    sent = lax.dynamic_index_in_dim(pairs, 1 - mine, dimension + 1, keepdims=False)
    kept = lax.dynamic_index_in_dim(pairs, mine, dimension + 1, keepdims=False)
    return kept + lax.ppermute(sent, axis, flip_pairs(lax.axis_size(axis), bit))


def context_double(whole, bit):
    received = lax.ppermute(whole, CONTEXT, flip_pairs(context_size(), bit))
    low = (lax.axis_index(CONTEXT) // bit) % 2 == 0
    return jnp.stack(
        [jnp.where(low, whole, received), jnp.where(low, received, whole)], axis=1
    ).reshape((2 * whole.shape[0],) + whole.shape[1:])


def far_gather(block):
    whole = block[None]
    bit = context_size() // 2
    while bit > 1:
        whole = context_double(whole, bit)
        bit //= 2
    return whole


def core_gather(whole):
    return context_double(whole, 1).reshape(-1, whole.shape[-1])


def context_gather(block):
    return core_gather(far_gather(block))


def after(done, *values):
    values, _ = lax.optimization_barrier((values, done))
    return values[0] if len(values) == 1 else values


def core_parts(piece_of):
    count = context_size()
    index = lax.axis_index(CONTEXT)
    return {place: piece_of(index ^ (place + 1)) for place in range(count - 2, -1, -2)}


def core_exchange(parts):
    pairs = flip_pairs(context_size(), 1)
    return {
        place: lax.ppermute(part.astype(jnp.bfloat16), CONTEXT, pairs)
        for place, part in parts.items()
    }


def core_sums(piece_of, received):
    index = lax.axis_index(CONTEXT)
    return {
        place // 2: piece_of(index ^ place, part) for place, part in received.items()
    }


def far_exchange(pieces):
    count = context_size()
    bit = 2
    while 2 * bit < count:
        merged = {}
        for place in sorted(pieces, reverse=True):
            if place % 2 == 0:
                received = lax.ppermute(
                    pieces[place + 1].astype(jnp.bfloat16), CONTEXT, flip_pairs(count, bit)
                )
                merged[place // 2] = pieces[place] + received.astype(jnp.float32)
        pieces = merged
        bit *= 2
    last = lax.ppermute(pieces[1].astype(jnp.bfloat16), CONTEXT, flip_pairs(count, bit))
    return pieces[0], last


def both_halves(pair):
    return pair[0] + pair[1].astype(jnp.float32)


def core_swap(values):
    return lax.ppermute(values, "core", [(0, 1), (1, 0)])


def chips_sum(values):
    return lax.psum_scatter(values, "far", scatter_dimension=0, tiled=True)[0]


def block_sums(values, received):
    def piece_of(target, part):
        return lax.dynamic_index_in_dim(values, target, 0, keepdims=False) + part.astype(jnp.float32)

    return core_sums(piece_of, received)


def block_parts(values):
    return core_parts(lambda target: lax.dynamic_index_in_dim(values, target, 0, keepdims=False))


def to_experts(stacked):
    return lax.all_to_all(stacked, "experts", split_axis=0, concat_axis=0, tiled=True)


VMEM_BYTES = 60 * 1024 * 1024


def kernel_options():
    return dict(
        compiler_params=pltpu.CompilerParams(vmem_limit_bytes=VMEM_BYTES),
        cost_estimate=pl.CostEstimate(flops=1024, bytes_accessed=1024, transcendentals=0),
    )


def in_vmem(count):
    return [pl.BlockSpec(memory_space=pltpu.VMEM)] * count


def in_smem(count):
    return [pl.BlockSpec(memory_space=pltpu.SMEM)] * count


def plain_dot(left, right):
    return jnp.dot(left, right, preferred_element_type=jnp.float32)


def last_dims(left, right):
    return lax.dot_general(
        left, right, (((1,), (1,)), ((), ())), preferred_element_type=jnp.float32
    )


def first_dims(left, right):
    return lax.dot_general(
        left, right, (((0,), (0,)), ((), ())), preferred_element_type=jnp.float32
    )


def project_kernel(piece_count, *refs):
    pieces = refs[:piece_count]
    weight_ref, cosine_ref, sine_ref, normed_ref, query_ref, key_value_ref = refs[piece_count:]
    start = 0
    for piece in pieces:
        rows = piece.shape[0]
        values = piece[...].astype(jnp.float32)
        scale = lax.rsqrt(jnp.mean(values * values, axis=-1, keepdims=True) + EPSILON)
        normed_ref[start : start + rows, :] = (values * scale).astype(jnp.bfloat16)
        start += rows
    query_width = query_ref.shape[1]
    heads = plain_dot(normed_ref[...], weight_ref[...])

    def rotated(offset):
        head = heads[:, offset : offset + HEAD_DIM]
        turned = pltpu.roll(head, HEAD_DIM // 2, 1)
        return (head * cosine_ref[...] + turned * sine_ref[...]).astype(jnp.bfloat16)

    for offset in range(0, query_width, HEAD_DIM):
        query_ref[:, offset : offset + HEAD_DIM] = rotated(offset)
    key_value_ref[:, :HEAD_DIM] = rotated(query_width)
    key_value_ref[:, HEAD_DIM:] = heads[:, query_width + HEAD_DIM :].astype(jnp.bfloat16)


def project(pieces, weight, cosine, sine, query_width):
    rows = sum(piece.shape[0] for piece in pieces)
    width = pieces[0].shape[1]
    return pl.pallas_call(
        functools.partial(project_kernel, len(pieces)),
        out_shape=(
            jax.ShapeDtypeStruct((rows, width), jnp.bfloat16),
            jax.ShapeDtypeStruct((rows, query_width), jnp.bfloat16),
            jax.ShapeDtypeStruct((rows, weight.shape[1] - query_width), jnp.bfloat16),
        ),
        in_specs=in_vmem(len(pieces) + 3),
        out_specs=tuple(in_vmem(3)),
        **kernel_options(),
    )(*pieces, weight, cosine, sine)


def stack_heads(values):
    heads = values.shape[1] // HEAD_DIM
    return jnp.concatenate(
        [values[:, i * HEAD_DIM : (i + 1) * HEAD_DIM] for i in range(heads)], axis=0
    )


def spread_heads(values, heads):
    rows = values.shape[0] // heads
    return jnp.concatenate([values[i * rows : (i + 1) * rows] for i in range(heads)], axis=1)


def stack_lanes(values):
    return jnp.concatenate([values[i : i + 1] for i in range(values.shape[0])], axis=1)


def visible_keys(shape, key_start, query_start, query_tile):
    key_pos = key_start + lax.broadcasted_iota(jnp.int32, shape, 0)
    query_pos = query_start + lax.rem(lax.broadcasted_iota(jnp.int32, shape, 1), query_tile)
    return query_pos >= key_pos


def ring_slices(order_ref, rows, first, count):
    spread = order_ref.shape[0]
    length = rows // spread
    found = []
    for i in range(count):
        number = first + i
        base = lax.div(number, spread) * rows
        place = order_ref[lax.rem(number, spread)] * length
        found.append(pl.ds(pl.multiple_of(base + place, length), length))
    return found


def forward_kernel(
    query_tile, key_tile, block_ref, order_ref, query_ref, key_value_ref, out_ref, low_ref, total_ref
):
    rows = query_ref.shape[0]
    length = rows // order_ref.shape[0]
    heads = query_ref.shape[1] // HEAD_DIM
    wide = heads * query_tile
    scale = HEAD_DIM ** (-0.5) * math.log2(math.e)

    @pl.loop(0, rows // query_tile)
    def _(index):
        offset = pl.multiple_of(index * query_tile, query_tile)
        places = ring_slices(order_ref, rows, index * (query_tile // length), query_tile // length)
        queries = stack_heads(jnp.concatenate([query_ref[place, :] for place in places], axis=0))
        start = block_ref[0] * rows + offset

        def step(tile, state, masked):
            top, total, summed = state
            here = ring_slices(order_ref, rows, tile * (key_tile // length), key_tile // length)
            keys = jnp.concatenate([key_value_ref[place, :HEAD_DIM] for place in here], axis=0)
            values = jnp.concatenate([key_value_ref[place, HEAD_DIM:] for place in here], axis=0)
            scores = last_dims(keys, queries) * scale
            if masked:
                seen = visible_keys(scores.shape, tile * key_tile, start, query_tile)
                scores = jnp.where(seen, scores, NEG_LARGE)
            new_top = jnp.maximum(top, jnp.max(scores, axis=0, keepdims=True))
            weights = jnp.exp2(scores - new_top)
            rescale = jnp.exp2(top - new_top)
            total = total * rescale + jnp.sum(weights, axis=0, keepdims=True)
            summed = summed * rescale + first_dims(values, weights.astype(jnp.bfloat16))
            return new_top, total, summed

        state = (
            jnp.full((1, wide), NEG_LARGE, jnp.float32),
            jnp.zeros((1, wide), jnp.float32),
            jnp.zeros((HEAD_DIM, wide), jnp.float32),
        )
        full = lax.div(start, key_tile)
        state = lax.fori_loop(0, full, lambda tile, state: step(tile, state, False), state)
        top, total, summed = step(full, state, True)
        result = spread_heads((summed / total).T, heads)
        out_ref[pl.ds(offset, query_tile), :] = result
        low_ref[pl.ds(offset, query_tile), :] = result.astype(jnp.bfloat16)
        log_total = top + jnp.log2(total)
        for i in range(heads):
            total_ref[i : i + 1, pl.ds(offset, query_tile)] = log_total[
                :, i * query_tile : (i + 1) * query_tile
            ]


def backward_kernel(
    query_tile,
    key_tile,
    block_ref,
    order_ref,
    query_ref,
    key_value_ref,
    out_ref,
    grad_ref,
    total_ref,
    cosine_ref,
    sine_ref,
    query_grad_ref,
    key_value_grad_ref,
):
    rows = query_ref.shape[0]
    length = rows // order_ref.shape[0]
    heads = query_ref.shape[1] // HEAD_DIM
    wide = heads * query_tile
    score_scale = HEAD_DIM ** (-0.5)
    scale = score_scale * math.log2(math.e)

    @pl.loop(0, key_value_ref.shape[0] // key_tile)
    def _(tile):
        key_start = pl.multiple_of(tile * key_tile, key_tile)
        key_value_grad_ref[pl.ds(key_start, key_tile), :] = jnp.zeros(
            (key_tile, 2 * HEAD_DIM), jnp.float32
        )

    @pl.loop(0, rows // query_tile)
    def _(index):
        offset = pl.multiple_of(index * query_tile, query_tile)
        places = ring_slices(order_ref, rows, index * (query_tile // length), query_tile // length)
        queries = stack_heads(jnp.concatenate([query_ref[place, :] for place in places], axis=0))
        grads = stack_heads(grad_ref[pl.ds(offset, query_tile), :])
        outs = stack_heads(out_ref[pl.ds(offset, query_tile), :])
        delta = jnp.sum((grads.astype(jnp.float32) * outs).T, axis=0, keepdims=True)
        log_total = stack_lanes(total_ref[:, pl.ds(offset, query_tile)])
        start = block_ref[0] * rows + offset

        def step(tile, query_grad, masked):
            here = ring_slices(order_ref, rows, tile * (key_tile // length), key_tile // length)
            keys = jnp.concatenate([key_value_ref[place, :HEAD_DIM] for place in here], axis=0)
            values = jnp.concatenate([key_value_ref[place, HEAD_DIM:] for place in here], axis=0)
            weights = jnp.exp2(last_dims(keys, queries) * scale - log_total)
            if masked:
                seen = visible_keys(weights.shape, tile * key_tile, start, query_tile)
                weights = jnp.where(seen, weights, 0.0)
            value_part = plain_dot(weights.astype(jnp.bfloat16), grads)
            score_grad = (weights * (last_dims(values, grads) - delta)).astype(jnp.bfloat16)
            key_part = plain_dot(score_grad, queries) * score_scale
            part = jnp.concatenate([key_part, value_part], axis=1)
            for i, place in enumerate(here):
                key_value_grad_ref[place, :] += part[i * length : (i + 1) * length]
            return query_grad + first_dims(score_grad, keys)

        full = lax.div(start, key_tile)
        query_grad = lax.fori_loop(
            0,
            full,
            lambda tile, state: step(tile, state, False),
            jnp.zeros((wide, HEAD_DIM), jnp.float32),
        )
        query_grad = step(full, query_grad, True) * score_scale
        for i, place in enumerate(places):
            cosine = cosine_ref[place, :]
            sine = sine_ref[place, :]
            for head in range(heads):
                begin = head * query_tile + i * length
                part = query_grad[begin : begin + length]
                turned = part * cosine - pltpu.roll(part, HEAD_DIM // 2, 1) * sine
                query_grad_ref[place, head * HEAD_DIM : (head + 1) * HEAD_DIM] = turned.astype(
                    jnp.bfloat16
                )


def attention_forward(block_index, order, queries, keys):
    rows, wide = queries.shape
    return pl.pallas_call(
        functools.partial(forward_kernel, math.gcd(rows, 1024), math.gcd(rows, 1024)),
        out_shape=(
            jax.ShapeDtypeStruct((rows, wide), jnp.float32),
            jax.ShapeDtypeStruct((rows, wide), jnp.bfloat16),
            jax.ShapeDtypeStruct((wide // HEAD_DIM, rows), jnp.float32),
        ),
        in_specs=in_smem(2) + in_vmem(2),
        out_specs=tuple(in_vmem(3)),
        **kernel_options(),
    )(block_index.reshape(1), order, queries, keys)


def attention_backward(block_index, order, queries, keys, outs, grads, log_total, cosine, sine):
    rows, wide = queries.shape
    return pl.pallas_call(
        functools.partial(backward_kernel, math.gcd(rows, 512), math.gcd(rows, 512)),
        out_shape=(
            jax.ShapeDtypeStruct((rows, wide), jnp.bfloat16),
            jax.ShapeDtypeStruct((keys.shape[0], 2 * HEAD_DIM), jnp.float32),
        ),
        in_specs=in_smem(2) + in_vmem(7),
        out_specs=tuple(in_vmem(2)),
        **kernel_options(),
    )(block_index.reshape(1), order, queries, keys, outs, grads, log_total, cosine, sine)


def dispatch_kernel(piece_count, experts, *refs):
    pieces = refs[:piece_count]
    chosen_ref, whole_ref, rows_ref = refs[piece_count:]
    start = 0
    for piece in pieces:
        whole_ref[start : start + piece.shape[0], :] = piece[...]
        start += piece.shape[0]
    length = chosen_ref.shape[2]
    capacity = chosen_ref.shape[1] // experts
    for block in range(chosen_ref.shape[0]):
        picked = plain_dot(chosen_ref[block], whole_ref[block * length : (block + 1) * length, :])
        picked = picked.astype(jnp.bfloat16)
        for expert in range(experts):
            rows_ref[expert, block * capacity : (block + 1) * capacity, :] = picked[
                expert * capacity : (expert + 1) * capacity
            ]


def dispatch(pieces, chosen, experts):
    rows = sum(piece.shape[0] for piece in pieces)
    width = pieces[0].shape[1]
    blocks, slots, _ = chosen.shape
    return pl.pallas_call(
        functools.partial(dispatch_kernel, len(pieces), experts),
        out_shape=(
            jax.ShapeDtypeStruct((rows, width), jnp.bfloat16),
            jax.ShapeDtypeStruct((experts, blocks * (slots // experts), width), jnp.bfloat16),
        ),
        in_specs=in_vmem(len(pieces) + 1),
        out_specs=tuple(in_vmem(2)),
        **kernel_options(),
    )(*pieces, chosen)


def hidden_tiles(width, tile):
    return [slice(start, min(start + tile, width)) for start in range(0, width, tile)]


def slopes(pre_gate, pre_up):
    sigmoid = 1.0 / (1.0 + jnp.exp(-pre_gate))
    silu = pre_gate * sigmoid
    return silu * pre_up, pre_up * sigmoid * (1.0 + pre_gate * (1.0 - sigmoid)), silu


def expert_forward_kernel(rows_ref, weight_gate_ref, weight_up_ref, act_ref, by_gate_ref, by_up_ref):
    for here in hidden_tiles(act_ref.shape[2], 256):
        pre_gate = plain_dot(rows_ref[0], weight_gate_ref[0, :, here])
        pre_up = plain_dot(rows_ref[0], weight_up_ref[0, :, here])
        act, by_gate, by_up = slopes(pre_gate, pre_up)
        act_ref[0, :, here] = act.astype(jnp.bfloat16)
        by_gate_ref[0, :, here] = by_gate.astype(jnp.bfloat16)
        by_up_ref[0, :, here] = by_up.astype(jnp.bfloat16)


def one_expert(*shape):
    return pl.BlockSpec((1,) + shape, lambda expert: (expert, 0, 0))


def expert_forward(rows, weight_gate, weight_up):
    experts, count, width = rows.shape
    hidden = weight_gate.shape[2]
    return pl.pallas_call(
        expert_forward_kernel,
        grid=(experts,),
        out_shape=(jax.ShapeDtypeStruct((experts, count, hidden), jnp.bfloat16),) * 3,
        in_specs=[one_expert(count, width), one_expert(width, hidden), one_expert(width, hidden)],
        out_specs=(one_expert(count, hidden),) * 3,
        **kernel_options(),
    )(rows, weight_gate, weight_up)


def expert_backward_kernel(
    first_ref,
    grad_ref,
    gate_ref,
    act_ref,
    by_gate_ref,
    by_up_ref,
    weight_gate_ref,
    weight_up_ref,
    weight_down_ref,
    gate_grad_ref,
    up_grad_ref,
    row_grad_ref,
):
    width = weight_gate_ref.shape[1]
    count = grad_ref.shape[1]
    score = jnp.zeros((count, 1), jnp.float32)
    for here in hidden_tiles(act_ref.shape[2], 256):
        act_grad = last_dims(grad_ref[0], weight_down_ref[0, here, :])
        score = score + jnp.sum(
            act_ref[0, :, here].astype(jnp.float32) * act_grad, axis=1, keepdims=True
        )
        act_grad = act_grad * gate_ref[0]
        gate_grad_ref[0, :, here] = (act_grad * by_gate_ref[0, :, here].astype(jnp.float32)).astype(
            jnp.bfloat16
        )
        up_grad_ref[0, :, here] = (act_grad * by_up_ref[0, :, here].astype(jnp.float32)).astype(
            jnp.bfloat16
        )

    for here in hidden_tiles(width, 512):
        row_grad_ref[0, :, here] = (
            last_dims(gate_grad_ref[0], weight_gate_ref[0, here, :])
            + last_dims(up_grad_ref[0], weight_up_ref[0, here, :])
        ).astype(jnp.bfloat16)

    lane = lax.broadcasted_iota(jnp.int32, (count, HEAD_DIM), 1)
    own = first_ref[0] + pl.program_id(0)
    row_grad_ref[0, :, width:] = jnp.where(lane == own, score, 0.0).astype(jnp.bfloat16)


def expert_backward(first_expert, grads, gates, act, by_gate, by_up, weight_gate, weight_up, weight_down):
    experts, count, width = grads.shape
    hidden = act.shape[2]
    low = one_expert(count, hidden)
    return pl.pallas_call(
        expert_backward_kernel,
        grid=(experts,),
        out_shape=(
            jax.ShapeDtypeStruct((experts, count, hidden), jnp.bfloat16),
            jax.ShapeDtypeStruct((experts, count, hidden), jnp.bfloat16),
            jax.ShapeDtypeStruct((experts, count, width + HEAD_DIM), jnp.bfloat16),
        ),
        in_specs=in_smem(1)
        + [
            one_expert(count, width),
            one_expert(count, 1),
            low,
            low,
            low,
            one_expert(width, hidden),
            one_expert(width, hidden),
            one_expert(hidden, width),
        ],
        out_specs=(low, low, one_expert(count, width + HEAD_DIM)),
        **kernel_options(),
    )(first_expert.reshape(1), grads, gates, act, by_gate, by_up, weight_gate, weight_up, weight_down)


def result_kernel(act_ref, gate_ref, weight_ref, out_ref):
    for here in hidden_tiles(out_ref.shape[2], 512):
        result = plain_dot(act_ref[0], weight_ref[0, :, here]).astype(jnp.bfloat16)
        out_ref[0, :, here] = (result.astype(jnp.float32) * gate_ref[0]).astype(jnp.bfloat16)


def expert_results(act, gates, weight_down):
    experts, count, hidden = act.shape
    width = weight_down.shape[2]

    def one(*shape):
        return pl.BlockSpec((1,) + shape, lambda expert: (expert, 0, 0))

    return pl.pallas_call(
        result_kernel,
        grid=(experts,),
        out_shape=jax.ShapeDtypeStruct((experts, count, width), jnp.bfloat16),
        in_specs=[one(count, hidden), one(count, 1), one(hidden, width)],
        out_specs=one(count, width),
        **kernel_options(),
    )(act, gates, weight_down)


def combine_kernel(turned, chosen_ref, values_ref, left_ref, right_ref, out_ref):
    width = right_ref.shape[0] if turned else right_ref.shape[1]
    experts = values_ref.shape[0]
    length = chosen_ref.shape[1]
    capacity = chosen_ref.shape[2] // experts
    blocks = chosen_ref.shape[0]

    def slots(block, here):
        values = [
            values_ref[expert, block * capacity : (block + 1) * capacity, here]
            for expert in range(experts)
        ]
        return plain_dot(chosen_ref[block], jnp.concatenate(values, axis=0))

    for here in hidden_tiles(width, 512):
        shared = (
            last_dims(left_ref[...], right_ref[here, :])
            if turned
            else plain_dot(left_ref[...], right_ref[:, here])
        )
        for block in range(blocks):
            rows = slice(block * length, (block + 1) * length)
            out_ref[rows, here] = (shared[rows] + slots(block, here)).astype(jnp.bfloat16)

    if out_ref.shape[1] > width:
        for block in range(blocks):
            out_ref[block * length : (block + 1) * length, width:] = slots(
                block, slice(width, out_ref.shape[1])
            ).astype(jnp.bfloat16)


def combine(chosen, values, left, right, turned):
    blocks, length, slots = chosen.shape
    experts, _, wide = values.shape
    capacity = slots // experts
    some = math.gcd(blocks, 2)
    return pl.pallas_call(
        functools.partial(combine_kernel, turned),
        grid=(blocks // some,),
        out_shape=jax.ShapeDtypeStruct((blocks * length, wide), jnp.bfloat16),
        in_specs=[
            pl.BlockSpec((some, length, slots), lambda i: (i, 0, 0)),
            pl.BlockSpec((experts, some * capacity, wide), lambda i: (0, i, 0)),
            pl.BlockSpec((some * length, left.shape[1]), lambda i: (i, 0)),
            pl.BlockSpec(right.shape, lambda i: (0, 0)),
        ],
        out_specs=pl.BlockSpec((some * length, wide), lambda i: (i, 0)),
        **kernel_options(),
    )(chosen, values, left, right)


def shared_kernel(normed_ref, grad_ref, weight_ref, down_ref, act_ref, both_ref):
    hidden = act_ref.shape[1]
    pre_gate = plain_dot(normed_ref[...], weight_ref[:, :hidden])
    pre_up = plain_dot(normed_ref[...], weight_ref[:, hidden:])
    act_grad = last_dims(grad_ref[...], down_ref[...])
    act, by_gate, by_up = slopes(pre_gate, pre_up)
    act_ref[...] = act.astype(jnp.bfloat16)
    both_ref[:, :hidden] = (act_grad * by_gate).astype(jnp.bfloat16)
    both_ref[:, hidden:] = (act_grad * by_up).astype(jnp.bfloat16)


def shared_pass(normed, grads, weight, down):
    rows, width = normed.shape
    hidden = down.shape[0]
    some = math.gcd(rows, 256)

    def part(columns):
        return pl.BlockSpec((some, columns), lambda i: (i, 0))

    return pl.pallas_call(
        shared_kernel,
        grid=(rows // some,),
        out_shape=(
            jax.ShapeDtypeStruct((rows, hidden), jnp.bfloat16),
            jax.ShapeDtypeStruct((rows, 2 * hidden), jnp.bfloat16),
        ),
        in_specs=[
            part(width),
            part(width),
            pl.BlockSpec(weight.shape, lambda i: (0, 0)),
            pl.BlockSpec(down.shape, lambda i: (0, 0)),
        ],
        out_specs=(part(hidden), part(2 * hidden)),
        **kernel_options(),
    )(normed, grads, weight, down)


def part_kernel(scaled, added, core_ref, left_ref, right_ref, *refs):
    right = right_ref[0]
    if scaled:
        right = (right.astype(jnp.float32) * refs[0][0]).astype(jnp.bfloat16)
    total = first_dims(left_ref[0], right)
    if added:
        total = total + refs[-2][0, 0].astype(jnp.float32)
    refs[-1][0, 0] = total.astype(jnp.bfloat16)


def weight_parts(core, left, right, cut_left, gates=None, received=None):
    chips = lax.axis_size("far")
    experts, count, left_width = left.shape
    right_width = right.shape[2]
    left_width, right_width = (
        (left_width // (2 * chips), right_width) if cut_left else (left_width, right_width // (2 * chips))
    )

    def spec(columns, cut):
        if cut:
            return pl.BlockSpec((1, count, columns), lambda f, e, c: (e, 0, 2 * f + c[0]))
        return pl.BlockSpec((1, count, columns), lambda f, e, c: (e, 0, 0))

    whole = pl.BlockSpec((1, 1, left_width, right_width), lambda f, e, c: (f, e, 0, 0))
    operands = [left, right]
    specs = [spec(left_width, cut_left), spec(right_width, not cut_left)]
    if gates is not None:
        operands.append(gates)
        specs.append(pl.BlockSpec((1, count, 1), lambda f, e, c: (e, 0, 0)))
    if received is not None:
        operands.append(received)
        specs.append(whole)
    return pl.pallas_call(
        functools.partial(part_kernel, gates is not None, received is not None),
        grid_spec=pltpu.PrefetchScalarGridSpec(
            num_scalar_prefetch=1, grid=(chips, experts), in_specs=specs, out_specs=whole
        ),
        out_shape=jax.ShapeDtypeStruct((chips, experts, left_width, right_width), jnp.bfloat16),
        **kernel_options(),
    )(core.reshape(1), *operands)


def output_weight_kernel(piece_count, index_ref, grad_ref, *refs):
    pieces = refs[:piece_count]
    out_ref = refs[piece_count]
    wide = pieces[0].shape[1]
    half = piece_count // 2

    def part(piece, start):
        return first_dims(piece[...], grad_ref[start : start + piece.shape[0], :])

    block = 0
    while block < index_ref.shape[0]:
        if block < half:
            total = part(pieces[block], 0)
        elif block == half:
            total = part(pieces[half], 0) + part(pieces[half + 1], pieces[half].shape[0])
        else:
            total = part(pieces[block + 1], 0)
        start = pl.multiple_of(index_ref[block] * wide, wide)
        out_ref[pl.ds(start, wide), :] = total.astype(jnp.bfloat16)
        block += 1


def output_weight(index, grads, pieces):
    return pl.pallas_call(
        functools.partial(output_weight_kernel, len(pieces)),
        out_shape=jax.ShapeDtypeStruct(
            (index.shape[0] * pieces[0].shape[1], grads.shape[1]), jnp.bfloat16
        ),
        in_specs=in_smem(1) + in_vmem(len(pieces) + 1),
        out_specs=pl.BlockSpec(memory_space=pltpu.VMEM),
        **kernel_options(),
    )(index, grads, *pieces)


def body(
    tokens,
    attn_gain,
    query_key_value_weight,
    out_weight,
    ffn_gain,
    router_weight,
    shared_gate,
    shared_up,
    shared_down,
    routed_gate_weight,
    routed_up_weight,
    routed_down_weight,
    routes,
    cotangent,
):
    f32 = jnp.float32
    bf16 = jnp.bfloat16
    both = CONTEXT + ("experts",)
    context_count = context_size()
    spread = lax.axis_size("experts")
    context_index = lax.axis_index(CONTEXT)
    expert_index = lax.axis_index("experts")
    token_count, width = tokens.shape
    local_experts = routed_gate_weight.shape[0]
    experts_all = local_experts * spread
    rows = token_count * spread
    weight_rows = query_key_value_weight.shape[0]
    query_width = QUERY_HEADS * HEAD_DIM
    key_width = KEY_VALUE_HEADS * HEAD_DIM
    repeat_times = spread // KEY_VALUE_HEADS
    head_share = QUERY_HEADS // spread
    own_width = head_share * HEAD_DIM
    block_width = width // context_count

    def key_columns(weight):
        heads = weight.reshape(weight_rows, KEY_VALUE_HEADS, HEAD_DIM)
        return jnp.repeat(heads, repeat_times, axis=1)

    own_gain = attn_gain.astype(f32)[:, None]
    qkv_scaled = (query_key_value_weight.astype(f32) * own_gain).astype(bf16)
    qkv_send = jnp.concatenate(
        [
            qkv_scaled[:, :query_width].reshape(weight_rows, spread, own_width),
            key_columns(qkv_scaled[:, query_width : query_width + key_width]),
            key_columns(qkv_scaled[:, query_width + key_width :]),
        ],
        axis=2,
    ).transpose(1, 0, 2)
    hidden_piece = shared_down.shape[0]
    hidden_own = hidden_piece * context_count
    hidden_wide = -(-hidden_own // HEAD_DIM) * HEAD_DIM

    def hidden_columns(weight):
        own_columns = (
            weight.reshape(weight_rows, context_count, spread, hidden_piece)
            .transpose(2, 0, 1, 3)
            .reshape(spread, weight_rows, hidden_own)
        )
        return jnp.pad(own_columns, ((0, 0), (0, 0), (0, hidden_wide - hidden_own)))

    shared_send = jnp.concatenate([hidden_columns(shared_gate), hidden_columns(shared_up)], axis=2)

    token_ring = RingGather(tokens)
    token_ring.step()
    position = context_index * rows + jnp.arange(rows, dtype=jnp.int32)
    position = ring_order(position.reshape(spread, token_count)).reshape(rows).astype(f32)
    half_width = HEAD_DIM // 2
    frequency = THETA ** (-jnp.arange(half_width, dtype=f32) * 2.0 / HEAD_DIM)
    angles = position[:, None] * frequency[None, :]
    cosine = jnp.cos(angles)
    sine = jnp.sin(angles)
    cosine = jnp.concatenate([cosine, cosine], axis=1)
    sine = jnp.concatenate([-sine, sine], axis=1)
    small = jnp.concatenate([ffn_gain[None], router_weight.T], axis=0)
    small = flip_double(small[None], CONTEXT)
    qkv_send = after(small, qkv_send)
    qkv_rows = to_experts(qkv_send).reshape(spread * weight_rows, -1)
    while small.shape[0] < context_count:
        small = flip_double(small, CONTEXT)
    small = jnp.concatenate([small.reshape(1, -1), routes.astype(bf16).reshape(1, -1)], axis=1)
    small, cosine, sine = meet([token_ring], small, cosine, sine)
    token_ring.step()
    qkv_rows, out_weight = meet([token_ring], qkv_rows, out_weight)
    token_ring.step()
    qkv_far = far_gather(qkv_rows)
    (qkv_far,) = meet([token_ring], qkv_far)
    token_ring.step()
    qkv_own = core_gather(qkv_far)
    (qkv_own,) = meet([token_ring], qkv_own)
    small = after(token_ring.latest(), small)

    out_full = lax.all_gather(out_weight, both, axis=0, tiled=True)
    normed_one, query_rows, key_value = project(
        token_ring.pieces(), qkv_own, cosine, sine, own_width
    )
    key_value = far_gather(key_value)
    small = flip_double(small, "experts")
    key_value, small = lax.optimization_barrier((key_value, small))
    key_value = core_gather(key_value)
    small = flip_double(small, "experts")
    place = ring_place(expert_index, spread)
    order = (ring_place(jnp.arange(spread, dtype=jnp.int32), spread) - place + spread) % spread
    attended, attended_low, log_total = attention_forward(
        context_index, order, query_rows, key_value
    )
    attended_low, small = lax.optimization_barrier((attended_low, small))
    attended_tok = (
        to_experts(attended_low.reshape(spread, token_count, own_width))
        .transpose(1, 0, 2)
        .reshape(token_count, query_width)
    )
    while small.shape[0] < spread:
        small = flip_double(small, "experts")
    attended_tok, small = lax.optimization_barrier((attended_tok, small))
    routes_block = small[:, -token_count * TOP :].reshape(spread, token_count, TOP)
    routes_block = routes_block.astype(jnp.int32).transpose(0, 2, 1)
    small = small[:, : -token_count * TOP].reshape(spread, context_count, -1, weight_rows)
    small = small.transpose(2, 1, 0, 3).reshape(-1, width)
    gain_two = small[0].astype(f32)
    router_full = small[1:]

    inputs = tokens.astype(f32)
    middle = inputs + jnp.dot(attended_tok, out_full, preferred_element_type=f32)
    scale_two = rms_scale(middle)
    normed_two = (middle * scale_two * gain_two).astype(bf16)
    normed_ring = RingGather(normed_two)
    normed_ring.step()
    routes_block, router_full, shared_down = meet(
        [normed_ring], routes_block, router_full, shared_down
    )

    normed_ring.step()
    down_far = far_gather(shared_down)
    first_expert = expert_index * local_experts
    own_ids = first_expert + jnp.arange(local_experts, dtype=jnp.int32)
    routes_block = ring_order(routes_block)
    member = jnp.any(routes_block[:, None] == own_ids[None, :, None, None], axis=2)
    counted = member.astype(jnp.int32)
    slot_index = jnp.cumsum(counted, axis=2) - counted
    capacity = token_count * TOP * 4 // (3 * experts_all)
    slot = jnp.arange(capacity, dtype=jnp.int32)
    chosen = member[:, :, None, :] & (slot_index[:, :, None, :] == slot[None, None, :, None])
    chosen_wide = chosen.astype(f32)
    slots = local_experts * capacity
    chosen_low = chosen.astype(bf16).reshape(spread, slots, token_count)
    chosen_back = chosen_low.transpose(0, 2, 1)
    down_far, chosen_low, chosen_wide, chosen_back = meet(
        [normed_ring], down_far, chosen_low, chosen_wide, chosen_back
    )
    normed_ring.step()
    down_own = jnp.pad(core_gather(down_far), ((0, hidden_wide - hidden_own), (0, 0)))
    (down_own,) = meet([normed_ring], down_own)
    normed_ring.step()
    (cotangent_late,) = meet([normed_ring], cotangent)
    grad_ring = RingGather(cotangent_late)
    grad_ring.step()
    normed_block, expert_rows = dispatch(normed_ring.pieces(), chosen_low, local_experts)

    (normed_block,) = meet([grad_ring], normed_block)
    grad_ring.step()
    router_probs = jax.nn.softmax(dot_last(normed_block, router_full), axis=-1)
    gate_tokens = (
        lax.dynamic_slice_in_dim(router_probs, first_expert, local_experts, 1)
        .reshape(spread, token_count, local_experts)
        .transpose(0, 2, 1)
    )
    gates = jnp.sum(chosen_wide * gate_tokens[:, :, None, :], axis=3)
    gates = gates.transpose(1, 0, 2).reshape(local_experts, spread * capacity, 1)
    expert_rows = after(gates, expert_rows)
    act, by_gate, by_up = expert_forward(expert_rows, routed_gate_weight, routed_up_weight)
    act, gates = meet([grad_ring], act, gates)
    grad_ring.step()
    meet([grad_ring])
    grad_ring.step()
    chosen_low, shared_send = meet([grad_ring], chosen_low, shared_send)
    grad_block, grad_rows = dispatch(grad_ring.pieces(), chosen_low, local_experts)

    own_core = lax.axis_index("core")
    other_core = 1 - own_core
    shared_rows = to_experts(shared_send).reshape(spread * weight_rows, -1)
    down_parts = weight_parts(other_core, act, grad_rows, False, gates)
    act = after(down_parts, act)
    down_received = core_swap(down_parts)
    weighted_y = expert_results(act, gates, routed_down_weight)
    shared_rows, down_received, weighted_y, attended_late = lax.optimization_barrier(
        (shared_rows, down_received, weighted_y, attended_low)
    )
    shared_far = far_gather(shared_rows)
    heads_ring = RingGather(attended_late)
    heads_ring.step()
    down_parts = weight_parts(own_core, act, grad_rows, False, gates, down_received)
    down_sum = chips_sum(down_parts)
    grad_rows, gates = after(down_parts, grad_rows, gates)
    expert_dg, expert_du, row_grad = expert_backward(
        first_expert,
        grad_rows,
        gates,
        act,
        by_gate,
        by_up,
        routed_gate_weight,
        routed_up_weight,
        routed_down_weight,
    )
    row_grad, shared_far = meet([heads_ring], row_grad, shared_far)
    heads_ring.step()
    shared_own = core_gather(shared_far)
    shared_act, shared_both = shared_pass(normed_block, grad_block, shared_own, down_own)
    shared_act, shared_both = meet([heads_ring], shared_act, shared_both)
    heads_ring.step()
    grad_part = combine(chosen_back, row_grad, shared_both, shared_own, True)
    (grad_part,) = meet([heads_ring], grad_part)
    grad_scatter = RingScatter(grad_part)
    grad_scatter.step()
    heads_ring.step()
    expert_dg = after(grad_part, expert_dg)
    gate_parts = weight_parts(other_core, expert_rows, expert_dg, True)
    (gate_parts,) = meet([grad_scatter, heads_ring], gate_parts)
    grad_scatter.step()
    gate_received = core_swap(gate_parts)
    shared_sum = inner_rows(normed_block, after(gate_parts, shared_both)).astype(bf16)
    shared_sum = shared_sum.reshape(context_count, block_width, -1)
    gate_received, shared_sum = meet([grad_scatter], gate_received, shared_sum)
    grad_scatter.step()
    gate_parts = weight_parts(own_core, expert_rows, expert_dg, True, None, gate_received)
    gate_parts, expert_du, down_sum = meet([grad_scatter], gate_parts, expert_du, down_sum)
    gate_sum = chips_sum(gate_parts)
    grad_scatter.step()
    up_parts = weight_parts(other_core, expert_rows, expert_du, True)
    up_parts, shared_sum, weighted_y = meet([grad_scatter], up_parts, shared_sum, weighted_y)
    gathered = grad_scatter.total()

    prob_grad = gathered[:, width : width + experts_all]
    probs_tok = router_probs[:token_count]
    logit_grad = (
        probs_tok * (prob_grad - jnp.sum(probs_tok * prob_grad, axis=-1, keepdims=True))
    ).astype(bf16)
    normed_grad = gathered[:, :width] + jnp.dot(
        logit_grad, router_full, preferred_element_type=f32
    )
    grad_final = cotangent.astype(f32)
    middle_norm_grad, ffn_gain_part = norm_back(middle, scale_two, gain_two, normed_grad)
    middle_grad = grad_final + middle_norm_grad
    branch_grad = middle_grad.astype(bf16)
    attended_grad = dot_last(branch_grad, out_full).astype(bf16)
    grad_heads = to_experts(
        attended_grad.reshape(token_count, spread, own_width).transpose(1, 0, 2)
    ).reshape(rows, own_width)
    shared_sum, shared_act, branch_late, up_parts, weighted_y = after(
        attended_grad, shared_sum, shared_act, branch_grad, up_parts, weighted_y
    )
    up_received = core_swap(up_parts)
    shared_received = core_exchange(block_parts(shared_sum))
    out_part = combine(chosen_back, weighted_y, shared_act, down_own, False)
    shared_sums = block_sums(shared_sum, shared_received)
    grad_heads, shared_sums, branch_late, up_received, out_part = lax.optimization_barrier(
        (grad_heads, shared_sums, branch_late, up_received, out_part)
    )

    branch_columns = to_experts(
        branch_late.reshape(token_count, spread, own_width).transpose(1, 0, 2)
    ).reshape(rows, own_width)
    out_scatter = RingScatter(out_part)
    out_scatter.step()
    shared_pair = far_exchange(shared_sums)
    query_grad, key_value_all = attention_backward(
        context_index,
        order,
        query_rows,
        key_value,
        attended,
        grad_heads,
        log_total,
        cosine,
        sine,
    )
    key_value_all, branch_columns, shared_pair = meet(
        [out_scatter], key_value_all, branch_columns, shared_pair
    )
    out_scatter.step()
    key_value_all = key_value_all.reshape(context_count, rows, -1)
    key_value_received = core_exchange(block_parts(key_value_all))
    key_value_sums = block_sums(key_value_all, key_value_received)
    key_value_sums, expert_du, shared_pair, gate_sum = lax.optimization_barrier(
        (key_value_sums, expert_du, shared_pair, gate_sum)
    )
    key_value_pair = far_exchange(key_value_sums)
    shared_far_sum = both_halves(shared_pair).astype(bf16)
    shared_back = to_experts(shared_far_sum.reshape(spread, weight_rows, -1))
    up_parts = weight_parts(own_core, expert_rows, expert_du, True, None, up_received)
    up_sum = chips_sum(up_parts)
    index = ring_index(place + jnp.arange(spread, dtype=jnp.int32), spread)
    out_sum = output_weight(index, after(key_value_sums, branch_columns), heads_ring.pieces())
    small_sum = jnp.concatenate(
        [
            inner_rows(normed_two, logit_grad),
            ffn_gain_part[:, None],
            jnp.zeros((width, HEAD_DIM - experts_all - 1), f32),
        ],
        axis=1,
    ).astype(bf16)
    out_sum = out_sum.reshape(context_count, block_width, -1)
    small_sum = small_sum.reshape(context_count, block_width, -1)
    out_received = core_exchange(block_parts(out_sum))
    small_received = core_exchange(block_parts(small_sum))
    key_value_pair, out_received, small_received, shared_back, up_parts = meet(
        [out_scatter], key_value_pair, out_received, small_received, shared_back, up_parts
    )
    out_scatter.step()
    key_value_grad = both_halves(key_value_pair)
    key_grad = key_value_grad[:, :HEAD_DIM]
    turned = jnp.concatenate([key_grad[:, half_width:], key_grad[:, :half_width]], axis=1)
    key_value_pre = jnp.concatenate(
        [key_grad * cosine - turned * sine, key_value_grad[:, HEAD_DIM:]], axis=1
    ).astype(bf16)
    projected_grad = jnp.concatenate([query_grad, key_value_pre], axis=1)
    input_scatter = RingScatter(dot_last(projected_grad, qkv_own).astype(bf16))
    input_scatter.step()
    normed_one, out_received, small_received = after(
        input_scatter.whole, normed_one, out_received, small_received
    )
    qkv_sum = inner_rows(normed_one, projected_grad).astype(bf16)
    qkv_sum = qkv_sum.reshape(context_count, block_width, -1)
    qkv_sums = block_sums(qkv_sum, core_exchange(block_parts(qkv_sum)))
    out_sums = block_sums(out_sum, out_received)
    small_sums = block_sums(small_sum, small_received)
    qkv_sums, out_sums, small_sums = meet(
        [input_scatter, out_scatter], qkv_sums, out_sums, small_sums
    )
    input_scatter.step()
    out_scatter.step()
    qkv_pair = far_exchange(qkv_sums)
    out_pair = far_exchange(out_sums)
    small_pair = far_exchange(small_sums)
    shared_down_sum = inner_rows(shared_act, grad_block)[:hidden_own].astype(bf16)
    shared_down_sum = shared_down_sum.reshape(context_count, hidden_piece, width)
    shared_down_sums = block_sums(shared_down_sum, core_exchange(block_parts(shared_down_sum)))
    qkv_pair, out_pair, small_pair, shared_down_sums = meet(
        [input_scatter, out_scatter], qkv_pair, out_pair, small_pair, shared_down_sums
    )
    input_scatter.step()
    dense_sum = jnp.concatenate(
        [
            both_halves(qkv_pair).astype(bf16),
            both_halves(out_pair).astype(bf16),
            both_halves(small_pair).astype(bf16),
        ],
        axis=1,
    )
    dense_back = to_experts(dense_sum.reshape(spread, weight_rows, -1))
    shared_down_pair = far_exchange(shared_down_sums)
    dense_back, shared_down_pair = meet([input_scatter], dense_back, shared_down_pair)
    input_scatter.step()
    dense_back = dense_back.astype(f32)
    qkv_back = dense_back[:, :, : qkv_own.shape[1]]
    out_weight_grad = (
        dense_back[:, :, qkv_own.shape[1] : qkv_own.shape[1] + own_width]
        .transpose(1, 0, 2)
        .reshape(weight_rows, width)
    )
    small_back = jnp.sum(dense_back[:, :, qkv_own.shape[1] + own_width :], axis=0)
    router_weight_grad = small_back[:, :experts_all]
    ffn_gain_grad = small_back[:, experts_all]
    shared_down_grad = both_halves(shared_down_pair)
    layer_out = (middle + out_scatter.total()).astype(bf16)
    expert_down_grad = down_sum.astype(f32)
    expert_gate_grad = gate_sum.astype(f32)
    expert_up_grad = up_sum.astype(f32)

    def hidden_home(values):
        return (
            values.reshape(spread, weight_rows, context_count, hidden_piece)
            .transpose(1, 2, 0, 3)
            .reshape(weight_rows, -1)
            .astype(f32)
        )

    shared_gate_grad = hidden_home(shared_back[:, :, :hidden_own])
    shared_up_grad = hidden_home(shared_back[:, :, hidden_wide : hidden_wide + hidden_own])

    def key_home(values):
        return (
            values.reshape(KEY_VALUE_HEADS, repeat_times, weight_rows, HEAD_DIM)
            .sum(axis=1)
            .transpose(1, 0, 2)
            .reshape(weight_rows, key_width)
        )

    qkv_weight_grad = jnp.concatenate(
        [
            qkv_back[:, :, :own_width].transpose(1, 0, 2).reshape(weight_rows, query_width),
            key_home(qkv_back[:, :, own_width : own_width + HEAD_DIM]),
            key_home(qkv_back[:, :, own_width + HEAD_DIM :]),
        ],
        axis=1,
    )
    attn_gain_grad = jnp.sum(query_key_value_weight.astype(f32) * qkv_weight_grad, axis=1)
    qkv_weight_grad = own_gain * qkv_weight_grad
    scale_one = rms_scale(inputs)
    weighted = input_scatter.total()
    inner_mean = jnp.mean(weighted * inputs, axis=-1, keepdims=True)
    tokens_grad = (
        middle_grad
        + scale_one * weighted
        - inputs * scale_one * scale_one * scale_one * inner_mean
    )
    return (
        layer_out,
        tokens_grad,
        attn_gain_grad,
        qkv_weight_grad,
        out_weight_grad,
        ffn_gain_grad,
        router_weight_grad,
        shared_gate_grad,
        shared_up_grad,
        shared_down_grad,
        expert_gate_grad,
        expert_up_grad,
        expert_down_grad,
    )


def solution(mesh):
    context_count, spread = mesh.devices.shape
    split = jax.sharding.Mesh(
        mesh.devices.reshape(context_count // 2, 2, spread), ("far", "core", "experts")
    )
    return jax.shard_map(
        body,
        mesh=split,
        in_specs=(
            P(("far", "core", "experts"), None),
            P(("far", "core", "experts")),
            P(("far", "core", "experts"), None),
            P(("far", "core", "experts"), None),
            P(("far", "core", "experts")),
            P(("far", "core", "experts"), None),
            P(("far", "core", "experts"), None),
            P(("far", "core", "experts"), None),
            P(("far", "core", "experts"), None),
            P("experts", None, None),
            P("experts", None, None),
            P("experts", None, None),
            P(("far", "core", "experts"), None),
            P(("far", "core", "experts"), None),
        ),
        out_specs=(
            P(("far", "core", "experts"), None),
            P(("far", "core", "experts"), None),
            P(("far", "core", "experts")),
            P(("far", "core", "experts"), None),
            P(("far", "core", "experts"), None),
            P(("far", "core", "experts")),
            P(("far", "core", "experts"), None),
            P(("far", "core", "experts"), None),
            P(("far", "core", "experts"), None),
            P(("far", "core", "experts"), None),
            P("experts", CONTEXT, None),
            P("experts", CONTEXT, None),
            P("experts", None, CONTEXT),
        ),
        check_vma=False,
    )
```

```python
import functools
import math

import jax
import jax.numpy as jnp
from jax import lax
from jax.experimental import pallas as pl
from jax.experimental.pallas import tpu as pltpu
from jax.sharding import PartitionSpec as P

QUERY_HEADS = 16
KEY_VALUE_HEADS = 4
HEAD_DIM = 128
TOP = 6


EPSILON = 1e-06
THETA = 10000.0
NEG_LARGE = -1e30
CONTEXT = ("far", "core")


def rms_scale(values):
    return lax.rsqrt(jnp.mean(values * values, axis=-1, keepdims=True) + EPSILON)


def norm_back(values, row_scale, gain_values, grad_out):
    weighted = grad_out * gain_values
    gain_grad = jnp.sum(grad_out * values * row_scale, axis=0)
    inner_mean = jnp.mean(weighted * values, axis=-1, keepdims=True)
    return (
        row_scale * weighted - values * row_scale * row_scale * row_scale * inner_mean,
        gain_grad,
    )


def inner_rows(left, right):
    return lax.dot_general(
        left, right, (((0,), (0,)), ((), ())), preferred_element_type=jnp.float32
    )


def dot_last(left, right):
    return lax.dot_general(
        left, right, (((1,), (1,)), ((), ())), preferred_element_type=jnp.float32
    )


def context_size():
    return lax.axis_size("far") * lax.axis_size("core")


def ring_pairs(count):
    order = [i for i in range(count) if i % 2 == 0] + [i for i in reversed(range(count)) if i % 2 == 1]
    right = [(order[i], order[(i + 1) % count]) for i in range(count)]
    left = [(order[i], order[(i - 1) % count]) for i in range(count)]
    return right, left


def ring_place(index, count):
    return jnp.where(index % 2 == 0, index // 2, count - 1 - index // 2)


def ring_index(place, count):
    place = (place + 2 * count) % count
    return jnp.where(place < count // 2, 2 * place, 2 * (count - 1 - place) + 1)


class RingGather:
    def __init__(self, block):
        self.count = lax.axis_size("experts")
        self.right, self.left = ring_pairs(self.count)
        self.half = block.shape[0] // 2
        self.block = block
        self.ahead = [block]
        self.behind = [block]
        self.far = None

    def step(self):
        if len(self.ahead) < self.count // 2:
            self.behind.append(lax.ppermute(self.behind[-1], "experts", self.right))
            self.ahead.append(lax.ppermute(self.ahead[-1], "experts", self.left))
        else:
            self.far = [
                lax.ppermute(self.behind[-1][: self.half], "experts", self.right),
                lax.ppermute(self.ahead[-1][self.half :], "experts", self.left),
            ]

    def latest(self):
        return self.far if self.far else [self.behind[-1], self.ahead[-1]]

    def replace(self, values):
        if self.far:
            self.far = list(values)
        else:
            self.behind[-1], self.ahead[-1] = values

    def pieces(self):
        return self.ahead + self.far + self.behind[:0:-1]


class RingScatter:
    def __init__(self, whole):
        self.count = lax.axis_size("experts")
        self.right, self.left = ring_pairs(self.count)
        self.whole = whole
        self.rows = whole.shape[0] // self.count
        self.half = self.rows // 2
        self.left_steps = self.count // 2
        self.first = None
        self.second = None

    def own(self, step):
        start = step % self.count * self.rows
        return self.whole[start : start + self.rows].astype(jnp.float32)

    def arrived(self):
        first = self.first.astype(jnp.float32)
        second = self.second.astype(jnp.float32)
        if self.left_steps == self.count // 2 - 1:
            blank = jnp.zeros((self.half, self.whole.shape[1]), jnp.float32)
            first = jnp.concatenate([first, blank], axis=0)
            second = jnp.concatenate([blank, second], axis=0)
        return first, second

    def step(self):
        if self.first is None:
            far = self.own(self.left_steps)
            first, second = far[: self.half], far[self.half :]
        else:
            first, second = self.arrived()
            first = first + self.own(self.left_steps)
            second = second + self.own(-self.left_steps)
        self.sent = (first.astype(jnp.bfloat16), second.astype(jnp.bfloat16))
        self.first = lax.ppermute(self.sent[0], "experts", self.right)
        self.second = lax.ppermute(self.sent[1], "experts", self.left)
        self.left_steps -= 1

    def latest(self):
        return [self.first, self.second]

    def replace(self, values):
        self.first, self.second = values

    def total(self):
        first, second = self.arrived()
        return first + second + self.own(0)


def meet(rings, *values):
    held, values = lax.optimization_barrier(([ring.latest() for ring in rings], values))
    for ring, value in zip(rings, held):
        ring.replace(value)
    return values


def ring_order(values):
    count = lax.axis_size("experts")
    place = ring_place(lax.axis_index("experts"), count)
    return jnp.concatenate(
        [
            lax.dynamic_slice_in_dim(values, ring_index(place + step, count), 1, 0)
            for step in range(count)
        ],
        axis=0,
    )


def flip_pairs(count, bit):
    return [(i, i ^ bit) for i in range(count)]


def flip_double(whole, axis):
    bit = whole.shape[0]
    received = lax.ppermute(whole, axis, flip_pairs(lax.axis_size(axis), bit))
    return jnp.where(
        (lax.axis_index(axis) // bit) % 2 == 0,
        jnp.concatenate([whole, received], axis=0),
        jnp.concatenate([received, whole], axis=0),
    )


def flip_gather(block, axis):
    whole = block[None]
    while whole.shape[0] < lax.axis_size(axis):
        whole = flip_double(whole, axis)
    return whole


def flip_half(values, axis, bit, dimension):
    shape = values.shape
    pairs = values.reshape(shape[:dimension] + (shape[dimension] // 2, 2) + shape[dimension + 1 :])
    mine = (lax.axis_index(axis) // bit) % 2
    sent = lax.dynamic_index_in_dim(pairs, 1 - mine, dimension + 1, keepdims=False)
    kept = lax.dynamic_index_in_dim(pairs, mine, dimension + 1, keepdims=False)
    return kept + lax.ppermute(sent, axis, flip_pairs(lax.axis_size(axis), bit))


def context_double(whole, bit):
    received = lax.ppermute(whole, CONTEXT, flip_pairs(context_size(), bit))
    low = (lax.axis_index(CONTEXT) // bit) % 2 == 0
    return jnp.stack(
        [jnp.where(low, whole, received), jnp.where(low, received, whole)], axis=1
    ).reshape((2 * whole.shape[0],) + whole.shape[1:])


def far_gather(block):
    whole = block[None]
    bit = context_size() // 2
    while bit > 1:
        whole = context_double(whole, bit)
        bit //= 2
    return whole


def core_gather(whole):
    return context_double(whole, 1).reshape(-1, whole.shape[-1])


def context_gather(block):
    return core_gather(far_gather(block))


def after(done, *values):
    values, _ = lax.optimization_barrier((values, done))
    return values[0] if len(values) == 1 else values


def core_parts(piece_of):
    count = context_size()
    index = lax.axis_index(CONTEXT)
    return {place: piece_of(index ^ (place + 1)) for place in range(count - 2, -1, -2)}


def core_exchange(parts):
    pairs = flip_pairs(context_size(), 1)
    return {
        place: lax.ppermute(part.astype(jnp.bfloat16), CONTEXT, pairs)
        for place, part in parts.items()
    }


def core_sums(piece_of, received):
    index = lax.axis_index(CONTEXT)
    return {
        place // 2: piece_of(index ^ place, part) for place, part in received.items()
    }


def far_exchange(pieces):
    count = context_size()
    bit = 2
    while 2 * bit < count:
        merged = {}
        for place in sorted(pieces, reverse=True):
            if place % 2 == 0:
                received = lax.ppermute(
                    pieces[place + 1].astype(jnp.bfloat16), CONTEXT, flip_pairs(count, bit)
                )
                merged[place // 2] = pieces[place] + received.astype(jnp.float32)
        pieces = merged
        bit *= 2
    last = lax.ppermute(pieces[1].astype(jnp.bfloat16), CONTEXT, flip_pairs(count, bit))
    return pieces[0], last


def both_halves(pair):
    return pair[0] + pair[1].astype(jnp.float32)


def core_swap(values):
    return lax.ppermute(values, "core", [(0, 1), (1, 0)])


def chips_sum(values):
    return lax.psum_scatter(values, "far", scatter_dimension=0, tiled=True)[0]


def chips_exchange(values):
    chip = lax.axis_index("far")
    pieces = {
        place: lax.dynamic_index_in_dim(values, chip ^ place, 0, keepdims=False)
        for place in range(values.shape[0])
    }
    return far_exchange(pieces)


def block_sums(values, received):
    def piece_of(target, part):
        return lax.dynamic_index_in_dim(values, target, 0, keepdims=False) + part.astype(jnp.float32)

    return core_sums(piece_of, received)


def block_parts(values):
    return core_parts(lambda target: lax.dynamic_index_in_dim(values, target, 0, keepdims=False))


def to_experts(stacked):
    return lax.all_to_all(stacked, "experts", split_axis=0, concat_axis=0, tiled=True)


VMEM_BYTES = 60 * 1024 * 1024


def kernel_options():
    return dict(
        compiler_params=pltpu.CompilerParams(vmem_limit_bytes=VMEM_BYTES),
        cost_estimate=pl.CostEstimate(flops=1024, bytes_accessed=1024, transcendentals=0),
    )


def in_vmem(count):
    return [pl.BlockSpec(memory_space=pltpu.VMEM)] * count


def in_smem(count):
    return [pl.BlockSpec(memory_space=pltpu.SMEM)] * count


def plain_dot(left, right):
    return jnp.dot(left, right, preferred_element_type=jnp.float32)


def last_dims(left, right):
    return lax.dot_general(
        left, right, (((1,), (1,)), ((), ())), preferred_element_type=jnp.float32
    )


def first_dims(left, right):
    return lax.dot_general(
        left, right, (((0,), (0,)), ((), ())), preferred_element_type=jnp.float32
    )


def project_kernel(piece_count, *refs):
    pieces = refs[:piece_count]
    weight_ref, cosine_ref, sine_ref, normed_ref, query_ref, key_value_ref = refs[piece_count:]
    start = 0
    for piece in pieces:
        rows = piece.shape[0]
        values = piece[...].astype(jnp.float32)
        scale = lax.rsqrt(jnp.mean(values * values, axis=-1, keepdims=True) + EPSILON)
        normed_ref[start : start + rows, :] = (values * scale).astype(jnp.bfloat16)
        start += rows
    query_width = query_ref.shape[1]
    heads = plain_dot(normed_ref[...], weight_ref[...])

    def rotated(offset):
        head = heads[:, offset : offset + HEAD_DIM]
        turned = pltpu.roll(head, HEAD_DIM // 2, 1)
        return (head * cosine_ref[...] + turned * sine_ref[...]).astype(jnp.bfloat16)

    for offset in range(0, query_width, HEAD_DIM):
        query_ref[:, offset : offset + HEAD_DIM] = rotated(offset)
    key_value_ref[:, :HEAD_DIM] = rotated(query_width)
    key_value_ref[:, HEAD_DIM:] = heads[:, query_width + HEAD_DIM :].astype(jnp.bfloat16)


def project(pieces, weight, cosine, sine, query_width):
    rows = sum(piece.shape[0] for piece in pieces)
    width = pieces[0].shape[1]
    return pl.pallas_call(
        functools.partial(project_kernel, len(pieces)),
        out_shape=(
            jax.ShapeDtypeStruct((rows, width), jnp.bfloat16),
            jax.ShapeDtypeStruct((rows, query_width), jnp.bfloat16),
            jax.ShapeDtypeStruct((rows, weight.shape[1] - query_width), jnp.bfloat16),
        ),
        in_specs=in_vmem(len(pieces) + 3),
        out_specs=tuple(in_vmem(3)),
        **kernel_options(),
    )(*pieces, weight, cosine, sine)


def stack_heads(values):
    heads = values.shape[1] // HEAD_DIM
    return jnp.concatenate(
        [values[:, i * HEAD_DIM : (i + 1) * HEAD_DIM] for i in range(heads)], axis=0
    )


def spread_heads(values, heads):
    rows = values.shape[0] // heads
    return jnp.concatenate([values[i * rows : (i + 1) * rows] for i in range(heads)], axis=1)


def stack_lanes(values):
    return jnp.concatenate([values[i : i + 1] for i in range(values.shape[0])], axis=1)


def visible_keys(shape, key_start, query_start, query_tile):
    key_pos = key_start + lax.broadcasted_iota(jnp.int32, shape, 0)
    query_pos = query_start + lax.rem(lax.broadcasted_iota(jnp.int32, shape, 1), query_tile)
    return query_pos >= key_pos


def ring_slices(order_ref, rows, first, count):
    spread = order_ref.shape[0]
    length = rows // spread
    found = []
    for i in range(count):
        number = first + i
        base = lax.div(number, spread) * rows
        place = order_ref[lax.rem(number, spread)] * length
        found.append(pl.ds(pl.multiple_of(base + place, length), length))
    return found


def forward_kernel(
    query_tile, key_tile, block_ref, order_ref, query_ref, key_value_ref, out_ref, low_ref, total_ref
):
    rows = query_ref.shape[0]
    length = rows // order_ref.shape[0]
    heads = query_ref.shape[1] // HEAD_DIM
    wide = heads * query_tile
    scale = HEAD_DIM ** (-0.5) * math.log2(math.e)

    @pl.loop(0, rows // query_tile)
    def _(index):
        offset = pl.multiple_of(index * query_tile, query_tile)
        places = ring_slices(order_ref, rows, index * (query_tile // length), query_tile // length)
        queries = stack_heads(jnp.concatenate([query_ref[place, :] for place in places], axis=0))
        start = block_ref[0] * rows + offset

        def step(tile, state, masked):
            top, total, summed = state
            here = ring_slices(order_ref, rows, tile * (key_tile // length), key_tile // length)
            keys = jnp.concatenate([key_value_ref[place, :HEAD_DIM] for place in here], axis=0)
            values = jnp.concatenate([key_value_ref[place, HEAD_DIM:] for place in here], axis=0)
            scores = last_dims(keys, queries) * scale
            if masked:
                seen = visible_keys(scores.shape, tile * key_tile, start, query_tile)
                scores = jnp.where(seen, scores, NEG_LARGE)
            new_top = jnp.maximum(top, jnp.max(scores, axis=0, keepdims=True))
            weights = jnp.exp2(scores - new_top)
            rescale = jnp.exp2(top - new_top)
            total = total * rescale + jnp.sum(weights, axis=0, keepdims=True)
            summed = summed * rescale + first_dims(values, weights.astype(jnp.bfloat16))
            return new_top, total, summed

        state = (
            jnp.full((1, wide), NEG_LARGE, jnp.float32),
            jnp.zeros((1, wide), jnp.float32),
            jnp.zeros((HEAD_DIM, wide), jnp.float32),
        )
        full = lax.div(start, key_tile)
        state = lax.fori_loop(0, full, lambda tile, state: step(tile, state, False), state)
        top, total, summed = step(full, state, True)
        result = spread_heads((summed / total).T, heads)
        out_ref[pl.ds(offset, query_tile), :] = result
        low_ref[pl.ds(offset, query_tile), :] = result.astype(jnp.bfloat16)
        log_total = top + jnp.log2(total)
        for i in range(heads):
            total_ref[i : i + 1, pl.ds(offset, query_tile)] = log_total[
                :, i * query_tile : (i + 1) * query_tile
            ]


def backward_kernel(
    query_tile,
    key_tile,
    block_ref,
    order_ref,
    query_ref,
    key_value_ref,
    out_ref,
    grad_ref,
    total_ref,
    cosine_ref,
    sine_ref,
    query_grad_ref,
    key_value_grad_ref,
):
    rows = query_ref.shape[0]
    length = rows // order_ref.shape[0]
    heads = query_ref.shape[1] // HEAD_DIM
    wide = heads * query_tile
    score_scale = HEAD_DIM ** (-0.5)
    scale = score_scale * math.log2(math.e)

    @pl.loop(0, key_value_ref.shape[0] // key_tile)
    def _(tile):
        key_start = pl.multiple_of(tile * key_tile, key_tile)
        key_value_grad_ref[pl.ds(key_start, key_tile), :] = jnp.zeros(
            (key_tile, 2 * HEAD_DIM), jnp.float32
        )

    @pl.loop(0, rows // query_tile)
    def _(index):
        offset = pl.multiple_of(index * query_tile, query_tile)
        places = ring_slices(order_ref, rows, index * (query_tile // length), query_tile // length)
        queries = stack_heads(jnp.concatenate([query_ref[place, :] for place in places], axis=0))
        grads = stack_heads(grad_ref[pl.ds(offset, query_tile), :])
        outs = stack_heads(out_ref[pl.ds(offset, query_tile), :])
        delta = jnp.sum((grads.astype(jnp.float32) * outs).T, axis=0, keepdims=True)
        log_total = stack_lanes(total_ref[:, pl.ds(offset, query_tile)])
        start = block_ref[0] * rows + offset

        def step(tile, query_grad, masked):
            here = ring_slices(order_ref, rows, tile * (key_tile // length), key_tile // length)
            keys = jnp.concatenate([key_value_ref[place, :HEAD_DIM] for place in here], axis=0)
            values = jnp.concatenate([key_value_ref[place, HEAD_DIM:] for place in here], axis=0)
            weights = jnp.exp2(last_dims(keys, queries) * scale - log_total)
            if masked:
                seen = visible_keys(weights.shape, tile * key_tile, start, query_tile)
                weights = jnp.where(seen, weights, 0.0)
            value_part = plain_dot(weights.astype(jnp.bfloat16), grads)
            score_grad = (weights * (last_dims(values, grads) - delta)).astype(jnp.bfloat16)
            key_part = plain_dot(score_grad, queries) * score_scale
            part = jnp.concatenate([key_part, value_part], axis=1)
            for i, place in enumerate(here):
                key_value_grad_ref[place, :] += part[i * length : (i + 1) * length]
            return query_grad + first_dims(score_grad, keys)

        full = lax.div(start, key_tile)
        query_grad = lax.fori_loop(
            0,
            full,
            lambda tile, state: step(tile, state, False),
            jnp.zeros((wide, HEAD_DIM), jnp.float32),
        )
        query_grad = step(full, query_grad, True) * score_scale
        for i, place in enumerate(places):
            cosine = cosine_ref[place, :]
            sine = sine_ref[place, :]
            for head in range(heads):
                begin = head * query_tile + i * length
                part = query_grad[begin : begin + length]
                turned = part * cosine - pltpu.roll(part, HEAD_DIM // 2, 1) * sine
                query_grad_ref[place, head * HEAD_DIM : (head + 1) * HEAD_DIM] = turned.astype(
                    jnp.bfloat16
                )


def attention_forward(block_index, order, queries, keys):
    rows, wide = queries.shape
    return pl.pallas_call(
        functools.partial(forward_kernel, math.gcd(rows, 1024), math.gcd(rows, 1024)),
        out_shape=(
            jax.ShapeDtypeStruct((rows, wide), jnp.float32),
            jax.ShapeDtypeStruct((rows, wide), jnp.bfloat16),
            jax.ShapeDtypeStruct((wide // HEAD_DIM, rows), jnp.float32),
        ),
        in_specs=in_smem(2) + in_vmem(2),
        out_specs=tuple(in_vmem(3)),
        **kernel_options(),
    )(block_index.reshape(1), order, queries, keys)


def attention_backward(block_index, order, queries, keys, outs, grads, log_total, cosine, sine):
    rows, wide = queries.shape
    return pl.pallas_call(
        functools.partial(backward_kernel, math.gcd(rows, 512), math.gcd(rows, 512)),
        out_shape=(
            jax.ShapeDtypeStruct((rows, wide), jnp.bfloat16),
            jax.ShapeDtypeStruct((keys.shape[0], 2 * HEAD_DIM), jnp.float32),
        ),
        in_specs=in_smem(2) + in_vmem(7),
        out_specs=tuple(in_vmem(2)),
        **kernel_options(),
    )(block_index.reshape(1), order, queries, keys, outs, grads, log_total, cosine, sine)


def dispatch_kernel(piece_count, experts, *refs):
    pieces = refs[:piece_count]
    chosen_ref, whole_ref, rows_ref = refs[piece_count:]
    start = 0
    for piece in pieces:
        whole_ref[start : start + piece.shape[0], :] = piece[...]
        start += piece.shape[0]
    length = chosen_ref.shape[2]
    capacity = chosen_ref.shape[1] // experts
    for block in range(chosen_ref.shape[0]):
        picked = plain_dot(chosen_ref[block], whole_ref[block * length : (block + 1) * length, :])
        picked = picked.astype(jnp.bfloat16)
        for expert in range(experts):
            rows_ref[expert, block * capacity : (block + 1) * capacity, :] = picked[
                expert * capacity : (expert + 1) * capacity
            ]


def dispatch(pieces, chosen, experts):
    rows = sum(piece.shape[0] for piece in pieces)
    width = pieces[0].shape[1]
    blocks, slots, _ = chosen.shape
    return pl.pallas_call(
        functools.partial(dispatch_kernel, len(pieces), experts),
        out_shape=(
            jax.ShapeDtypeStruct((rows, width), jnp.bfloat16),
            jax.ShapeDtypeStruct((experts, blocks * (slots // experts), width), jnp.bfloat16),
        ),
        in_specs=in_vmem(len(pieces) + 1),
        out_specs=tuple(in_vmem(2)),
        **kernel_options(),
    )(*pieces, chosen)


def hidden_tiles(width, tile):
    return [slice(start, min(start + tile, width)) for start in range(0, width, tile)]


def slopes(pre_gate, pre_up):
    sigmoid = 1.0 / (1.0 + jnp.exp(-pre_gate))
    silu = pre_gate * sigmoid
    return silu * pre_up, pre_up * sigmoid * (1.0 + pre_gate * (1.0 - sigmoid)), silu


def expert_forward_kernel(rows_ref, weight_gate_ref, weight_up_ref, act_ref, by_gate_ref, by_up_ref):
    for here in hidden_tiles(act_ref.shape[2], 256):
        pre_gate = plain_dot(rows_ref[0], weight_gate_ref[0, :, here])
        pre_up = plain_dot(rows_ref[0], weight_up_ref[0, :, here])
        act, by_gate, by_up = slopes(pre_gate, pre_up)
        act_ref[0, :, here] = act.astype(jnp.bfloat16)
        by_gate_ref[0, :, here] = by_gate.astype(jnp.bfloat16)
        by_up_ref[0, :, here] = by_up.astype(jnp.bfloat16)


def one_expert(*shape):
    return pl.BlockSpec((1,) + shape, lambda expert: (expert, 0, 0))


def expert_forward(rows, weight_gate, weight_up):
    experts, count, width = rows.shape
    hidden = weight_gate.shape[2]
    return pl.pallas_call(
        expert_forward_kernel,
        grid=(experts,),
        out_shape=(jax.ShapeDtypeStruct((experts, count, hidden), jnp.bfloat16),) * 3,
        in_specs=[one_expert(count, width), one_expert(width, hidden), one_expert(width, hidden)],
        out_specs=(one_expert(count, hidden),) * 3,
        **kernel_options(),
    )(rows, weight_gate, weight_up)


def expert_backward_kernel(
    first_ref,
    grad_ref,
    gate_ref,
    act_ref,
    by_gate_ref,
    by_up_ref,
    weight_gate_ref,
    weight_up_ref,
    weight_down_ref,
    gate_grad_ref,
    up_grad_ref,
    row_grad_ref,
):
    width = weight_gate_ref.shape[1]
    count = grad_ref.shape[1]
    score = jnp.zeros((count, 1), jnp.float32)
    for here in hidden_tiles(act_ref.shape[2], 256):
        act_grad = last_dims(grad_ref[0], weight_down_ref[0, here, :])
        score = score + jnp.sum(
            act_ref[0, :, here].astype(jnp.float32) * act_grad, axis=1, keepdims=True
        )
        act_grad = act_grad * gate_ref[0]
        gate_grad_ref[0, :, here] = (act_grad * by_gate_ref[0, :, here].astype(jnp.float32)).astype(
            jnp.bfloat16
        )
        up_grad_ref[0, :, here] = (act_grad * by_up_ref[0, :, here].astype(jnp.float32)).astype(
            jnp.bfloat16
        )

    for here in hidden_tiles(width, 512):
        row_grad_ref[0, :, here] = (
            last_dims(gate_grad_ref[0], weight_gate_ref[0, here, :])
            + last_dims(up_grad_ref[0], weight_up_ref[0, here, :])
        ).astype(jnp.bfloat16)

    lane = lax.broadcasted_iota(jnp.int32, (count, HEAD_DIM), 1)
    own = first_ref[0] + pl.program_id(0)
    row_grad_ref[0, :, width:] = jnp.where(lane == own, score, 0.0).astype(jnp.bfloat16)


def expert_backward(first_expert, grads, gates, act, by_gate, by_up, weight_gate, weight_up, weight_down):
    experts, count, width = grads.shape
    hidden = act.shape[2]
    low = one_expert(count, hidden)
    return pl.pallas_call(
        expert_backward_kernel,
        grid=(experts,),
        out_shape=(
            jax.ShapeDtypeStruct((experts, count, hidden), jnp.bfloat16),
            jax.ShapeDtypeStruct((experts, count, hidden), jnp.bfloat16),
            jax.ShapeDtypeStruct((experts, count, width + HEAD_DIM), jnp.bfloat16),
        ),
        in_specs=in_smem(1)
        + [
            one_expert(count, width),
            one_expert(count, 1),
            low,
            low,
            low,
            one_expert(width, hidden),
            one_expert(width, hidden),
            one_expert(hidden, width),
        ],
        out_specs=(low, low, one_expert(count, width + HEAD_DIM)),
        **kernel_options(),
    )(first_expert.reshape(1), grads, gates, act, by_gate, by_up, weight_gate, weight_up, weight_down)


def result_kernel(act_ref, gate_ref, weight_ref, out_ref):
    for here in hidden_tiles(out_ref.shape[2], 512):
        result = plain_dot(act_ref[0], weight_ref[0, :, here]).astype(jnp.bfloat16)
        out_ref[0, :, here] = (result.astype(jnp.float32) * gate_ref[0]).astype(jnp.bfloat16)


def expert_results(act, gates, weight_down):
    experts, count, hidden = act.shape
    width = weight_down.shape[2]

    def one(*shape):
        return pl.BlockSpec((1,) + shape, lambda expert: (expert, 0, 0))

    return pl.pallas_call(
        result_kernel,
        grid=(experts,),
        out_shape=jax.ShapeDtypeStruct((experts, count, width), jnp.bfloat16),
        in_specs=[one(count, hidden), one(count, 1), one(hidden, width)],
        out_specs=one(count, width),
        **kernel_options(),
    )(act, gates, weight_down)


def combine_kernel(turned, chosen_ref, values_ref, left_ref, right_ref, out_ref):
    width = right_ref.shape[0] if turned else right_ref.shape[1]
    experts = values_ref.shape[0]
    length = chosen_ref.shape[1]
    capacity = chosen_ref.shape[2] // experts
    blocks = chosen_ref.shape[0]

    def slots(block, here):
        values = [
            values_ref[expert, block * capacity : (block + 1) * capacity, here]
            for expert in range(experts)
        ]
        return plain_dot(chosen_ref[block], jnp.concatenate(values, axis=0))

    for here in hidden_tiles(width, 512):
        shared = (
            last_dims(left_ref[...], right_ref[here, :])
            if turned
            else plain_dot(left_ref[...], right_ref[:, here])
        )
        for block in range(blocks):
            rows = slice(block * length, (block + 1) * length)
            out_ref[rows, here] = (shared[rows] + slots(block, here)).astype(jnp.bfloat16)

    if out_ref.shape[1] > width:
        for block in range(blocks):
            out_ref[block * length : (block + 1) * length, width:] = slots(
                block, slice(width, out_ref.shape[1])
            ).astype(jnp.bfloat16)


def combine(chosen, values, left, right, turned):
    blocks, length, slots = chosen.shape
    experts, _, wide = values.shape
    capacity = slots // experts
    some = math.gcd(blocks, 2)
    return pl.pallas_call(
        functools.partial(combine_kernel, turned),
        grid=(blocks // some,),
        out_shape=jax.ShapeDtypeStruct((blocks * length, wide), jnp.bfloat16),
        in_specs=[
            pl.BlockSpec((some, length, slots), lambda i: (i, 0, 0)),
            pl.BlockSpec((experts, some * capacity, wide), lambda i: (0, i, 0)),
            pl.BlockSpec((some * length, left.shape[1]), lambda i: (i, 0)),
            pl.BlockSpec(right.shape, lambda i: (0, 0)),
        ],
        out_specs=pl.BlockSpec((some * length, wide), lambda i: (i, 0)),
        **kernel_options(),
    )(chosen, values, left, right)


def shared_kernel(normed_ref, grad_ref, weight_ref, down_ref, act_ref, both_ref):
    hidden = act_ref.shape[1]
    pre_gate = plain_dot(normed_ref[...], weight_ref[:, :hidden])
    pre_up = plain_dot(normed_ref[...], weight_ref[:, hidden:])
    act_grad = last_dims(grad_ref[...], down_ref[...])
    act, by_gate, by_up = slopes(pre_gate, pre_up)
    act_ref[...] = act.astype(jnp.bfloat16)
    both_ref[:, :hidden] = (act_grad * by_gate).astype(jnp.bfloat16)
    both_ref[:, hidden:] = (act_grad * by_up).astype(jnp.bfloat16)


def shared_pass(normed, grads, weight, down):
    rows, width = normed.shape
    hidden = down.shape[0]
    some = math.gcd(rows, 256)

    def part(columns):
        return pl.BlockSpec((some, columns), lambda i: (i, 0))

    return pl.pallas_call(
        shared_kernel,
        grid=(rows // some,),
        out_shape=(
            jax.ShapeDtypeStruct((rows, hidden), jnp.bfloat16),
            jax.ShapeDtypeStruct((rows, 2 * hidden), jnp.bfloat16),
        ),
        in_specs=[
            part(width),
            part(width),
            pl.BlockSpec(weight.shape, lambda i: (0, 0)),
            pl.BlockSpec(down.shape, lambda i: (0, 0)),
        ],
        out_specs=(part(hidden), part(2 * hidden)),
        **kernel_options(),
    )(normed, grads, weight, down)


def part_kernel(scaled, added, core_ref, left_ref, right_ref, *refs):
    right = right_ref[0]
    if scaled:
        right = (right.astype(jnp.float32) * refs[0][0]).astype(jnp.bfloat16)
    total = first_dims(left_ref[0], right)
    if added:
        total = total + refs[-2][0, 0].astype(jnp.float32)
    refs[-1][0, 0] = total.astype(jnp.bfloat16)


def weight_parts(core, left, right, cut_left, gates=None, received=None, slices=1, number=0):
    chips = lax.axis_size("far")
    parts = 2 * chips * slices
    experts, count, left_width = left.shape
    right_width = right.shape[2]
    left_width, right_width = (
        (left_width // parts, right_width) if cut_left else (left_width, right_width // parts)
    )

    def spec(columns, cut):
        if cut:
            return pl.BlockSpec(
                (1, count, columns), lambda f, e, c: (e, 0, (2 * f + c[0]) * slices + number)
            )
        return pl.BlockSpec((1, count, columns), lambda f, e, c: (e, 0, 0))

    whole = pl.BlockSpec((1, 1, left_width, right_width), lambda f, e, c: (f, e, 0, 0))
    operands = [left, right]
    specs = [spec(left_width, cut_left), spec(right_width, not cut_left)]
    if gates is not None:
        operands.append(gates)
        specs.append(pl.BlockSpec((1, count, 1), lambda f, e, c: (e, 0, 0)))
    if received is not None:
        operands.append(received)
        place = (lambda f, e, c: (f, e, number, 0)) if cut_left else (lambda f, e, c: (f, e, 0, number))
        specs.append(pl.BlockSpec((1, 1, left_width, right_width), place))
    return pl.pallas_call(
        functools.partial(part_kernel, gates is not None, received is not None),
        grid_spec=pltpu.PrefetchScalarGridSpec(
            num_scalar_prefetch=1, grid=(chips, experts), in_specs=specs, out_specs=whole
        ),
        out_shape=jax.ShapeDtypeStruct((chips, experts, left_width, right_width), jnp.bfloat16),
        **kernel_options(),
    )(core.reshape(1), *operands)


def output_weight_kernel(piece_count, index_ref, core_ref, grad_ref, *refs):
    pieces = refs[:piece_count]
    keep_ref, send_ref = refs[piece_count:]
    wide = pieces[0].shape[1]
    half = piece_count // 2
    length = keep_ref.shape[1]
    some = min(wide, length)

    def part(piece, start):
        return first_dims(piece[...], grad_ref[start : start + piece.shape[0], :])

    def place(total, first):
        target = lax.div(first, length)
        chip = lax.div(target, 2)
        offset = pl.multiple_of(lax.rem(first, length), some)
        mine = lax.rem(target, 2) == core_ref[0]

        @pl.when(mine)
        def _():
            keep_ref[chip, pl.ds(offset, some), :] = total

        @pl.when(jnp.logical_not(mine))
        def _():
            send_ref[chip, pl.ds(offset, some), :] = total

    for block in range(index_ref.shape[0]):
        if block < half:
            total = part(pieces[block], 0)
        elif block == half:
            total = part(pieces[half], 0) + part(pieces[half + 1], pieces[half].shape[0])
        else:
            total = part(pieces[block + 1], 0)
        total = total.astype(jnp.bfloat16)
        for start in range(0, wide, some):
            place(total[start : start + some], index_ref[block] * wide + start)


def output_weight(index, core, grads, pieces):
    chips = lax.axis_size("far")
    length = index.shape[0] * pieces[0].shape[1] // (2 * chips)
    return pl.pallas_call(
        functools.partial(output_weight_kernel, len(pieces)),
        out_shape=(jax.ShapeDtypeStruct((chips, length, grads.shape[1]), jnp.bfloat16),) * 2,
        in_specs=in_smem(2) + in_vmem(len(pieces) + 1),
        out_specs=tuple(in_vmem(2)),
        **kernel_options(),
    )(index, core.reshape(1), grads, *pieces)


def hidden_send_kernel(own, chips, gate_ref, up_ref, out_ref):
    spread = out_ref.shape[0]
    wide = out_ref.shape[2] // 2
    piece = own // chips
    blank = [jnp.zeros((gate_ref.shape[0], wide - own), jnp.float32)] if wide > own else []
    for start, weight_ref in ((0, gate_ref), (wide, up_ref)):
        weight = weight_ref[...].astype(jnp.float32)
        for device in range(spread):
            columns = [
                weight[:, (chip * spread + device) * piece : (chip * spread + device + 1) * piece]
                for chip in range(chips)
            ]
            out_ref[device, :, start : start + wide] = jnp.concatenate(
                columns + blank, axis=1
            ).astype(jnp.bfloat16)


def hidden_send(gate, up, own, wide, chips, spread):
    return pl.pallas_call(
        functools.partial(hidden_send_kernel, own, chips),
        out_shape=jax.ShapeDtypeStruct((spread, gate.shape[0], 2 * wide), jnp.bfloat16),
        in_specs=in_vmem(2),
        out_specs=pl.BlockSpec(memory_space=pltpu.VMEM),
        **kernel_options(),
    )(gate, up)


def hidden_home_kernel(own, chips, back_ref, gate_ref, up_ref):
    spread = back_ref.shape[0]
    wide = back_ref.shape[2] // 2
    piece = own // chips
    for start, out_ref in ((0, gate_ref), (wide, up_ref)):
        values = [
            back_ref[device, :, start : start + wide].astype(jnp.float32)
            for device in range(spread)
        ]
        out_ref[...] = jnp.concatenate(
            [
                values[device][:, chip * piece : (chip + 1) * piece]
                for chip in range(chips)
                for device in range(spread)
            ],
            axis=1,
        )


def hidden_home(back, own, chips):
    spread, rows, _ = back.shape
    return pl.pallas_call(
        functools.partial(hidden_home_kernel, own, chips),
        out_shape=(jax.ShapeDtypeStruct((rows, own * spread), jnp.float32),) * 2,
        in_specs=in_vmem(1),
        out_specs=tuple(in_vmem(2)),
        **kernel_options(),
    )(back)


def dense_home_kernel(back_ref, weight_ref, gain_ref, qkv_ref, out_ref, small_ref, gain_grad_ref):
    spread, _, wide = back_ref.shape
    own = QUERY_HEADS * HEAD_DIM // spread
    repeat = spread // KEY_VALUE_HEADS
    out_wide = out_ref.shape[1] // spread
    score = jnp.zeros(gain_ref.shape, jnp.float32)

    def keep(score, start, values):
        columns = slice(start, start + values.shape[1])
        qkv_ref[:, columns] = values * gain_ref[...]
        weight = weight_ref[:, columns].astype(jnp.float32)
        return score + jnp.sum(weight * values, axis=1, keepdims=True)

    small = jnp.zeros(small_ref.shape, jnp.float32)
    for device in range(spread):
        score = keep(score, device * own, back_ref[device, :, :own].astype(jnp.float32))
        start = own + 2 * HEAD_DIM
        out_ref[:, device * out_wide : (device + 1) * out_wide] = back_ref[
            device, :, start : start + out_wide
        ].astype(jnp.float32)
        small = small + back_ref[device, :, start + out_wide :].astype(jnp.float32)
    for part in range(2):
        for head in range(KEY_VALUE_HEADS):
            start = own + part * HEAD_DIM
            values = sum(
                back_ref[head * repeat + i, :, start : start + HEAD_DIM].astype(jnp.float32)
                for i in range(repeat)
            )
            place = QUERY_HEADS * HEAD_DIM + (part * KEY_VALUE_HEADS + head) * HEAD_DIM
            score = keep(score, place, values)
    small_ref[...] = small
    gain_grad_ref[...] = score


def dense_home(back, weight, gain, width):
    rows, qkv_width = weight.shape
    return pl.pallas_call(
        dense_home_kernel,
        out_shape=(
            jax.ShapeDtypeStruct((rows, qkv_width), jnp.float32),
            jax.ShapeDtypeStruct((rows, width), jnp.float32),
            jax.ShapeDtypeStruct((rows, HEAD_DIM), jnp.float32),
            jax.ShapeDtypeStruct((rows, 1), jnp.float32),
        ),
        in_specs=in_vmem(3),
        out_specs=tuple(in_vmem(4)),
        **kernel_options(),
    )(back, weight, gain)


def product_kernel(left_ref, right_ref, out_ref):
    for here in hidden_tiles(out_ref.shape[0], 512):
        out_ref[here, :] = first_dims(left_ref[:, here], right_ref[...]).astype(jnp.bfloat16)


def row_product(left, right, columns):
    return pl.pallas_call(
        product_kernel,
        out_shape=jax.ShapeDtypeStruct((columns, right.shape[1]), jnp.bfloat16),
        in_specs=in_vmem(2),
        out_specs=pl.BlockSpec(memory_space=pltpu.VMEM),
        **kernel_options(),
    )(left, right)


def widen_kernel(*refs):
    out_ref = refs[-1]
    start = 0
    for part_ref in refs[:-1]:
        rows = part_ref.shape[1]
        out_ref[0, start : start + rows, :] = part_ref[0].astype(jnp.float32)
        start += rows


def widen(*parts):
    experts, _, columns = parts[0].shape
    rows = sum(part.shape[1] for part in parts)
    return pl.pallas_call(
        widen_kernel,
        grid=(experts,),
        out_shape=jax.ShapeDtypeStruct((experts, rows, columns), jnp.float32),
        in_specs=[one_expert(part.shape[1], columns) for part in parts],
        out_specs=one_expert(rows, columns),
        **kernel_options(),
    )(*parts)


def project_back_kernel(
    query_ref, own_ref, last_ref, cosine_ref, sine_ref, weight_ref, projected_ref, out_ref
):
    wide = query_ref.shape[1]
    projected_ref[:, :wide] = query_ref[...]
    total = own_ref[...] + last_ref[...].astype(jnp.float32)
    keys = total[:, :HEAD_DIM]
    turned = keys * cosine_ref[...] - pltpu.roll(keys, HEAD_DIM // 2, 1) * sine_ref[...]
    projected_ref[:, wide : wide + HEAD_DIM] = turned.astype(jnp.bfloat16)
    projected_ref[:, wide + HEAD_DIM :] = total[:, HEAD_DIM:].astype(jnp.bfloat16)
    for here in hidden_tiles(out_ref.shape[1], 512):
        out_ref[:, here] = last_dims(projected_ref[...], weight_ref[here, :]).astype(jnp.bfloat16)


def project_back(queries, own, last, cosine, sine, weight):
    rows = queries.shape[0]
    return pl.pallas_call(
        project_back_kernel,
        out_shape=(
            jax.ShapeDtypeStruct((rows, weight.shape[1]), jnp.bfloat16),
            jax.ShapeDtypeStruct((rows, weight.shape[0]), jnp.bfloat16),
        ),
        in_specs=in_vmem(6),
        out_specs=tuple(in_vmem(2)),
        **kernel_options(),
    )(queries, own, last, cosine, sine, weight)


def finish_kernel(first_ref, second_ref, own_ref, tokens_ref, grad_ref, out_ref):
    weighted = (
        first_ref[...].astype(jnp.float32)
        + second_ref[...].astype(jnp.float32)
        + own_ref[...].astype(jnp.float32)
    )
    inputs = tokens_ref[...].astype(jnp.float32)
    scale = lax.rsqrt(jnp.mean(inputs * inputs, axis=-1, keepdims=True) + EPSILON)
    inner_mean = jnp.mean(weighted * inputs, axis=-1, keepdims=True)
    out_ref[...] = grad_ref[...] + scale * weighted - inputs * (scale * scale * scale * inner_mean)


def finish(first, second, own, tokens, grads):
    return pl.pallas_call(
        finish_kernel,
        out_shape=jax.ShapeDtypeStruct(grads.shape, jnp.float32),
        in_specs=in_vmem(5),
        out_specs=pl.BlockSpec(memory_space=pltpu.VMEM),
        **kernel_options(),
    )(first, second, own, tokens, grads)


def body(
    tokens,
    attn_gain,
    query_key_value_weight,
    out_weight,
    ffn_gain,
    router_weight,
    shared_gate,
    shared_up,
    shared_down,
    routed_gate_weight,
    routed_up_weight,
    routed_down_weight,
    routes,
    cotangent,
):
    f32 = jnp.float32
    bf16 = jnp.bfloat16
    both = CONTEXT + ("experts",)
    context_count = context_size()
    spread = lax.axis_size("experts")
    context_index = lax.axis_index(CONTEXT)
    expert_index = lax.axis_index("experts")
    token_count, width = tokens.shape
    local_experts = routed_gate_weight.shape[0]
    experts_all = local_experts * spread
    rows = token_count * spread
    weight_rows = query_key_value_weight.shape[0]
    query_width = QUERY_HEADS * HEAD_DIM
    key_width = KEY_VALUE_HEADS * HEAD_DIM
    repeat_times = spread // KEY_VALUE_HEADS
    head_share = QUERY_HEADS // spread
    own_width = head_share * HEAD_DIM
    block_width = width // context_count

    def key_columns(weight):
        heads = weight.reshape(weight_rows, KEY_VALUE_HEADS, HEAD_DIM)
        return jnp.repeat(heads, repeat_times, axis=1)

    own_gain = attn_gain.astype(f32)[:, None]
    qkv_scaled = (query_key_value_weight.astype(f32) * own_gain).astype(bf16)
    qkv_send = jnp.concatenate(
        [
            qkv_scaled[:, :query_width].reshape(weight_rows, spread, own_width),
            key_columns(qkv_scaled[:, query_width : query_width + key_width]),
            key_columns(qkv_scaled[:, query_width + key_width :]),
        ],
        axis=2,
    ).transpose(1, 0, 2)
    hidden_piece = shared_down.shape[0]
    hidden_own = hidden_piece * context_count
    hidden_wide = -(-hidden_own // HEAD_DIM) * HEAD_DIM

    shared_send = hidden_send(
        shared_gate, shared_up, hidden_own, hidden_wide, context_count, spread
    )

    token_ring = RingGather(tokens)
    token_ring.step()
    position = context_index * rows + jnp.arange(rows, dtype=jnp.int32)
    position = ring_order(position.reshape(spread, token_count)).reshape(rows).astype(f32)
    half_width = HEAD_DIM // 2
    frequency = THETA ** (-jnp.arange(half_width, dtype=f32) * 2.0 / HEAD_DIM)
    angles = position[:, None] * frequency[None, :]
    cosine = jnp.cos(angles)
    sine = jnp.sin(angles)
    cosine = jnp.concatenate([cosine, cosine], axis=1)
    sine = jnp.concatenate([-sine, sine], axis=1)
    small = jnp.concatenate([ffn_gain[None], router_weight.T], axis=0)
    small = flip_double(small[None], CONTEXT)
    qkv_send = after(small, qkv_send)
    qkv_rows = to_experts(qkv_send).reshape(spread * weight_rows, -1)
    while small.shape[0] < context_count:
        small = flip_double(small, CONTEXT)
    small = jnp.concatenate([small.reshape(1, -1), routes.astype(bf16).reshape(1, -1)], axis=1)
    small, cosine, sine = meet([token_ring], small, cosine, sine)
    token_ring.step()
    (qkv_rows,) = meet([token_ring], qkv_rows)
    token_ring.step()
    qkv_far = far_gather(qkv_rows)
    qkv_far, out_weight = meet([token_ring], qkv_far, out_weight)
    token_ring.step()
    qkv_own = core_gather(qkv_far)
    (qkv_own,) = meet([token_ring], qkv_own)
    small = after(token_ring.latest(), small)

    out_full = lax.all_gather(out_weight, both, axis=0, tiled=True)
    normed_one, query_rows, key_value = project(
        token_ring.pieces(), qkv_own, cosine, sine, own_width
    )
    key_value = far_gather(key_value)
    small = flip_double(small, "experts")
    key_value, small = lax.optimization_barrier((key_value, small))
    key_value = core_gather(key_value)
    small = flip_double(small, "experts")
    place = ring_place(expert_index, spread)
    order = (ring_place(jnp.arange(spread, dtype=jnp.int32), spread) - place + spread) % spread
    attended, attended_low, log_total = attention_forward(
        context_index, order, query_rows, key_value
    )
    attended_low, small = lax.optimization_barrier((attended_low, small))
    attended_tok = (
        to_experts(attended_low.reshape(spread, token_count, own_width))
        .transpose(1, 0, 2)
        .reshape(token_count, query_width)
    )
    while small.shape[0] < spread:
        small = flip_double(small, "experts")
    attended_tok, small = lax.optimization_barrier((attended_tok, small))
    routes_block = small[:, -token_count * TOP :].reshape(spread, token_count, TOP)
    routes_block = routes_block.astype(jnp.int32).transpose(0, 2, 1)
    small = small[:, : -token_count * TOP].reshape(spread, context_count, -1, weight_rows)
    small = small.transpose(2, 1, 0, 3).reshape(-1, width)
    gain_two = small[0].astype(f32)
    router_full = small[1:]

    inputs = tokens.astype(f32)
    middle = inputs + jnp.dot(attended_tok, out_full, preferred_element_type=f32)
    scale_two = rms_scale(middle)
    normed_two = (middle * scale_two * gain_two).astype(bf16)
    normed_ring = RingGather(normed_two)
    normed_ring.step()
    routes_block, router_full, shared_down = meet(
        [normed_ring], routes_block, router_full, shared_down
    )

    normed_ring.step()
    down_far = far_gather(shared_down)
    first_expert = expert_index * local_experts
    own_ids = first_expert + jnp.arange(local_experts, dtype=jnp.int32)
    routes_block = ring_order(routes_block)
    member = jnp.any(routes_block[:, None] == own_ids[None, :, None, None], axis=2)
    counted = member.astype(jnp.int32)
    slot_index = jnp.cumsum(counted, axis=2) - counted
    capacity = token_count * TOP * 4 // (3 * experts_all)
    slot = jnp.arange(capacity, dtype=jnp.int32)
    chosen = member[:, :, None, :] & (slot_index[:, :, None, :] == slot[None, None, :, None])
    chosen_wide = chosen.astype(f32)
    slots = local_experts * capacity
    chosen_low = chosen.astype(bf16).reshape(spread, slots, token_count)
    chosen_back = chosen_low.transpose(0, 2, 1)
    down_far, chosen_low, chosen_wide, chosen_back = meet(
        [normed_ring], down_far, chosen_low, chosen_wide, chosen_back
    )
    normed_ring.step()
    down_own = jnp.pad(core_gather(down_far), ((0, hidden_wide - hidden_own), (0, 0)))
    (down_own,) = meet([normed_ring], down_own)
    normed_ring.step()
    (cotangent_late,) = meet([normed_ring], cotangent)
    grad_ring = RingGather(cotangent_late)
    grad_ring.step()
    normed_block, expert_rows = dispatch(normed_ring.pieces(), chosen_low, local_experts)

    (normed_block,) = meet([grad_ring], normed_block)
    grad_ring.step()
    router_probs = jax.nn.softmax(dot_last(normed_block, router_full), axis=-1)
    gate_tokens = (
        lax.dynamic_slice_in_dim(router_probs, first_expert, local_experts, 1)
        .reshape(spread, token_count, local_experts)
        .transpose(0, 2, 1)
    )
    gates = jnp.sum(chosen_wide * gate_tokens[:, :, None, :], axis=3)
    gates = gates.transpose(1, 0, 2).reshape(local_experts, spread * capacity, 1)
    expert_rows = after(gates, expert_rows)
    act, by_gate, by_up = expert_forward(expert_rows, routed_gate_weight, routed_up_weight)
    act, gates = meet([grad_ring], act, gates)
    grad_ring.step()
    weighted_y = expert_results(act, gates, routed_down_weight)
    (weighted_y,) = meet([grad_ring], weighted_y)
    grad_ring.step()
    chosen_low, shared_send = meet([grad_ring], chosen_low, shared_send)
    grad_block, grad_rows = dispatch(grad_ring.pieces(), chosen_low, local_experts)

    own_core = lax.axis_index("core")
    other_core = 1 - own_core
    shared_rows = to_experts(shared_send).reshape(spread * weight_rows, -1)
    down_parts = weight_parts(other_core, act, grad_rows, False, gates)
    down_parts, shared_rows, attended_late = lax.optimization_barrier(
        (down_parts, shared_rows, attended_low)
    )
    shared_far = far_gather(shared_rows)
    down_received = core_swap(down_parts)
    heads_ring = RingGather(attended_late)
    heads_ring.step()
    grad_rows, gates = after(down_parts, grad_rows, gates)
    expert_dg, expert_du, row_grad = expert_backward(
        first_expert,
        grad_rows,
        gates,
        act,
        by_gate,
        by_up,
        routed_gate_weight,
        routed_up_weight,
        routed_down_weight,
    )
    row_grad, shared_far, down_received = meet(
        [heads_ring], row_grad, shared_far, down_received
    )
    heads_ring.step()
    shared_own = core_gather(shared_far)
    shared_act, shared_both = shared_pass(normed_block, grad_block, shared_own, down_own)
    shared_act, shared_both = meet([heads_ring], shared_act, shared_both)
    heads_ring.step()
    grad_part = combine(chosen_back, row_grad, shared_both, shared_own, True)
    (grad_part,) = meet([heads_ring], grad_part)
    grad_scatter = RingScatter(grad_part)
    grad_scatter.step()
    heads_ring.step()
    expert_dg, expert_du, weighted_y, act = after(
        grad_part, expert_dg, expert_du, weighted_y, act
    )
    down_parts = weight_parts(own_core, act, grad_rows, False, gates, down_received)
    (down_parts,) = meet([grad_scatter, heads_ring], down_parts)
    down_sum = chips_sum(down_parts)
    grad_scatter.step()
    expert_dg = after(down_parts, expert_dg)
    gate_parts = weight_parts(other_core, expert_rows, expert_dg, True)
    shared_parts = weight_parts(
        other_core, after(gate_parts, normed_block)[None], shared_both[None], True
    )
    gate_parts, shared_parts = meet([grad_scatter], gate_parts, shared_parts)
    grad_scatter.step()
    gate_received = core_swap(gate_parts)
    shared_received = core_swap(shared_parts)
    weighted_y = after(shared_parts, weighted_y)
    out_part = combine(chosen_back, weighted_y, shared_act, down_own, False)
    out_part, gate_received = lax.optimization_barrier((out_part, gate_received))
    gate_parts = weight_parts(own_core, expert_rows, expert_dg, True, None, gate_received)
    gate_parts, shared_received, out_part = meet(
        [grad_scatter], gate_parts, shared_received, out_part
    )
    grad_scatter.step()
    expert_du = after(gate_parts, expert_du)
    up_parts = weight_parts(other_core, expert_rows, expert_du, True)
    shared_parts = weight_parts(
        own_core,
        after(up_parts, normed_block)[None],
        shared_both[None],
        True,
        None,
        shared_received,
    )
    up_parts, shared_parts, out_part = meet([grad_scatter], up_parts, shared_parts, out_part)
    gathered = grad_scatter.total()
    out_scatter = RingScatter(out_part)
    out_scatter.step()
    shared_pair = chips_exchange(shared_parts)

    prob_grad = gathered[:, width : width + experts_all]
    probs_tok = router_probs[:token_count]
    logit_grad = (
        probs_tok * (prob_grad - jnp.sum(probs_tok * prob_grad, axis=-1, keepdims=True))
    ).astype(bf16)
    normed_grad = gathered[:, :width] + jnp.dot(
        logit_grad, router_full, preferred_element_type=f32
    )
    grad_final = cotangent.astype(f32)
    weighted = normed_grad * gain_two
    inner_mean = jnp.mean(weighted * middle, axis=-1, keepdims=True)
    middle_grad = (
        grad_final
        + scale_two * weighted
        - middle * scale_two * scale_two * scale_two * inner_mean
    )
    gain_rows = (normed_grad * middle * scale_two).astype(bf16)
    branch_grad = middle_grad.astype(bf16)
    attended_grad = dot_last(branch_grad, out_full).astype(bf16)
    (attended_grad,) = meet([out_scatter], attended_grad)
    grad_heads = to_experts(
        attended_grad.reshape(token_count, spread, own_width).transpose(1, 0, 2)
    ).reshape(rows, own_width)
    lane = jnp.arange(HEAD_DIM, dtype=jnp.int32)[None, :]
    gain_column = jnp.broadcast_to(lane == experts_all, (token_count, HEAD_DIM)).astype(bf16)
    small_left = jnp.concatenate([normed_two, gain_rows], axis=0)
    small_right = jnp.concatenate(
        [jnp.pad(logit_grad, ((0, 0), (0, HEAD_DIM - experts_all))), gain_column], axis=0
    )
    small_left, small_right, expert_du = after(attended_grad, small_left, small_right, expert_du)
    up_received = core_swap(up_parts)
    slices = 2 if block_width % (2 * HEAD_DIM) == 0 else 1
    up_parts = [
        weight_parts(own_core, expert_rows, expert_du, True, None, up_received, slices, number)
        for number in range(slices)
    ]
    small_parts = weight_parts(other_core, small_left[None], small_right[None], True)
    branch_late, up_parts = after(small_parts, branch_grad, up_parts)
    branch_columns = to_experts(
        branch_late.reshape(token_count, spread, own_width).transpose(1, 0, 2)
    ).reshape(rows, own_width)
    grad_heads, small_parts, up_parts = lax.optimization_barrier((grad_heads, small_parts, up_parts))

    out_scatter.step()
    small_received = core_swap(small_parts)
    query_grad, key_value_all = attention_backward(
        context_index,
        order,
        query_rows,
        key_value,
        attended,
        grad_heads,
        log_total,
        cosine,
        sine,
    )
    key_value_all, branch_columns, small_received, down_sum, shared_last = meet(
        [out_scatter], key_value_all, branch_columns, small_received, down_sum, shared_pair[1]
    )
    gate_sum = chips_sum(gate_parts)
    key_value_all = key_value_all.reshape(context_count, rows, -1)
    key_value_received = core_exchange(block_parts(key_value_all))
    key_value_sums = block_sums(key_value_all, key_value_received)
    (key_value_sums,) = lax.optimization_barrier((key_value_sums,))
    key_value_own, key_value_last = far_exchange(key_value_sums)
    out_scatter.first = after(key_value_sums, out_scatter.first)
    out_scatter.step()
    branch_columns, shared_last, small_left = after(
        key_value_sums, branch_columns, shared_last, small_left
    )
    index = ring_index(place + jnp.arange(spread, dtype=jnp.int32), spread)
    out_keep, out_send = output_weight(index, own_core, branch_columns, heads_ring.pieces())
    small_parts = weight_parts(
        own_core, small_left[None], small_right[None], True, None, small_received
    )
    shared_own_part = both_halves((shared_pair[0].astype(f32), shared_last)).astype(bf16)
    shared_back = to_experts(shared_own_part.reshape(spread, weight_rows, -1))
    key_value_last, out_keep, out_send, small_parts, gate_sum, shared_act = meet(
        [out_scatter], key_value_last, out_keep, out_send, small_parts, gate_sum, shared_act
    )
    up_first = chips_sum(up_parts[0])
    projected_grad, input_part = project_back(
        query_grad, key_value_own, key_value_last, cosine, sine, qkv_own
    )
    input_scatter = RingScatter(input_part)
    input_scatter.step()
    out_received = core_swap(out_send)
    normed_one = after(input_scatter.sent, normed_one)
    qkv_parts = weight_parts(other_core, normed_one[None], projected_grad[None], True)
    qkv_received = core_swap(qkv_parts)
    qkv_parts = weight_parts(
        own_core, normed_one[None], projected_grad[None], True, None, qkv_received
    )
    qkv_parts, out_received, shared_back = meet(
        [input_scatter, out_scatter], qkv_parts, out_received, shared_back
    )
    input_scatter.step()
    qkv_parts, out_received, shared_back, out_scatter.first = after(
        input_scatter.sent, qkv_parts, out_received, shared_back, out_scatter.first
    )
    out_scatter.step()
    out_sums = out_keep.astype(f32) + out_received.astype(f32)
    dense_parts = jnp.concatenate(
        [qkv_parts[:, 0], out_sums.astype(bf16), small_parts[:, 0]], axis=2
    )
    dense_pair = chips_exchange(dense_parts)
    down_sum, shared_act, shared_back = after(dense_parts, down_sum, shared_act, shared_back)
    shared_gate_grad, shared_up_grad = hidden_home(shared_back, hidden_own, context_count)
    expert_down_grad = widen(after(shared_gate_grad, down_sum))
    shared_down_sum = row_product(shared_act, after(expert_down_grad, grad_block), hidden_own)
    shared_down_sum = shared_down_sum.reshape(context_count, hidden_piece, width)
    shared_down_sum, shared_gate_grad = meet(
        [input_scatter, out_scatter], shared_down_sum, shared_gate_grad
    )
    input_scatter.step()
    gate_sum, shared_down_sum = after(input_scatter.sent, gate_sum, shared_down_sum)
    shared_down_received = core_exchange(block_parts(shared_down_sum))
    expert_gate_grad = widen(gate_sum)
    expert_gate_grad, dense_last, shared_down_received = meet(
        [input_scatter], expert_gate_grad, dense_pair[1], shared_down_received
    )
    input_scatter.step()
    up_later = [chips_sum(after((dense_last, up_first), part)) for part in up_parts[1:]]
    dense_last, out_scatter.first, shared_down_received = after(
        input_scatter.sent, dense_last, out_scatter.first, shared_down_received
    )
    dense_sum = both_halves((dense_pair[0].astype(f32), dense_last)).astype(bf16)
    dense_back = to_experts(dense_sum.reshape(spread, weight_rows, -1))
    shared_down_pair = far_exchange(block_sums(shared_down_sum, shared_down_received))
    dense_back, shared_down_pair = meet([input_scatter], dense_back, shared_down_pair)
    shared_down_grad = both_halves(shared_down_pair)
    layer_out = (middle + out_scatter.total()).astype(bf16)
    expert_up_grad = widen(up_first, *up_later)
    qkv_weight_grad, out_weight_grad, small_grad, attn_gain_grad = dense_home(
        dense_back, query_key_value_weight, own_gain, width
    )
    attn_gain_grad = attn_gain_grad[:, 0]
    router_weight_grad = small_grad[:, :experts_all]
    ffn_gain_grad = small_grad[:, experts_all]
    tokens_grad = finish(
        input_scatter.first, input_scatter.second, input_part[:token_count], tokens, middle_grad
    )
    return (
        layer_out,
        tokens_grad,
        attn_gain_grad,
        qkv_weight_grad,
        out_weight_grad,
        ffn_gain_grad,
        router_weight_grad,
        shared_gate_grad,
        shared_up_grad,
        shared_down_grad,
        expert_gate_grad,
        expert_up_grad,
        expert_down_grad,
    )


def solution(mesh):
    context_count, spread = mesh.devices.shape
    split = jax.sharding.Mesh(
        mesh.devices.reshape(context_count // 2, 2, spread), ("far", "core", "experts")
    )
    return jax.shard_map(
        body,
        mesh=split,
        in_specs=(
            P(("far", "core", "experts"), None),
            P(("far", "core", "experts")),
            P(("far", "core", "experts"), None),
            P(("far", "core", "experts"), None),
            P(("far", "core", "experts")),
            P(("far", "core", "experts"), None),
            P(("far", "core", "experts"), None),
            P(("far", "core", "experts"), None),
            P(("far", "core", "experts"), None),
            P("experts", None, None),
            P("experts", None, None),
            P("experts", None, None),
            P(("far", "core", "experts"), None),
            P(("far", "core", "experts"), None),
        ),
        out_specs=(
            P(("far", "core", "experts"), None),
            P(("far", "core", "experts"), None),
            P(("far", "core", "experts")),
            P(("far", "core", "experts"), None),
            P(("far", "core", "experts"), None),
            P(("far", "core", "experts")),
            P(("far", "core", "experts"), None),
            P(("far", "core", "experts"), None),
            P(("far", "core", "experts"), None),
            P(("far", "core", "experts"), None),
            P("experts", CONTEXT, None),
            P("experts", CONTEXT, None),
            P("experts", None, CONTEXT),
        ),
        check_vma=False,
    )
```

```python
import functools
import math

import jax
import jax.numpy as jnp
from jax import lax
from jax.experimental import pallas as pl
from jax.experimental.pallas import tpu as pltpu
from jax.sharding import PartitionSpec as P

QUERY_HEADS = 16
KEY_VALUE_HEADS = 4
HEAD_DIM = 128
TOP = 6


EPSILON = 1e-06
THETA = 10000.0
NEG_LARGE = -1e30
CONTEXT = ("far", "core")


def rms_scale(values):
    return lax.rsqrt(jnp.mean(values * values, axis=-1, keepdims=True) + EPSILON)


def norm_back(values, row_scale, gain_values, grad_out):
    weighted = grad_out * gain_values
    gain_grad = jnp.sum(grad_out * values * row_scale, axis=0)
    inner_mean = jnp.mean(weighted * values, axis=-1, keepdims=True)
    return (
        row_scale * weighted - values * row_scale * row_scale * row_scale * inner_mean,
        gain_grad,
    )


def inner_rows(left, right):
    return lax.dot_general(
        left, right, (((0,), (0,)), ((), ())), preferred_element_type=jnp.float32
    )


def dot_last(left, right):
    return lax.dot_general(
        left, right, (((1,), (1,)), ((), ())), preferred_element_type=jnp.float32
    )


def context_size():
    return lax.axis_size("far") * lax.axis_size("core")


def ring_pairs(count):
    order = [i for i in range(count) if i % 2 == 0] + [i for i in reversed(range(count)) if i % 2 == 1]
    right = [(order[i], order[(i + 1) % count]) for i in range(count)]
    left = [(order[i], order[(i - 1) % count]) for i in range(count)]
    return right, left


def ring_place(index, count):
    return jnp.where(index % 2 == 0, index // 2, count - 1 - index // 2)


def ring_index(place, count):
    place = (place + 2 * count) % count
    return jnp.where(place < count // 2, 2 * place, 2 * (count - 1 - place) + 1)


class RingGather:
    def __init__(self, block):
        self.count = lax.axis_size("experts")
        self.right, self.left = ring_pairs(self.count)
        self.half = block.shape[0] // 2
        self.block = block
        self.ahead = [block]
        self.behind = [block]
        self.far = None

    def step(self):
        if len(self.ahead) < self.count // 2:
            self.behind.append(lax.ppermute(self.behind[-1], "experts", self.right))
            self.ahead.append(lax.ppermute(self.ahead[-1], "experts", self.left))
        else:
            self.far = [
                lax.ppermute(self.behind[-1][: self.half], "experts", self.right),
                lax.ppermute(self.ahead[-1][self.half :], "experts", self.left),
            ]

    def latest(self):
        return self.far if self.far else [self.behind[-1], self.ahead[-1]]

    def replace(self, values):
        if self.far:
            self.far = list(values)
        else:
            self.behind[-1], self.ahead[-1] = values

    def pieces(self):
        return self.ahead + self.far + self.behind[:0:-1]


class RingScatter:
    def __init__(self, whole):
        self.count = lax.axis_size("experts")
        self.right, self.left = ring_pairs(self.count)
        self.whole = whole
        self.rows = whole.shape[0] // self.count
        self.half = self.rows // 2
        self.left_steps = self.count // 2
        self.first = None
        self.second = None

    def own(self, step):
        start = step % self.count * self.rows
        return self.whole[start : start + self.rows].astype(jnp.float32)

    def arrived(self):
        first = self.first.astype(jnp.float32)
        second = self.second.astype(jnp.float32)
        if self.left_steps == self.count // 2 - 1:
            blank = jnp.zeros((self.half, self.whole.shape[1]), jnp.float32)
            first = jnp.concatenate([first, blank], axis=0)
            second = jnp.concatenate([blank, second], axis=0)
        return first, second

    def step(self):
        if self.first is None:
            far = self.own(self.left_steps)
            first, second = far[: self.half], far[self.half :]
        else:
            first, second = self.arrived()
            first = first + self.own(self.left_steps)
            second = second + self.own(-self.left_steps)
        self.sent = (first.astype(jnp.bfloat16), second.astype(jnp.bfloat16))
        self.first = lax.ppermute(self.sent[0], "experts", self.right)
        self.second = lax.ppermute(self.sent[1], "experts", self.left)
        self.left_steps -= 1

    def latest(self):
        return [self.first, self.second]

    def replace(self, values):
        self.first, self.second = values

    def total(self):
        first, second = self.arrived()
        return first + second + self.own(0)


def meet(rings, *values):
    held, values = lax.optimization_barrier(([ring.latest() for ring in rings], values))
    for ring, value in zip(rings, held):
        ring.replace(value)
    return values


def ring_order(values):
    count = lax.axis_size("experts")
    place = ring_place(lax.axis_index("experts"), count)
    return jnp.concatenate(
        [
            lax.dynamic_slice_in_dim(values, ring_index(place + step, count), 1, 0)
            for step in range(count)
        ],
        axis=0,
    )


def flip_pairs(count, bit):
    return [(i, i ^ bit) for i in range(count)]


def flip_double(whole, axis):
    bit = whole.shape[0]
    received = lax.ppermute(whole, axis, flip_pairs(lax.axis_size(axis), bit))
    return jnp.where(
        (lax.axis_index(axis) // bit) % 2 == 0,
        jnp.concatenate([whole, received], axis=0),
        jnp.concatenate([received, whole], axis=0),
    )


def flip_gather(block, axis):
    whole = block[None]
    while whole.shape[0] < lax.axis_size(axis):
        whole = flip_double(whole, axis)
    return whole


def flip_half(values, axis, bit, dimension):
    shape = values.shape
    pairs = values.reshape(shape[:dimension] + (shape[dimension] // 2, 2) + shape[dimension + 1 :])
    mine = (lax.axis_index(axis) // bit) % 2
    sent = lax.dynamic_index_in_dim(pairs, 1 - mine, dimension + 1, keepdims=False)
    kept = lax.dynamic_index_in_dim(pairs, mine, dimension + 1, keepdims=False)
    return kept + lax.ppermute(sent, axis, flip_pairs(lax.axis_size(axis), bit))


def context_double(whole, bit):
    received = lax.ppermute(whole, CONTEXT, flip_pairs(context_size(), bit))
    low = (lax.axis_index(CONTEXT) // bit) % 2 == 0
    return jnp.stack(
        [jnp.where(low, whole, received), jnp.where(low, received, whole)], axis=1
    ).reshape((2 * whole.shape[0],) + whole.shape[1:])


def far_gather(block):
    whole = block[None]
    bit = context_size() // 2
    while bit > 1:
        whole = context_double(whole, bit)
        bit //= 2
    return whole


def core_gather(whole):
    return context_double(whole, 1).reshape(-1, whole.shape[-1])


def context_gather(block):
    return core_gather(far_gather(block))


def after(done, *values):
    values, _ = lax.optimization_barrier((values, done))
    return values[0] if len(values) == 1 else values


def core_parts(piece_of):
    count = context_size()
    index = lax.axis_index(CONTEXT)
    return {place: piece_of(index ^ (place + 1)) for place in range(count - 2, -1, -2)}


def core_exchange(parts):
    pairs = flip_pairs(context_size(), 1)
    return {
        place: lax.ppermute(part.astype(jnp.bfloat16), CONTEXT, pairs)
        for place, part in parts.items()
    }


def core_sums(piece_of, received):
    index = lax.axis_index(CONTEXT)
    return {
        place // 2: piece_of(index ^ place, part) for place, part in received.items()
    }


def far_exchange(pieces):
    count = context_size()
    bit = 2
    while 2 * bit < count:
        merged = {}
        for place in sorted(pieces, reverse=True):
            if place % 2 == 0:
                received = lax.ppermute(
                    pieces[place + 1].astype(jnp.bfloat16), CONTEXT, flip_pairs(count, bit)
                )
                merged[place // 2] = pieces[place] + received.astype(jnp.float32)
        pieces = merged
        bit *= 2
    last = lax.ppermute(pieces[1].astype(jnp.bfloat16), CONTEXT, flip_pairs(count, bit))
    return pieces[0], last


def both_halves(pair):
    return pair[0] + pair[1].astype(jnp.float32)


def core_swap(values):
    return lax.ppermute(values, "core", [(0, 1), (1, 0)])


def chips_sum(values):
    return lax.psum_scatter(values, "far", scatter_dimension=0, tiled=True)[0]


def chips_exchange(values):
    chip = lax.axis_index("far")
    pieces = {
        place: lax.dynamic_index_in_dim(values, chip ^ place, 0, keepdims=False)
        for place in range(values.shape[0])
    }
    return far_exchange(pieces)


def block_sums(values, received):
    def piece_of(target, part):
        return lax.dynamic_index_in_dim(values, target, 0, keepdims=False) + part.astype(jnp.float32)

    return core_sums(piece_of, received)


def block_parts(values):
    return core_parts(lambda target: lax.dynamic_index_in_dim(values, target, 0, keepdims=False))


def to_experts(stacked):
    return lax.all_to_all(stacked, "experts", split_axis=0, concat_axis=0, tiled=True)


def kernel_options(mebibytes=60):
    return dict(
        compiler_params=pltpu.CompilerParams(vmem_limit_bytes=mebibytes * 1024 * 1024),
        cost_estimate=pl.CostEstimate(flops=1024, bytes_accessed=1024, transcendentals=0),
    )


def in_vmem(count):
    return [pl.BlockSpec(memory_space=pltpu.VMEM)] * count


def in_smem(count):
    return [pl.BlockSpec(memory_space=pltpu.SMEM)] * count


def plain_dot(left, right):
    return jnp.dot(left, right, preferred_element_type=jnp.float32)


def last_dims(left, right):
    return lax.dot_general(
        left, right, (((1,), (1,)), ((), ())), preferred_element_type=jnp.float32
    )


def first_dims(left, right):
    return lax.dot_general(
        left, right, (((0,), (0,)), ((), ())), preferred_element_type=jnp.float32
    )


def project_kernel(piece_count, *refs):
    pieces = refs[:piece_count]
    weight_ref, cosine_ref, sine_ref, normed_ref, query_ref, key_value_ref = refs[piece_count:]
    start = 0
    for piece in pieces:
        rows = piece.shape[0]
        values = piece[...].astype(jnp.float32)
        scale = lax.rsqrt(jnp.mean(values * values, axis=-1, keepdims=True) + EPSILON)
        normed_ref[start : start + rows, :] = (values * scale).astype(jnp.bfloat16)
        start += rows
    query_width = query_ref.shape[1]
    heads = plain_dot(normed_ref[...], weight_ref[...])

    def rotated(offset):
        head = heads[:, offset : offset + HEAD_DIM]
        turned = pltpu.roll(head, HEAD_DIM // 2, 1)
        return (head * cosine_ref[...] + turned * sine_ref[...]).astype(jnp.bfloat16)

    for offset in range(0, query_width, HEAD_DIM):
        query_ref[:, offset : offset + HEAD_DIM] = rotated(offset)
    key_value_ref[:, :HEAD_DIM] = rotated(query_width)
    key_value_ref[:, HEAD_DIM:] = heads[:, query_width + HEAD_DIM :].astype(jnp.bfloat16)


def project(pieces, weight, cosine, sine, query_width):
    rows = sum(piece.shape[0] for piece in pieces)
    width = pieces[0].shape[1]
    return pl.pallas_call(
        functools.partial(project_kernel, len(pieces)),
        out_shape=(
            jax.ShapeDtypeStruct((rows, width), jnp.bfloat16),
            jax.ShapeDtypeStruct((rows, query_width), jnp.bfloat16),
            jax.ShapeDtypeStruct((rows, weight.shape[1] - query_width), jnp.bfloat16),
        ),
        in_specs=in_vmem(len(pieces) + 3),
        out_specs=tuple(in_vmem(3)),
        **kernel_options(),
    )(*pieces, weight, cosine, sine)


def stack_heads(values):
    heads = values.shape[1] // HEAD_DIM
    return jnp.concatenate(
        [values[:, i * HEAD_DIM : (i + 1) * HEAD_DIM] for i in range(heads)], axis=0
    )


def spread_heads(values, heads):
    rows = values.shape[0] // heads
    return jnp.concatenate([values[i * rows : (i + 1) * rows] for i in range(heads)], axis=1)


def stack_lanes(values):
    return jnp.concatenate([values[i : i + 1] for i in range(values.shape[0])], axis=1)


def visible_keys(shape, key_start, query_start, query_tile):
    key_pos = key_start + lax.broadcasted_iota(jnp.int32, shape, 0)
    query_pos = query_start + lax.rem(lax.broadcasted_iota(jnp.int32, shape, 1), query_tile)
    return query_pos >= key_pos


def ring_slices(order_ref, rows, first, count):
    spread = order_ref.shape[0]
    length = rows // spread
    found = []
    for i in range(count):
        number = first + i
        base = lax.div(number, spread) * rows
        place = order_ref[lax.rem(number, spread)] * length
        found.append(pl.ds(pl.multiple_of(base + place, length), length))
    return found


def forward_kernel(
    query_tile, key_tile, block_ref, order_ref, query_ref, key_value_ref, out_ref, low_ref, total_ref
):
    rows = query_ref.shape[0]
    length = rows // order_ref.shape[0]
    heads = query_ref.shape[1] // HEAD_DIM
    wide = heads * query_tile
    scale = HEAD_DIM ** (-0.5) * math.log2(math.e)

    @pl.loop(0, rows // query_tile)
    def _(index):
        offset = pl.multiple_of(index * query_tile, query_tile)
        places = ring_slices(order_ref, rows, index * (query_tile // length), query_tile // length)
        queries = stack_heads(jnp.concatenate([query_ref[place, :] for place in places], axis=0))
        start = block_ref[0] * rows + offset

        def step(tile, state, masked):
            top, total, summed = state
            here = ring_slices(order_ref, rows, tile * (key_tile // length), key_tile // length)
            keys = jnp.concatenate([key_value_ref[place, :HEAD_DIM] for place in here], axis=0)
            values = jnp.concatenate([key_value_ref[place, HEAD_DIM:] for place in here], axis=0)
            scores = last_dims(keys, queries) * scale
            if masked:
                seen = visible_keys(scores.shape, tile * key_tile, start, query_tile)
                scores = jnp.where(seen, scores, NEG_LARGE)
            new_top = jnp.maximum(top, jnp.max(scores, axis=0, keepdims=True))
            weights = jnp.exp2(scores - new_top)
            rescale = jnp.exp2(top - new_top)
            total = total * rescale + jnp.sum(weights, axis=0, keepdims=True)
            summed = summed * rescale + first_dims(values, weights.astype(jnp.bfloat16))
            return new_top, total, summed

        state = (
            jnp.full((1, wide), NEG_LARGE, jnp.float32),
            jnp.zeros((1, wide), jnp.float32),
            jnp.zeros((HEAD_DIM, wide), jnp.float32),
        )
        full = lax.div(start, key_tile)
        state = lax.fori_loop(0, full, lambda tile, state: step(tile, state, False), state)
        top, total, summed = step(full, state, True)
        result = spread_heads((summed / total).T, heads)
        out_ref[pl.ds(offset, query_tile), :] = result
        low_ref[pl.ds(offset, query_tile), :] = result.astype(jnp.bfloat16)
        log_total = top + jnp.log2(total)
        for i in range(heads):
            total_ref[i : i + 1, pl.ds(offset, query_tile)] = log_total[
                :, i * query_tile : (i + 1) * query_tile
            ]


def backward_kernel(
    query_tile,
    key_tile,
    block_ref,
    order_ref,
    query_ref,
    key_value_ref,
    out_ref,
    grad_ref,
    total_ref,
    cosine_ref,
    sine_ref,
    query_grad_ref,
    key_value_grad_ref,
):
    rows = query_ref.shape[0]
    length = rows // order_ref.shape[0]
    heads = query_ref.shape[1] // HEAD_DIM
    wide = heads * query_tile
    score_scale = HEAD_DIM ** (-0.5)
    scale = score_scale * math.log2(math.e)

    @pl.loop(0, key_value_ref.shape[0] // key_tile)
    def _(tile):
        key_start = pl.multiple_of(tile * key_tile, key_tile)
        key_value_grad_ref[pl.ds(key_start, key_tile), :] = jnp.zeros(
            (key_tile, 2 * HEAD_DIM), jnp.float32
        )

    @pl.loop(0, rows // query_tile)
    def _(index):
        offset = pl.multiple_of(index * query_tile, query_tile)
        places = ring_slices(order_ref, rows, index * (query_tile // length), query_tile // length)
        queries = stack_heads(jnp.concatenate([query_ref[place, :] for place in places], axis=0))
        grads = stack_heads(grad_ref[pl.ds(offset, query_tile), :])
        outs = stack_heads(out_ref[pl.ds(offset, query_tile), :])
        delta = jnp.sum((grads.astype(jnp.float32) * outs).T, axis=0, keepdims=True)
        log_total = stack_lanes(total_ref[:, pl.ds(offset, query_tile)])
        start = block_ref[0] * rows + offset

        def step(tile, query_grad, masked):
            here = ring_slices(order_ref, rows, tile * (key_tile // length), key_tile // length)
            keys = jnp.concatenate([key_value_ref[place, :HEAD_DIM] for place in here], axis=0)
            values = jnp.concatenate([key_value_ref[place, HEAD_DIM:] for place in here], axis=0)
            weights = jnp.exp2(last_dims(keys, queries) * scale - log_total)
            if masked:
                seen = visible_keys(weights.shape, tile * key_tile, start, query_tile)
                weights = jnp.where(seen, weights, 0.0)
            value_part = plain_dot(weights.astype(jnp.bfloat16), grads)
            score_grad = (weights * (last_dims(values, grads) - delta)).astype(jnp.bfloat16)
            key_part = plain_dot(score_grad, queries) * score_scale
            part = jnp.concatenate([key_part, value_part], axis=1)
            for i, place in enumerate(here):
                key_value_grad_ref[place, :] += part[i * length : (i + 1) * length]
            return query_grad + first_dims(score_grad, keys)

        full = lax.div(start, key_tile)
        query_grad = lax.fori_loop(
            0,
            full,
            lambda tile, state: step(tile, state, False),
            jnp.zeros((wide, HEAD_DIM), jnp.float32),
        )
        query_grad = step(full, query_grad, True) * score_scale
        for i, place in enumerate(places):
            cosine = cosine_ref[place, :]
            sine = sine_ref[place, :]
            for head in range(heads):
                begin = head * query_tile + i * length
                part = query_grad[begin : begin + length]
                turned = part * cosine - pltpu.roll(part, HEAD_DIM // 2, 1) * sine
                query_grad_ref[place, head * HEAD_DIM : (head + 1) * HEAD_DIM] = turned.astype(
                    jnp.bfloat16
                )


def attention_forward(block_index, order, queries, keys):
    rows, wide = queries.shape
    return pl.pallas_call(
        functools.partial(forward_kernel, math.gcd(rows, 1024), math.gcd(rows, 1024)),
        out_shape=(
            jax.ShapeDtypeStruct((rows, wide), jnp.float32),
            jax.ShapeDtypeStruct((rows, wide), jnp.bfloat16),
            jax.ShapeDtypeStruct((wide // HEAD_DIM, rows), jnp.float32),
        ),
        in_specs=in_smem(2) + in_vmem(2),
        out_specs=tuple(in_vmem(3)),
        **kernel_options(),
    )(block_index.reshape(1), order, queries, keys)


def attention_backward(block_index, order, queries, keys, outs, grads, log_total, cosine, sine):
    rows, wide = queries.shape
    return pl.pallas_call(
        functools.partial(backward_kernel, math.gcd(rows, 512), math.gcd(rows, 512)),
        out_shape=(
            jax.ShapeDtypeStruct((rows, wide), jnp.bfloat16),
            jax.ShapeDtypeStruct((keys.shape[0], 2 * HEAD_DIM), jnp.float32),
        ),
        in_specs=in_smem(2) + in_vmem(7),
        out_specs=tuple(in_vmem(2)),
        **kernel_options(),
    )(block_index.reshape(1), order, queries, keys, outs, grads, log_total, cosine, sine)


def dispatch_kernel(piece_count, experts, *refs):
    pieces = refs[:piece_count]
    chosen_ref, whole_ref, rows_ref = refs[piece_count:]
    start = 0
    for piece in pieces:
        whole_ref[start : start + piece.shape[0], :] = piece[...]
        start += piece.shape[0]
    length = chosen_ref.shape[2]
    capacity = chosen_ref.shape[1] // experts
    for block in range(chosen_ref.shape[0]):
        picked = plain_dot(chosen_ref[block], whole_ref[block * length : (block + 1) * length, :])
        picked = picked.astype(jnp.bfloat16)
        for expert in range(experts):
            rows_ref[expert, block * capacity : (block + 1) * capacity, :] = picked[
                expert * capacity : (expert + 1) * capacity
            ]


def dispatch(pieces, chosen, experts):
    rows = sum(piece.shape[0] for piece in pieces)
    width = pieces[0].shape[1]
    blocks, slots, _ = chosen.shape
    return pl.pallas_call(
        functools.partial(dispatch_kernel, len(pieces), experts),
        out_shape=(
            jax.ShapeDtypeStruct((rows, width), jnp.bfloat16),
            jax.ShapeDtypeStruct((experts, blocks * (slots // experts), width), jnp.bfloat16),
        ),
        in_specs=in_vmem(len(pieces) + 1),
        out_specs=tuple(in_vmem(2)),
        **kernel_options(),
    )(*pieces, chosen)


def hidden_tiles(width, tile):
    return [slice(start, min(start + tile, width)) for start in range(0, width, tile)]


def slopes(pre_gate, pre_up):
    sigmoid = 1.0 / (1.0 + jnp.exp(-pre_gate))
    silu = pre_gate * sigmoid
    return silu * pre_up, pre_up * sigmoid * (1.0 + pre_gate * (1.0 - sigmoid)), silu


def expert_forward_kernel(rows_ref, weight_gate_ref, weight_up_ref, act_ref, by_gate_ref, by_up_ref):
    for here in hidden_tiles(act_ref.shape[2], 256):
        pre_gate = plain_dot(rows_ref[0], weight_gate_ref[0, :, here])
        pre_up = plain_dot(rows_ref[0], weight_up_ref[0, :, here])
        act, by_gate, by_up = slopes(pre_gate, pre_up)
        act_ref[0, :, here] = act.astype(jnp.bfloat16)
        by_gate_ref[0, :, here] = by_gate.astype(jnp.bfloat16)
        by_up_ref[0, :, here] = by_up.astype(jnp.bfloat16)


def one_expert(*shape):
    return pl.BlockSpec((1,) + shape, lambda expert: (expert, 0, 0))


def expert_forward(rows, weight_gate, weight_up):
    experts, count, width = rows.shape
    hidden = weight_gate.shape[2]
    return pl.pallas_call(
        expert_forward_kernel,
        grid=(experts,),
        out_shape=(jax.ShapeDtypeStruct((experts, count, hidden), jnp.bfloat16),) * 3,
        in_specs=[one_expert(count, width), one_expert(width, hidden), one_expert(width, hidden)],
        out_specs=(one_expert(count, hidden),) * 3,
        **kernel_options(),
    )(rows, weight_gate, weight_up)


def expert_backward_kernel(
    first_ref,
    grad_ref,
    gate_ref,
    act_ref,
    by_gate_ref,
    by_up_ref,
    weight_gate_ref,
    weight_up_ref,
    weight_down_ref,
    gate_grad_ref,
    up_grad_ref,
    row_grad_ref,
):
    width = weight_gate_ref.shape[1]
    count = grad_ref.shape[1]
    score = jnp.zeros((count, 1), jnp.float32)
    for here in hidden_tiles(act_ref.shape[2], 256):
        act_grad = last_dims(grad_ref[0], weight_down_ref[0, here, :])
        score = score + jnp.sum(
            act_ref[0, :, here].astype(jnp.float32) * act_grad, axis=1, keepdims=True
        )
        act_grad = act_grad * gate_ref[0]
        gate_grad_ref[0, :, here] = (act_grad * by_gate_ref[0, :, here].astype(jnp.float32)).astype(
            jnp.bfloat16
        )
        up_grad_ref[0, :, here] = (act_grad * by_up_ref[0, :, here].astype(jnp.float32)).astype(
            jnp.bfloat16
        )

    for here in hidden_tiles(width, 512):
        row_grad_ref[0, :, here] = (
            last_dims(gate_grad_ref[0], weight_gate_ref[0, here, :])
            + last_dims(up_grad_ref[0], weight_up_ref[0, here, :])
        ).astype(jnp.bfloat16)

    lane = lax.broadcasted_iota(jnp.int32, (count, HEAD_DIM), 1)
    own = first_ref[0] + pl.program_id(0)
    row_grad_ref[0, :, width:] = jnp.where(lane == own, score, 0.0).astype(jnp.bfloat16)


def expert_backward(first_expert, grads, gates, act, by_gate, by_up, weight_gate, weight_up, weight_down):
    experts, count, width = grads.shape
    hidden = act.shape[2]
    low = one_expert(count, hidden)
    return pl.pallas_call(
        expert_backward_kernel,
        grid=(experts,),
        out_shape=(
            jax.ShapeDtypeStruct((experts, count, hidden), jnp.bfloat16),
            jax.ShapeDtypeStruct((experts, count, hidden), jnp.bfloat16),
            jax.ShapeDtypeStruct((experts, count, width + HEAD_DIM), jnp.bfloat16),
        ),
        in_specs=in_smem(1)
        + [
            one_expert(count, width),
            one_expert(count, 1),
            low,
            low,
            low,
            one_expert(width, hidden),
            one_expert(width, hidden),
            one_expert(hidden, width),
        ],
        out_specs=(low, low, one_expert(count, width + HEAD_DIM)),
        **kernel_options(),
    )(first_expert.reshape(1), grads, gates, act, by_gate, by_up, weight_gate, weight_up, weight_down)


def result_kernel(act_ref, gate_ref, weight_ref, out_ref):
    for here in hidden_tiles(out_ref.shape[2], 512):
        result = plain_dot(act_ref[0], weight_ref[0, :, here]).astype(jnp.bfloat16)
        out_ref[0, :, here] = (result.astype(jnp.float32) * gate_ref[0]).astype(jnp.bfloat16)


def expert_results(act, gates, weight_down):
    experts, count, hidden = act.shape
    width = weight_down.shape[2]

    def one(*shape):
        return pl.BlockSpec((1,) + shape, lambda expert: (expert, 0, 0))

    return pl.pallas_call(
        result_kernel,
        grid=(experts,),
        out_shape=jax.ShapeDtypeStruct((experts, count, width), jnp.bfloat16),
        in_specs=[one(count, hidden), one(count, 1), one(hidden, width)],
        out_specs=one(count, width),
        **kernel_options(),
    )(act, gates, weight_down)


def combine_kernel(turned, chosen_ref, values_ref, left_ref, right_ref, out_ref):
    width = right_ref.shape[0] if turned else right_ref.shape[1]
    experts = values_ref.shape[0]
    length = chosen_ref.shape[1]
    capacity = chosen_ref.shape[2] // experts
    blocks = chosen_ref.shape[0]

    def slots(block, here):
        values = [
            values_ref[expert, block * capacity : (block + 1) * capacity, here]
            for expert in range(experts)
        ]
        return plain_dot(chosen_ref[block], jnp.concatenate(values, axis=0))

    for here in hidden_tiles(width, 512):
        shared = (
            last_dims(left_ref[...], right_ref[here, :])
            if turned
            else plain_dot(left_ref[...], right_ref[:, here])
        )
        for block in range(blocks):
            rows = slice(block * length, (block + 1) * length)
            out_ref[rows, here] = (shared[rows] + slots(block, here)).astype(jnp.bfloat16)

    if out_ref.shape[1] > width:
        for block in range(blocks):
            out_ref[block * length : (block + 1) * length, width:] = slots(
                block, slice(width, out_ref.shape[1])
            ).astype(jnp.bfloat16)


def combine(chosen, values, left, right, turned):
    blocks, length, slots = chosen.shape
    experts, _, wide = values.shape
    capacity = slots // experts
    some = math.gcd(blocks, 2)
    return pl.pallas_call(
        functools.partial(combine_kernel, turned),
        grid=(blocks // some,),
        out_shape=jax.ShapeDtypeStruct((blocks * length, wide), jnp.bfloat16),
        in_specs=[
            pl.BlockSpec((some, length, slots), lambda i: (i, 0, 0)),
            pl.BlockSpec((experts, some * capacity, wide), lambda i: (0, i, 0)),
            pl.BlockSpec((some * length, left.shape[1]), lambda i: (i, 0)),
            pl.BlockSpec(right.shape, lambda i: (0, 0)),
        ],
        out_specs=pl.BlockSpec((some * length, wide), lambda i: (i, 0)),
        **kernel_options(32),
    )(chosen, values, left, right)


def shared_kernel(normed_ref, grad_ref, weight_ref, down_ref, act_ref, both_ref):
    hidden = act_ref.shape[1]
    pre_gate = plain_dot(normed_ref[...], weight_ref[:, :hidden])
    pre_up = plain_dot(normed_ref[...], weight_ref[:, hidden:])
    act_grad = last_dims(grad_ref[...], down_ref[...])
    act, by_gate, by_up = slopes(pre_gate, pre_up)
    act_ref[...] = act.astype(jnp.bfloat16)
    both_ref[:, :hidden] = (act_grad * by_gate).astype(jnp.bfloat16)
    both_ref[:, hidden:] = (act_grad * by_up).astype(jnp.bfloat16)


def shared_pass(normed, grads, weight, down):
    rows, width = normed.shape
    hidden = down.shape[0]
    some = math.gcd(rows, 256)

    def part(columns):
        return pl.BlockSpec((some, columns), lambda i: (i, 0))

    return pl.pallas_call(
        shared_kernel,
        grid=(rows // some,),
        out_shape=(
            jax.ShapeDtypeStruct((rows, hidden), jnp.bfloat16),
            jax.ShapeDtypeStruct((rows, 2 * hidden), jnp.bfloat16),
        ),
        in_specs=[
            part(width),
            part(width),
            pl.BlockSpec(weight.shape, lambda i: (0, 0)),
            pl.BlockSpec(down.shape, lambda i: (0, 0)),
        ],
        out_specs=(part(hidden), part(2 * hidden)),
        **kernel_options(32),
    )(normed, grads, weight, down)


def part_kernel(scaled, added, core_ref, left_ref, right_ref, *refs):
    right = right_ref[0]
    if scaled:
        right = (right.astype(jnp.float32) * refs[0][0]).astype(jnp.bfloat16)
    total = first_dims(left_ref[0], right)
    if added:
        total = total + refs[-2][0, 0].astype(jnp.float32)
    refs[-1][0, 0] = total.astype(jnp.bfloat16)


def weight_parts(core, left, right, cut_left, gates=None, received=None, slices=1, number=0, wide=False):
    chips = lax.axis_size("far")
    parts = 2 * chips * slices
    experts, count, left_width = left.shape
    right_width = right.shape[2]
    left_width, right_width = (
        (left_width // parts, right_width) if cut_left else (left_width, right_width // parts)
    )

    def spec(columns, cut):
        if cut:
            return pl.BlockSpec(
                (1, count, columns), lambda f, e, c: (e, 0, (2 * f + c[0]) * slices + number)
            )
        return pl.BlockSpec((1, count, columns), lambda f, e, c: (e, 0, 0))

    whole = pl.BlockSpec((1, 1, left_width, right_width), lambda f, e, c: (f, e, 0, 0))
    operands = [left, right]
    specs = [spec(left_width, cut_left), spec(right_width, not cut_left)]
    if gates is not None:
        operands.append(gates)
        specs.append(pl.BlockSpec((1, count, 1), lambda f, e, c: (e, 0, 0)))
    if received is not None:
        operands.append(received)
        place = (lambda f, e, c: (f, e, number, 0)) if cut_left else (lambda f, e, c: (f, e, 0, number))
        specs.append(pl.BlockSpec((1, 1, left_width, right_width), place))
    return pl.pallas_call(
        functools.partial(part_kernel, gates is not None, received is not None),
        grid_spec=pltpu.PrefetchScalarGridSpec(
            num_scalar_prefetch=1, grid=(chips, experts), in_specs=specs, out_specs=whole
        ),
        out_shape=jax.ShapeDtypeStruct((chips, experts, left_width, right_width), jnp.bfloat16),
        **kernel_options(60 if wide else 24),
    )(core.reshape(1), *operands)


def output_weight_kernel(piece_count, index_ref, core_ref, grad_ref, *refs):
    pieces = refs[:piece_count]
    keep_ref, send_ref = refs[piece_count:]
    wide = pieces[0].shape[1]
    half = piece_count // 2
    length = keep_ref.shape[1]
    some = min(wide, length)

    def part(piece, start):
        return first_dims(piece[...], grad_ref[start : start + piece.shape[0], :])

    def place(total, first):
        target = lax.div(first, length)
        chip = lax.div(target, 2)
        offset = pl.multiple_of(lax.rem(first, length), some)
        mine = lax.rem(target, 2) == core_ref[0]

        @pl.when(mine)
        def _():
            keep_ref[chip, pl.ds(offset, some), :] = total

        @pl.when(jnp.logical_not(mine))
        def _():
            send_ref[chip, pl.ds(offset, some), :] = total

    for block in range(index_ref.shape[0]):
        if block < half:
            total = part(pieces[block], 0)
        elif block == half:
            total = part(pieces[half], 0) + part(pieces[half + 1], pieces[half].shape[0])
        else:
            total = part(pieces[block + 1], 0)
        total = total.astype(jnp.bfloat16)
        for start in range(0, wide, some):
            place(total[start : start + some], index_ref[block] * wide + start)


def output_weight(index, core, grads, pieces):
    chips = lax.axis_size("far")
    length = index.shape[0] * pieces[0].shape[1] // (2 * chips)
    return pl.pallas_call(
        functools.partial(output_weight_kernel, len(pieces)),
        out_shape=(jax.ShapeDtypeStruct((chips, length, grads.shape[1]), jnp.bfloat16),) * 2,
        in_specs=in_smem(2) + in_vmem(len(pieces) + 1),
        out_specs=tuple(in_vmem(2)),
        **kernel_options(),
    )(index, core.reshape(1), grads, *pieces)


def hidden_send_kernel(own, chips, gate_ref, up_ref, out_ref):
    spread = out_ref.shape[0]
    wide = out_ref.shape[2] // 2
    piece = own // chips
    blank = [jnp.zeros((gate_ref.shape[0], wide - own), jnp.float32)] if wide > own else []
    for start, weight_ref in ((0, gate_ref), (wide, up_ref)):
        weight = weight_ref[...].astype(jnp.float32)
        for device in range(spread):
            columns = [
                weight[:, (chip * spread + device) * piece : (chip * spread + device + 1) * piece]
                for chip in range(chips)
            ]
            out_ref[device, :, start : start + wide] = jnp.concatenate(
                columns + blank, axis=1
            ).astype(jnp.bfloat16)


def hidden_send(gate, up, own, wide, chips, spread):
    return pl.pallas_call(
        functools.partial(hidden_send_kernel, own, chips),
        out_shape=jax.ShapeDtypeStruct((spread, gate.shape[0], 2 * wide), jnp.bfloat16),
        in_specs=in_vmem(2),
        out_specs=pl.BlockSpec(memory_space=pltpu.VMEM),
        **kernel_options(),
    )(gate, up)


def hidden_home_kernel(own, chips, back_ref, gate_ref, up_ref):
    spread = back_ref.shape[0]
    wide = back_ref.shape[2] // 2
    piece = own // chips
    for start, out_ref in ((0, gate_ref), (wide, up_ref)):
        values = [
            back_ref[device, :, start : start + wide].astype(jnp.float32)
            for device in range(spread)
        ]
        out_ref[...] = jnp.concatenate(
            [
                values[device][:, chip * piece : (chip + 1) * piece]
                for chip in range(chips)
                for device in range(spread)
            ],
            axis=1,
        )


def hidden_home(back, own, chips):
    spread, rows, _ = back.shape
    return pl.pallas_call(
        functools.partial(hidden_home_kernel, own, chips),
        out_shape=(jax.ShapeDtypeStruct((rows, own * spread), jnp.float32),) * 2,
        in_specs=in_vmem(1),
        out_specs=tuple(in_vmem(2)),
        **kernel_options(12),
    )(back)


def dense_home_kernel(back_ref, weight_ref, gain_ref, qkv_ref, out_ref, small_ref, gain_grad_ref):
    spread, _, wide = back_ref.shape
    own = QUERY_HEADS * HEAD_DIM // spread
    repeat = spread // KEY_VALUE_HEADS
    out_wide = out_ref.shape[1] // spread
    score = jnp.zeros(gain_ref.shape, jnp.float32)

    def keep(score, start, values):
        columns = slice(start, start + values.shape[1])
        qkv_ref[:, columns] = values * gain_ref[...]
        weight = weight_ref[:, columns].astype(jnp.float32)
        return score + jnp.sum(weight * values, axis=1, keepdims=True)

    small = jnp.zeros(small_ref.shape, jnp.float32)
    for device in range(spread):
        score = keep(score, device * own, back_ref[device, :, :own].astype(jnp.float32))
        start = own + 2 * HEAD_DIM
        out_ref[:, device * out_wide : (device + 1) * out_wide] = back_ref[
            device, :, start : start + out_wide
        ].astype(jnp.float32)
        small = small + back_ref[device, :, start + out_wide :].astype(jnp.float32)
    for part in range(2):
        for head in range(KEY_VALUE_HEADS):
            start = own + part * HEAD_DIM
            values = sum(
                back_ref[head * repeat + i, :, start : start + HEAD_DIM].astype(jnp.float32)
                for i in range(repeat)
            )
            place = QUERY_HEADS * HEAD_DIM + (part * KEY_VALUE_HEADS + head) * HEAD_DIM
            score = keep(score, place, values)
    small_ref[...] = small
    gain_grad_ref[...] = score


def dense_home(back, weight, gain, width):
    rows, qkv_width = weight.shape
    return pl.pallas_call(
        dense_home_kernel,
        out_shape=(
            jax.ShapeDtypeStruct((rows, qkv_width), jnp.float32),
            jax.ShapeDtypeStruct((rows, width), jnp.float32),
            jax.ShapeDtypeStruct((rows, HEAD_DIM), jnp.float32),
            jax.ShapeDtypeStruct((rows, 1), jnp.float32),
        ),
        in_specs=in_vmem(3),
        out_specs=tuple(in_vmem(4)),
        **kernel_options(12),
    )(back, weight, gain)


def product_kernel(left_ref, right_ref, out_ref):
    for here in hidden_tiles(out_ref.shape[0], 512):
        out_ref[here, :] = first_dims(left_ref[:, here], right_ref[...]).astype(jnp.bfloat16)


def row_product(left, right, columns):
    return pl.pallas_call(
        product_kernel,
        out_shape=jax.ShapeDtypeStruct((columns, right.shape[1]), jnp.bfloat16),
        in_specs=in_vmem(2),
        out_specs=pl.BlockSpec(memory_space=pltpu.VMEM),
        **kernel_options(24),
    )(left, right)


def widen_kernel(*refs):
    out_ref = refs[-1]
    start = 0
    for part_ref in refs[:-1]:
        rows = part_ref.shape[1]
        out_ref[0, start : start + rows, :] = part_ref[0].astype(jnp.float32)
        start += rows


def widen(*parts):
    experts, _, columns = parts[0].shape
    rows = sum(part.shape[1] for part in parts)
    return pl.pallas_call(
        widen_kernel,
        grid=(experts,),
        out_shape=jax.ShapeDtypeStruct((experts, rows, columns), jnp.float32),
        in_specs=[one_expert(part.shape[1], columns) for part in parts],
        out_specs=one_expert(rows, columns),
        **kernel_options(28),
    )(*parts)


def project_back_kernel(
    query_ref, own_ref, last_ref, cosine_ref, sine_ref, weight_ref, projected_ref, out_ref
):
    wide = query_ref.shape[1]
    projected_ref[:, :wide] = query_ref[...]
    total = own_ref[...] + last_ref[...].astype(jnp.float32)
    keys = total[:, :HEAD_DIM]
    turned = keys * cosine_ref[...] - pltpu.roll(keys, HEAD_DIM // 2, 1) * sine_ref[...]
    projected_ref[:, wide : wide + HEAD_DIM] = turned.astype(jnp.bfloat16)
    projected_ref[:, wide + HEAD_DIM :] = total[:, HEAD_DIM:].astype(jnp.bfloat16)
    for here in hidden_tiles(out_ref.shape[1], 512):
        out_ref[:, here] = last_dims(projected_ref[...], weight_ref[here, :]).astype(jnp.bfloat16)


def project_back(queries, own, last, cosine, sine, weight):
    rows = queries.shape[0]
    return pl.pallas_call(
        project_back_kernel,
        out_shape=(
            jax.ShapeDtypeStruct((rows, weight.shape[1]), jnp.bfloat16),
            jax.ShapeDtypeStruct((rows, weight.shape[0]), jnp.bfloat16),
        ),
        in_specs=in_vmem(6),
        out_specs=tuple(in_vmem(2)),
        **kernel_options(24),
    )(queries, own, last, cosine, sine, weight)


def finish_kernel(first_ref, second_ref, own_ref, tokens_ref, grad_ref, out_ref):
    weighted = (
        first_ref[...].astype(jnp.float32)
        + second_ref[...].astype(jnp.float32)
        + own_ref[...].astype(jnp.float32)
    )
    inputs = tokens_ref[...].astype(jnp.float32)
    scale = lax.rsqrt(jnp.mean(inputs * inputs, axis=-1, keepdims=True) + EPSILON)
    inner_mean = jnp.mean(weighted * inputs, axis=-1, keepdims=True)
    out_ref[...] = grad_ref[...] + scale * weighted - inputs * (scale * scale * scale * inner_mean)


def finish(first, second, own, tokens, grads):
    block = pl.BlockSpec(grads.shape, lambda i: (0, 0))
    return pl.pallas_call(
        finish_kernel,
        grid=(1,),
        out_shape=jax.ShapeDtypeStruct(grads.shape, jnp.float32),
        in_specs=[block] * 5,
        out_specs=block,
        **kernel_options(16),
    )(first, second, own, tokens, grads)


def body(
    tokens,
    attn_gain,
    query_key_value_weight,
    out_weight,
    ffn_gain,
    router_weight,
    shared_gate,
    shared_up,
    shared_down,
    routed_gate_weight,
    routed_up_weight,
    routed_down_weight,
    routes,
    cotangent,
):
    f32 = jnp.float32
    bf16 = jnp.bfloat16
    both = CONTEXT + ("experts",)
    context_count = context_size()
    spread = lax.axis_size("experts")
    context_index = lax.axis_index(CONTEXT)
    expert_index = lax.axis_index("experts")
    token_count, width = tokens.shape
    local_experts = routed_gate_weight.shape[0]
    experts_all = local_experts * spread
    rows = token_count * spread
    weight_rows = query_key_value_weight.shape[0]
    query_width = QUERY_HEADS * HEAD_DIM
    key_width = KEY_VALUE_HEADS * HEAD_DIM
    repeat_times = spread // KEY_VALUE_HEADS
    head_share = QUERY_HEADS // spread
    own_width = head_share * HEAD_DIM
    block_width = width // context_count

    def key_columns(weight):
        heads = weight.reshape(weight_rows, KEY_VALUE_HEADS, HEAD_DIM)
        return jnp.repeat(heads, repeat_times, axis=1)

    own_gain = attn_gain.astype(f32)[:, None]
    qkv_scaled = (query_key_value_weight.astype(f32) * own_gain).astype(bf16)
    qkv_send = jnp.concatenate(
        [
            qkv_scaled[:, :query_width].reshape(weight_rows, spread, own_width),
            key_columns(qkv_scaled[:, query_width : query_width + key_width]),
            key_columns(qkv_scaled[:, query_width + key_width :]),
        ],
        axis=2,
    ).transpose(1, 0, 2)
    hidden_piece = shared_down.shape[0]
    hidden_own = hidden_piece * context_count
    hidden_wide = -(-hidden_own // HEAD_DIM) * HEAD_DIM

    shared_send = hidden_send(
        shared_gate, shared_up, hidden_own, hidden_wide, context_count, spread
    )

    token_ring = RingGather(tokens)
    token_ring.step()
    position = context_index * rows + jnp.arange(rows, dtype=jnp.int32)
    position = ring_order(position.reshape(spread, token_count)).reshape(rows).astype(f32)
    half_width = HEAD_DIM // 2
    frequency = THETA ** (-jnp.arange(half_width, dtype=f32) * 2.0 / HEAD_DIM)
    angles = position[:, None] * frequency[None, :]
    cosine = jnp.cos(angles)
    sine = jnp.sin(angles)
    cosine = jnp.concatenate([cosine, cosine], axis=1)
    sine = jnp.concatenate([-sine, sine], axis=1)
    small = jnp.concatenate([ffn_gain[None], router_weight.T], axis=0)
    small = flip_double(small[None], CONTEXT)
    qkv_send = after(small, qkv_send)
    qkv_rows = to_experts(qkv_send).reshape(spread * weight_rows, -1)
    while small.shape[0] < context_count:
        small = flip_double(small, CONTEXT)
    small = jnp.concatenate([small.reshape(1, -1), routes.astype(bf16).reshape(1, -1)], axis=1)
    small, cosine, sine = meet([token_ring], small, cosine, sine)
    token_ring.step()
    (qkv_rows,) = meet([token_ring], qkv_rows)
    token_ring.step()
    qkv_far = far_gather(qkv_rows)
    qkv_far, out_weight = meet([token_ring], qkv_far, out_weight)
    token_ring.step()
    qkv_own = core_gather(qkv_far)
    (qkv_own,) = meet([token_ring], qkv_own)
    small = after(token_ring.latest(), small)

    out_full = lax.all_gather(out_weight, both, axis=0, tiled=True)
    normed_one, query_rows, key_value = project(
        token_ring.pieces(), qkv_own, cosine, sine, own_width
    )
    key_value = far_gather(key_value)
    small = flip_double(small, "experts")
    key_value, small = lax.optimization_barrier((key_value, small))
    key_value = core_gather(key_value)
    small = flip_double(small, "experts")
    place = ring_place(expert_index, spread)
    order = (ring_place(jnp.arange(spread, dtype=jnp.int32), spread) - place + spread) % spread
    attended, attended_low, log_total = attention_forward(
        context_index, order, query_rows, key_value
    )
    attended_low, small = lax.optimization_barrier((attended_low, small))
    attended_tok = (
        to_experts(attended_low.reshape(spread, token_count, own_width))
        .transpose(1, 0, 2)
        .reshape(token_count, query_width)
    )
    while small.shape[0] < spread:
        small = flip_double(small, "experts")
    attended_tok, small = lax.optimization_barrier((attended_tok, small))
    routes_block = small[:, -token_count * TOP :].reshape(spread, token_count, TOP)
    routes_block = routes_block.astype(jnp.int32).transpose(0, 2, 1)
    small = small[:, : -token_count * TOP].reshape(spread, context_count, -1, weight_rows)
    small = small.transpose(2, 1, 0, 3).reshape(-1, width)
    gain_two = small[0].astype(f32)
    router_full = small[1:]

    inputs = tokens.astype(f32)
    middle = inputs + jnp.dot(attended_tok, out_full, preferred_element_type=f32)
    scale_two = rms_scale(middle)
    normed_two = (middle * scale_two * gain_two).astype(bf16)
    normed_ring = RingGather(normed_two)
    normed_ring.step()
    routes_block, router_full, shared_down = meet(
        [normed_ring], routes_block, router_full, shared_down
    )

    normed_ring.step()
    down_far = far_gather(shared_down)
    first_expert = expert_index * local_experts
    own_ids = first_expert + jnp.arange(local_experts, dtype=jnp.int32)
    routes_block = ring_order(routes_block)
    member = jnp.any(routes_block[:, None] == own_ids[None, :, None, None], axis=2)
    counted = member.astype(jnp.int32)
    slot_index = jnp.cumsum(counted, axis=2) - counted
    capacity = token_count * TOP * 4 // (3 * experts_all)
    slot = jnp.arange(capacity, dtype=jnp.int32)
    chosen = member[:, :, None, :] & (slot_index[:, :, None, :] == slot[None, None, :, None])
    chosen_wide = chosen.astype(f32)
    slots = local_experts * capacity
    chosen_low = chosen.astype(bf16).reshape(spread, slots, token_count)
    chosen_back = chosen_low.transpose(0, 2, 1)
    down_far, chosen_low, chosen_wide, chosen_back = meet(
        [normed_ring], down_far, chosen_low, chosen_wide, chosen_back
    )
    normed_ring.step()
    down_own = jnp.pad(core_gather(down_far), ((0, hidden_wide - hidden_own), (0, 0)))
    (down_own,) = meet([normed_ring], down_own)
    normed_ring.step()
    (cotangent_late,) = meet([normed_ring], cotangent)
    grad_ring = RingGather(cotangent_late)
    grad_ring.step()
    normed_block, expert_rows = dispatch(normed_ring.pieces(), chosen_low, local_experts)

    (normed_block,) = meet([grad_ring], normed_block)
    grad_ring.step()
    router_probs = jax.nn.softmax(dot_last(normed_block, router_full), axis=-1)
    gate_tokens = (
        lax.dynamic_slice_in_dim(router_probs, first_expert, local_experts, 1)
        .reshape(spread, token_count, local_experts)
        .transpose(0, 2, 1)
    )
    gates = jnp.sum(chosen_wide * gate_tokens[:, :, None, :], axis=3)
    gates = gates.transpose(1, 0, 2).reshape(local_experts, spread * capacity, 1)
    expert_rows = after(gates, expert_rows)
    act, by_gate, by_up = expert_forward(expert_rows, routed_gate_weight, routed_up_weight)
    act, gates = meet([grad_ring], act, gates)
    grad_ring.step()
    weighted_y = expert_results(act, gates, routed_down_weight)
    (weighted_y,) = meet([grad_ring], weighted_y)
    grad_ring.step()
    chosen_low, shared_send = meet([grad_ring], chosen_low, shared_send)
    grad_block, grad_rows = dispatch(grad_ring.pieces(), chosen_low, local_experts)

    own_core = lax.axis_index("core")
    other_core = 1 - own_core
    shared_rows = to_experts(shared_send).reshape(spread * weight_rows, -1)
    down_parts = weight_parts(other_core, act, grad_rows, False, gates, wide=True)
    down_parts, shared_rows, attended_late = lax.optimization_barrier(
        (down_parts, shared_rows, attended_low)
    )
    shared_far = far_gather(shared_rows)
    down_received = core_swap(down_parts)
    heads_ring = RingGather(attended_late)
    heads_ring.step()
    grad_rows, gates = after(down_parts, grad_rows, gates)
    expert_dg, expert_du, row_grad = expert_backward(
        first_expert,
        grad_rows,
        gates,
        act,
        by_gate,
        by_up,
        routed_gate_weight,
        routed_up_weight,
        routed_down_weight,
    )
    row_grad, shared_far, down_received = meet(
        [heads_ring], row_grad, shared_far, down_received
    )
    heads_ring.step()
    shared_own = core_gather(shared_far)
    shared_act, shared_both = shared_pass(normed_block, grad_block, shared_own, down_own)
    shared_act, shared_both = meet([heads_ring], shared_act, shared_both)
    heads_ring.step()
    grad_part = combine(chosen_back, row_grad, shared_both, shared_own, True)
    grad_scatter = RingScatter(grad_part)
    grad_scatter.step()
    expert_dg, expert_du, weighted_y, act = after(
        grad_part, expert_dg, expert_du, weighted_y, act
    )
    down_parts = weight_parts(own_core, act, grad_rows, False, gates, down_received)
    (down_parts,) = meet([grad_scatter, heads_ring], down_parts)
    down_sum = chips_sum(down_parts)
    grad_scatter.step()
    heads_ring.step()
    expert_dg = after(down_parts, expert_dg)
    gate_parts = weight_parts(other_core, expert_rows, expert_dg, True)
    shared_parts = weight_parts(
        other_core, after(gate_parts, normed_block)[None], shared_both[None], True
    )
    gate_parts, shared_parts = meet([grad_scatter, heads_ring], gate_parts, shared_parts)
    grad_scatter.step()
    gate_received = core_swap(gate_parts)
    shared_received = core_swap(shared_parts)
    weighted_y = after(shared_parts, weighted_y)
    out_part = combine(chosen_back, weighted_y, shared_act, down_own, False)
    out_part, gate_received = lax.optimization_barrier((out_part, gate_received))
    gate_parts = weight_parts(own_core, expert_rows, expert_dg, True, None, gate_received)
    gate_parts, shared_received, out_part = meet(
        [grad_scatter], gate_parts, shared_received, out_part
    )
    grad_scatter.step()
    expert_du = after(gate_parts, expert_du)
    up_parts = weight_parts(other_core, expert_rows, expert_du, True)
    shared_parts = weight_parts(
        own_core,
        after(up_parts, normed_block)[None],
        shared_both[None],
        True,
        None,
        shared_received,
    )
    up_parts, shared_parts, out_part = meet([grad_scatter], up_parts, shared_parts, out_part)
    gathered = grad_scatter.total()
    out_scatter = RingScatter(out_part)
    out_scatter.step()
    shared_pair = chips_exchange(shared_parts)

    prob_grad = gathered[:, width : width + experts_all]
    probs_tok = router_probs[:token_count]
    logit_grad = (
        probs_tok * (prob_grad - jnp.sum(probs_tok * prob_grad, axis=-1, keepdims=True))
    ).astype(bf16)
    normed_grad = gathered[:, :width] + jnp.dot(
        logit_grad, router_full, preferred_element_type=f32
    )
    grad_final = cotangent.astype(f32)
    weighted = normed_grad * gain_two
    inner_mean = jnp.mean(weighted * middle, axis=-1, keepdims=True)
    middle_grad = (
        grad_final
        + scale_two * weighted
        - middle * scale_two * scale_two * scale_two * inner_mean
    )
    gain_rows = (normed_grad * middle * scale_two).astype(bf16)
    branch_grad = middle_grad.astype(bf16)
    attended_grad = dot_last(branch_grad, out_full).astype(bf16)
    (attended_grad,) = meet([out_scatter], attended_grad)
    grad_heads = to_experts(
        attended_grad.reshape(token_count, spread, own_width).transpose(1, 0, 2)
    ).reshape(rows, own_width)
    lane = jnp.arange(HEAD_DIM, dtype=jnp.int32)[None, :]
    gain_column = jnp.broadcast_to(lane == experts_all, (token_count, HEAD_DIM)).astype(bf16)
    small_left = jnp.concatenate([normed_two, gain_rows], axis=0)
    small_right = jnp.concatenate(
        [jnp.pad(logit_grad, ((0, 0), (0, HEAD_DIM - experts_all))), gain_column], axis=0
    )
    small_left, small_right, expert_du = after(attended_grad, small_left, small_right, expert_du)
    up_received = core_swap(up_parts)
    slices = 2 if block_width % (2 * HEAD_DIM) == 0 else 1
    up_parts = [
        weight_parts(own_core, expert_rows, expert_du, True, None, up_received, slices, number)
        for number in range(slices)
    ]
    small_parts = weight_parts(other_core, small_left[None], small_right[None], True)
    branch_late, up_parts = after(small_parts, branch_grad, up_parts)
    branch_columns = to_experts(
        branch_late.reshape(token_count, spread, own_width).transpose(1, 0, 2)
    ).reshape(rows, own_width)
    grad_heads, small_parts, up_parts = lax.optimization_barrier((grad_heads, small_parts, up_parts))

    out_scatter.step()
    small_received = core_swap(small_parts)
    query_grad, key_value_all = attention_backward(
        context_index,
        order,
        query_rows,
        key_value,
        attended,
        grad_heads,
        log_total,
        cosine,
        sine,
    )
    key_value_all, branch_columns, small_received, down_sum, shared_last = meet(
        [out_scatter], key_value_all, branch_columns, small_received, down_sum, shared_pair[1]
    )
    gate_sum = chips_sum(gate_parts)
    key_value_all = key_value_all.reshape(context_count, rows, -1)
    key_value_received = core_exchange(block_parts(key_value_all))
    key_value_sums = block_sums(key_value_all, key_value_received)
    (key_value_sums,) = lax.optimization_barrier((key_value_sums,))
    key_value_own, key_value_last = far_exchange(key_value_sums)
    out_scatter.first = after(key_value_sums, out_scatter.first)
    out_scatter.step()
    branch_columns, shared_last, small_left = after(
        key_value_sums, branch_columns, shared_last, small_left
    )
    index = ring_index(place + jnp.arange(spread, dtype=jnp.int32), spread)
    out_keep, out_send = output_weight(index, own_core, branch_columns, heads_ring.pieces())
    small_parts = weight_parts(
        own_core, small_left[None], small_right[None], True, None, small_received
    )
    shared_own_part = both_halves((shared_pair[0].astype(f32), shared_last)).astype(bf16)
    shared_back = to_experts(shared_own_part.reshape(spread, weight_rows, -1))
    key_value_last, out_keep, out_send, small_parts, gate_sum, shared_act = meet(
        [out_scatter], key_value_last, out_keep, out_send, small_parts, gate_sum, shared_act
    )
    up_first = chips_sum(up_parts[0])
    projected_grad, input_part = project_back(
        query_grad, key_value_own, key_value_last, cosine, sine, qkv_own
    )
    input_scatter = RingScatter(input_part)
    input_scatter.step()
    out_received = core_swap(out_send)
    normed_one = after(input_scatter.sent, normed_one)
    qkv_parts = weight_parts(other_core, normed_one[None], projected_grad[None], True)
    qkv_received = core_swap(qkv_parts)
    qkv_parts = weight_parts(
        own_core, normed_one[None], projected_grad[None], True, None, qkv_received
    )
    qkv_parts, out_received, shared_back = meet(
        [input_scatter, out_scatter], qkv_parts, out_received, shared_back
    )
    input_scatter.step()
    qkv_parts, out_received, shared_back, out_scatter.first = after(
        input_scatter.sent, qkv_parts, out_received, shared_back, out_scatter.first
    )
    out_scatter.step()
    out_sums = out_keep.astype(f32) + out_received.astype(f32)
    dense_parts = jnp.concatenate(
        [qkv_parts[:, 0], out_sums.astype(bf16), small_parts[:, 0]], axis=2
    )
    dense_pair = chips_exchange(dense_parts)
    down_sum, shared_act, shared_back = after(dense_parts, down_sum, shared_act, shared_back)
    shared_gate_grad, shared_up_grad = hidden_home(shared_back, hidden_own, context_count)
    expert_down_grad = widen(after(shared_gate_grad, down_sum))
    shared_down_sum = row_product(shared_act, after(expert_down_grad, grad_block), hidden_own)
    shared_down_sum = shared_down_sum.reshape(context_count, hidden_piece, width)
    shared_down_sum, shared_gate_grad = meet(
        [input_scatter, out_scatter], shared_down_sum, shared_gate_grad
    )
    input_scatter.step()
    gate_sum, shared_down_sum = after(input_scatter.sent, gate_sum, shared_down_sum)
    shared_down_received = core_exchange(block_parts(shared_down_sum))
    expert_gate_grad = widen(gate_sum)
    expert_gate_grad, dense_last, shared_down_received = meet(
        [input_scatter], expert_gate_grad, dense_pair[1], shared_down_received
    )
    input_scatter.step()
    up_later = [chips_sum(after((dense_last, up_first), part)) for part in up_parts[1:]]
    dense_last, out_scatter.first, shared_down_received = after(
        input_scatter.sent, dense_last, out_scatter.first, shared_down_received
    )
    dense_sum = both_halves((dense_pair[0].astype(f32), dense_last)).astype(bf16)
    dense_back = to_experts(dense_sum.reshape(spread, weight_rows, -1))
    shared_down_pair = far_exchange(block_sums(shared_down_sum, shared_down_received))
    dense_back, shared_down_pair = meet([input_scatter], dense_back, shared_down_pair)
    shared_down_grad = both_halves(shared_down_pair)
    layer_out = (middle + out_scatter.total()).astype(bf16)
    expert_up_grad = widen(up_first, *up_later)
    qkv_weight_grad, out_weight_grad, small_grad, attn_gain_grad = dense_home(
        dense_back, query_key_value_weight, own_gain, width
    )
    attn_gain_grad = attn_gain_grad[:, 0]
    router_weight_grad = small_grad[:, :experts_all]
    ffn_gain_grad = small_grad[:, experts_all]
    tokens_grad = finish(
        input_scatter.first, input_scatter.second, input_part, tokens, middle_grad
    )
    return (
        layer_out,
        tokens_grad,
        attn_gain_grad,
        qkv_weight_grad,
        out_weight_grad,
        ffn_gain_grad,
        router_weight_grad,
        shared_gate_grad,
        shared_up_grad,
        shared_down_grad,
        expert_gate_grad,
        expert_up_grad,
        expert_down_grad,
    )


def solution(mesh):
    context_count, spread = mesh.devices.shape
    split = jax.sharding.Mesh(
        mesh.devices.reshape(context_count // 2, 2, spread), ("far", "core", "experts")
    )
    return jax.shard_map(
        body,
        mesh=split,
        in_specs=(
            P(("far", "core", "experts"), None),
            P(("far", "core", "experts")),
            P(("far", "core", "experts"), None),
            P(("far", "core", "experts"), None),
            P(("far", "core", "experts")),
            P(("far", "core", "experts"), None),
            P(("far", "core", "experts"), None),
            P(("far", "core", "experts"), None),
            P(("far", "core", "experts"), None),
            P("experts", None, None),
            P("experts", None, None),
            P("experts", None, None),
            P(("far", "core", "experts"), None),
            P(("far", "core", "experts"), None),
        ),
        out_specs=(
            P(("far", "core", "experts"), None),
            P(("far", "core", "experts"), None),
            P(("far", "core", "experts")),
            P(("far", "core", "experts"), None),
            P(("far", "core", "experts"), None),
            P(("far", "core", "experts")),
            P(("far", "core", "experts"), None),
            P(("far", "core", "experts"), None),
            P(("far", "core", "experts"), None),
            P(("far", "core", "experts"), None),
            P("experts", CONTEXT, None),
            P("experts", CONTEXT, None),
            P("experts", None, CONTEXT),
        ),
        check_vma=False,
    )
```

```python
import functools
import math

import jax
import jax.numpy as jnp
from jax import lax
from jax.experimental import pallas as pl
from jax.experimental.pallas import tpu as pltpu
from jax.sharding import PartitionSpec as P

QUERY_HEADS = 16
KEY_VALUE_HEADS = 4
HEAD_DIM = 128
TOP = 6


EPSILON = 1e-06
THETA = 10000.0
NEG_LARGE = -1e30
CONTEXT = ("far", "core")


def rms_scale(values):
    return lax.rsqrt(jnp.mean(values * values, axis=-1, keepdims=True) + EPSILON)


def norm_back(values, row_scale, gain_values, grad_out):
    weighted = grad_out * gain_values
    gain_grad = jnp.sum(grad_out * values * row_scale, axis=0)
    inner_mean = jnp.mean(weighted * values, axis=-1, keepdims=True)
    return (
        row_scale * weighted - values * row_scale * row_scale * row_scale * inner_mean,
        gain_grad,
    )


def inner_rows(left, right):
    return lax.dot_general(
        left, right, (((0,), (0,)), ((), ())), preferred_element_type=jnp.float32
    )


def dot_last(left, right):
    return lax.dot_general(
        left, right, (((1,), (1,)), ((), ())), preferred_element_type=jnp.float32
    )


def context_size():
    return lax.axis_size("far") * lax.axis_size("core")


def ring_pairs(count):
    order = [i for i in range(count) if i % 2 == 0] + [i for i in reversed(range(count)) if i % 2 == 1]
    right = [(order[i], order[(i + 1) % count]) for i in range(count)]
    left = [(order[i], order[(i - 1) % count]) for i in range(count)]
    return right, left


def ring_place(index, count):
    return jnp.where(index % 2 == 0, index // 2, count - 1 - index // 2)


def ring_index(place, count):
    place = (place + 2 * count) % count
    return jnp.where(place < count // 2, 2 * place, 2 * (count - 1 - place) + 1)


class RingGather:
    def __init__(self, block):
        self.count = lax.axis_size("experts")
        self.right, self.left = ring_pairs(self.count)
        self.half = block.shape[0] // 2
        self.block = block
        self.ahead = [block]
        self.behind = [block]
        self.far = None

    def step(self):
        if len(self.ahead) < self.count // 2:
            self.behind.append(lax.ppermute(self.behind[-1], "experts", self.right))
            self.ahead.append(lax.ppermute(self.ahead[-1], "experts", self.left))
        else:
            self.far = [
                lax.ppermute(self.behind[-1][: self.half], "experts", self.right),
                lax.ppermute(self.ahead[-1][self.half :], "experts", self.left),
            ]

    def latest(self):
        return self.far if self.far else [self.behind[-1], self.ahead[-1]]

    def replace(self, values):
        if self.far:
            self.far = list(values)
        else:
            self.behind[-1], self.ahead[-1] = values

    def pieces(self):
        return self.ahead + self.far + self.behind[:0:-1]


class RingScatter:
    def __init__(self, whole):
        self.count = lax.axis_size("experts")
        self.right, self.left = ring_pairs(self.count)
        self.whole = whole
        self.rows = whole.shape[0] // self.count
        self.half = self.rows // 2
        self.left_steps = self.count // 2
        self.first = None
        self.second = None

    def own(self, step):
        start = step % self.count * self.rows
        return self.whole[start : start + self.rows].astype(jnp.float32)

    def arrived(self):
        first = self.first.astype(jnp.float32)
        second = self.second.astype(jnp.float32)
        if self.left_steps == self.count // 2 - 1:
            blank = jnp.zeros((self.half, self.whole.shape[1]), jnp.float32)
            first = jnp.concatenate([first, blank], axis=0)
            second = jnp.concatenate([blank, second], axis=0)
        return first, second

    def step(self):
        if self.first is None:
            far = self.own(self.left_steps)
            first, second = far[: self.half], far[self.half :]
        else:
            first, second = self.arrived()
            first = first + self.own(self.left_steps)
            second = second + self.own(-self.left_steps)
        self.sent = (first.astype(jnp.bfloat16), second.astype(jnp.bfloat16))
        self.first = lax.ppermute(self.sent[0], "experts", self.right)
        self.second = lax.ppermute(self.sent[1], "experts", self.left)
        self.left_steps -= 1

    def latest(self):
        return [self.first, self.second]

    def replace(self, values):
        self.first, self.second = values

    def total(self):
        first, second = self.arrived()
        return first + second + self.own(0)


def meet(rings, *values):
    held, values = lax.optimization_barrier(([ring.latest() for ring in rings], values))
    for ring, value in zip(rings, held):
        ring.replace(value)
    return values


def ring_order(values):
    count = lax.axis_size("experts")
    place = ring_place(lax.axis_index("experts"), count)
    return jnp.concatenate(
        [
            lax.dynamic_slice_in_dim(values, ring_index(place + step, count), 1, 0)
            for step in range(count)
        ],
        axis=0,
    )


def flip_pairs(count, bit):
    return [(i, i ^ bit) for i in range(count)]


def flip_double(whole, axis):
    bit = whole.shape[0]
    received = lax.ppermute(whole, axis, flip_pairs(lax.axis_size(axis), bit))
    return jnp.where(
        (lax.axis_index(axis) // bit) % 2 == 0,
        jnp.concatenate([whole, received], axis=0),
        jnp.concatenate([received, whole], axis=0),
    )


def flip_gather(block, axis):
    whole = block[None]
    while whole.shape[0] < lax.axis_size(axis):
        whole = flip_double(whole, axis)
    return whole


def flip_half(values, axis, bit, dimension):
    shape = values.shape
    pairs = values.reshape(shape[:dimension] + (shape[dimension] // 2, 2) + shape[dimension + 1 :])
    mine = (lax.axis_index(axis) // bit) % 2
    sent = lax.dynamic_index_in_dim(pairs, 1 - mine, dimension + 1, keepdims=False)
    kept = lax.dynamic_index_in_dim(pairs, mine, dimension + 1, keepdims=False)
    return kept + lax.ppermute(sent, axis, flip_pairs(lax.axis_size(axis), bit))


def context_double(whole, bit):
    received = lax.ppermute(whole, CONTEXT, flip_pairs(context_size(), bit))
    low = (lax.axis_index(CONTEXT) // bit) % 2 == 0
    return jnp.stack(
        [jnp.where(low, whole, received), jnp.where(low, received, whole)], axis=1
    ).reshape((2 * whole.shape[0],) + whole.shape[1:])


def far_gather(block):
    whole = block[None]
    bit = context_size() // 2
    while bit > 1:
        whole = context_double(whole, bit)
        bit //= 2
    return whole


def core_gather(whole):
    return context_double(whole, 1).reshape(-1, whole.shape[-1])


def context_gather(block):
    return core_gather(far_gather(block))


def after(done, *values):
    values, _ = lax.optimization_barrier((values, done))
    return values[0] if len(values) == 1 else values


def core_parts(piece_of):
    count = context_size()
    index = lax.axis_index(CONTEXT)
    return {place: piece_of(index ^ (place + 1)) for place in range(count - 2, -1, -2)}


def core_exchange(parts):
    pairs = flip_pairs(context_size(), 1)
    return {
        place: lax.ppermute(part.astype(jnp.bfloat16), CONTEXT, pairs)
        for place, part in parts.items()
    }


def core_sums(piece_of, received):
    index = lax.axis_index(CONTEXT)
    return {
        place // 2: piece_of(index ^ place, part) for place, part in received.items()
    }


def far_exchange(pieces):
    count = context_size()
    bit = 2
    while 2 * bit < count:
        merged = {}
        for place in sorted(pieces, reverse=True):
            if place % 2 == 0:
                received = lax.ppermute(
                    pieces[place + 1].astype(jnp.bfloat16), CONTEXT, flip_pairs(count, bit)
                )
                merged[place // 2] = pieces[place] + received.astype(jnp.float32)
        pieces = merged
        bit *= 2
    last = lax.ppermute(pieces[1].astype(jnp.bfloat16), CONTEXT, flip_pairs(count, bit))
    return pieces[0], last


def both_halves(pair):
    return pair[0] + pair[1].astype(jnp.float32)


def core_swap(values):
    return lax.ppermute(values, "core", [(0, 1), (1, 0)])


def chips_sum(values):
    return lax.psum_scatter(values, "far", scatter_dimension=0, tiled=True)[0]


def chips_exchange(values):
    chip = lax.axis_index("far")
    pieces = {
        place: lax.dynamic_index_in_dim(values, chip ^ place, 0, keepdims=False)
        for place in range(values.shape[0])
    }
    return far_exchange(pieces)


def block_sums(values, received):
    def piece_of(target, part):
        return lax.dynamic_index_in_dim(values, target, 0, keepdims=False) + part.astype(jnp.float32)

    return core_sums(piece_of, received)


def block_parts(values):
    return core_parts(lambda target: lax.dynamic_index_in_dim(values, target, 0, keepdims=False))


def to_experts(stacked):
    return lax.all_to_all(stacked, "experts", split_axis=0, concat_axis=0, tiled=True)


def kernel_options(mebibytes=60):
    return dict(
        compiler_params=pltpu.CompilerParams(vmem_limit_bytes=mebibytes * 1024 * 1024),
        cost_estimate=pl.CostEstimate(flops=1024, bytes_accessed=1024, transcendentals=0),
    )


def in_vmem(count):
    return [pl.BlockSpec(memory_space=pltpu.VMEM)] * count


def in_smem(count):
    return [pl.BlockSpec(memory_space=pltpu.SMEM)] * count


def plain_dot(left, right):
    return jnp.dot(left, right, preferred_element_type=jnp.float32)


def last_dims(left, right):
    return lax.dot_general(
        left, right, (((1,), (1,)), ((), ())), preferred_element_type=jnp.float32
    )


def first_dims(left, right):
    return lax.dot_general(
        left, right, (((0,), (0,)), ((), ())), preferred_element_type=jnp.float32
    )


def project_kernel(piece_count, *refs):
    pieces = refs[:piece_count]
    weight_ref, cosine_ref, sine_ref, normed_ref, query_ref, key_value_ref = refs[piece_count:]
    start = 0
    for piece in pieces:
        rows = piece.shape[0]
        values = piece[...].astype(jnp.float32)
        scale = lax.rsqrt(jnp.mean(values * values, axis=-1, keepdims=True) + EPSILON)
        normed_ref[start : start + rows, :] = (values * scale).astype(jnp.bfloat16)
        start += rows
    query_width = query_ref.shape[1]
    heads = plain_dot(normed_ref[...], weight_ref[...])

    def rotated(offset):
        head = heads[:, offset : offset + HEAD_DIM]
        turned = pltpu.roll(head, HEAD_DIM // 2, 1)
        return (head * cosine_ref[...] + turned * sine_ref[...]).astype(jnp.bfloat16)

    for offset in range(0, query_width, HEAD_DIM):
        query_ref[:, offset : offset + HEAD_DIM] = rotated(offset)
    key_value_ref[:, :HEAD_DIM] = rotated(query_width)
    key_value_ref[:, HEAD_DIM:] = heads[:, query_width + HEAD_DIM :].astype(jnp.bfloat16)


def project(pieces, weight, cosine, sine, query_width):
    rows = sum(piece.shape[0] for piece in pieces)
    width = pieces[0].shape[1]
    return pl.pallas_call(
        functools.partial(project_kernel, len(pieces)),
        out_shape=(
            jax.ShapeDtypeStruct((rows, width), jnp.bfloat16),
            jax.ShapeDtypeStruct((rows, query_width), jnp.bfloat16),
            jax.ShapeDtypeStruct((rows, weight.shape[1] - query_width), jnp.bfloat16),
        ),
        in_specs=in_vmem(len(pieces) + 3),
        out_specs=tuple(in_vmem(3)),
        **kernel_options(),
    )(*pieces, weight, cosine, sine)


def stack_heads(values):
    heads = values.shape[1] // HEAD_DIM
    return jnp.concatenate(
        [values[:, i * HEAD_DIM : (i + 1) * HEAD_DIM] for i in range(heads)], axis=0
    )


def spread_heads(values, heads):
    rows = values.shape[0] // heads
    return jnp.concatenate([values[i * rows : (i + 1) * rows] for i in range(heads)], axis=1)


def stack_lanes(values):
    return jnp.concatenate([values[i : i + 1] for i in range(values.shape[0])], axis=1)


def visible_keys(shape, key_start, query_start, query_tile):
    key_pos = key_start + lax.broadcasted_iota(jnp.int32, shape, 0)
    query_pos = query_start + lax.rem(lax.broadcasted_iota(jnp.int32, shape, 1), query_tile)
    return query_pos >= key_pos


def ring_slices(order_ref, rows, first, count):
    spread = order_ref.shape[0]
    length = rows // spread
    found = []
    for i in range(count):
        number = first + i
        base = lax.div(number, spread) * rows
        place = order_ref[lax.rem(number, spread)] * length
        found.append(pl.ds(pl.multiple_of(base + place, length), length))
    return found


def forward_kernel(
    query_tile, key_tile, block_ref, order_ref, query_ref, key_value_ref, out_ref, low_ref, total_ref
):
    rows = query_ref.shape[0]
    length = rows // order_ref.shape[0]
    heads = query_ref.shape[1] // HEAD_DIM
    wide = heads * query_tile
    scale = HEAD_DIM ** (-0.5) * math.log2(math.e)

    @pl.loop(0, rows // query_tile)
    def _(index):
        offset = pl.multiple_of(index * query_tile, query_tile)
        places = ring_slices(order_ref, rows, index * (query_tile // length), query_tile // length)
        queries = stack_heads(jnp.concatenate([query_ref[place, :] for place in places], axis=0))
        start = block_ref[0] * rows + offset

        def step(tile, state, masked):
            top, total, summed = state
            here = ring_slices(order_ref, rows, tile * (key_tile // length), key_tile // length)
            keys = jnp.concatenate([key_value_ref[place, :HEAD_DIM] for place in here], axis=0)
            values = jnp.concatenate([key_value_ref[place, HEAD_DIM:] for place in here], axis=0)
            scores = last_dims(keys, queries) * scale
            if masked:
                seen = visible_keys(scores.shape, tile * key_tile, start, query_tile)
                scores = jnp.where(seen, scores, NEG_LARGE)
            new_top = jnp.maximum(top, jnp.max(scores, axis=0, keepdims=True))
            weights = jnp.exp2(scores - new_top)
            rescale = jnp.exp2(top - new_top)
            total = total * rescale + jnp.sum(weights, axis=0, keepdims=True)
            summed = summed * rescale + first_dims(values, weights.astype(jnp.bfloat16))
            return new_top, total, summed

        state = (
            jnp.full((1, wide), NEG_LARGE, jnp.float32),
            jnp.zeros((1, wide), jnp.float32),
            jnp.zeros((HEAD_DIM, wide), jnp.float32),
        )
        full = lax.div(start, key_tile)
        state = lax.fori_loop(0, full, lambda tile, state: step(tile, state, False), state)
        top, total, summed = step(full, state, True)
        result = spread_heads((summed / total).T, heads)
        out_ref[pl.ds(offset, query_tile), :] = result
        low_ref[pl.ds(offset, query_tile), :] = result.astype(jnp.bfloat16)
        log_total = top + jnp.log2(total)
        for i in range(heads):
            total_ref[i : i + 1, pl.ds(offset, query_tile)] = log_total[
                :, i * query_tile : (i + 1) * query_tile
            ]


def backward_kernel(
    query_tile,
    key_tile,
    block_ref,
    order_ref,
    query_ref,
    key_value_ref,
    out_ref,
    grad_ref,
    total_ref,
    cosine_ref,
    sine_ref,
    query_grad_ref,
    key_value_grad_ref,
):
    rows = query_ref.shape[0]
    length = rows // order_ref.shape[0]
    heads = query_ref.shape[1] // HEAD_DIM
    wide = heads * query_tile
    score_scale = HEAD_DIM ** (-0.5)
    scale = score_scale * math.log2(math.e)

    @pl.loop(0, key_value_ref.shape[0] // key_tile)
    def _(tile):
        key_start = pl.multiple_of(tile * key_tile, key_tile)
        key_value_grad_ref[pl.ds(key_start, key_tile), :] = jnp.zeros(
            (key_tile, 2 * HEAD_DIM), jnp.float32
        )

    @pl.loop(0, rows // query_tile)
    def _(index):
        offset = pl.multiple_of(index * query_tile, query_tile)
        places = ring_slices(order_ref, rows, index * (query_tile // length), query_tile // length)
        queries = stack_heads(jnp.concatenate([query_ref[place, :] for place in places], axis=0))
        grads = stack_heads(grad_ref[pl.ds(offset, query_tile), :])
        outs = stack_heads(out_ref[pl.ds(offset, query_tile), :])
        delta = jnp.sum((grads.astype(jnp.float32) * outs).T, axis=0, keepdims=True)
        log_total = stack_lanes(total_ref[:, pl.ds(offset, query_tile)])
        start = block_ref[0] * rows + offset

        def step(tile, query_grad, masked):
            here = ring_slices(order_ref, rows, tile * (key_tile // length), key_tile // length)
            keys = jnp.concatenate([key_value_ref[place, :HEAD_DIM] for place in here], axis=0)
            values = jnp.concatenate([key_value_ref[place, HEAD_DIM:] for place in here], axis=0)
            weights = jnp.exp2(last_dims(keys, queries) * scale - log_total)
            if masked:
                seen = visible_keys(weights.shape, tile * key_tile, start, query_tile)
                weights = jnp.where(seen, weights, 0.0)
            value_part = plain_dot(weights.astype(jnp.bfloat16), grads)
            score_grad = (weights * (last_dims(values, grads) - delta)).astype(jnp.bfloat16)
            key_part = plain_dot(score_grad, queries) * score_scale
            part = jnp.concatenate([key_part, value_part], axis=1)
            for i, place in enumerate(here):
                key_value_grad_ref[place, :] += part[i * length : (i + 1) * length]
            return query_grad + first_dims(score_grad, keys)

        full = lax.div(start, key_tile)
        query_grad = lax.fori_loop(
            0,
            full,
            lambda tile, state: step(tile, state, False),
            jnp.zeros((wide, HEAD_DIM), jnp.float32),
        )
        query_grad = step(full, query_grad, True) * score_scale
        for i, place in enumerate(places):
            cosine = cosine_ref[place, :]
            sine = sine_ref[place, :]
            for head in range(heads):
                begin = head * query_tile + i * length
                part = query_grad[begin : begin + length]
                turned = part * cosine - pltpu.roll(part, HEAD_DIM // 2, 1) * sine
                query_grad_ref[place, head * HEAD_DIM : (head + 1) * HEAD_DIM] = turned.astype(
                    jnp.bfloat16
                )


def attention_forward(block_index, order, queries, keys):
    rows, wide = queries.shape
    return pl.pallas_call(
        functools.partial(forward_kernel, math.gcd(rows, 1024), math.gcd(rows, 1024)),
        out_shape=(
            jax.ShapeDtypeStruct((rows, wide), jnp.float32),
            jax.ShapeDtypeStruct((rows, wide), jnp.bfloat16),
            jax.ShapeDtypeStruct((wide // HEAD_DIM, rows), jnp.float32),
        ),
        in_specs=in_smem(2) + in_vmem(2),
        out_specs=tuple(in_vmem(3)),
        **kernel_options(50),
    )(block_index.reshape(1), order, queries, keys)


def attention_backward(block_index, order, queries, keys, outs, grads, log_total, cosine, sine):
    rows, wide = queries.shape
    return pl.pallas_call(
        functools.partial(backward_kernel, math.gcd(rows, 512), math.gcd(rows, 512)),
        out_shape=(
            jax.ShapeDtypeStruct((rows, wide), jnp.bfloat16),
            jax.ShapeDtypeStruct((keys.shape[0], 2 * HEAD_DIM), jnp.float32),
        ),
        in_specs=in_smem(2) + in_vmem(7),
        out_specs=tuple(in_vmem(2)),
        **kernel_options(44),
    )(block_index.reshape(1), order, queries, keys, outs, grads, log_total, cosine, sine)


def dispatch_kernel(piece_count, experts, *refs):
    pieces = refs[:piece_count]
    chosen_ref, whole_ref, rows_ref = refs[piece_count:]
    start = 0
    for piece in pieces:
        whole_ref[start : start + piece.shape[0], :] = piece[...]
        start += piece.shape[0]
    length = chosen_ref.shape[2]
    capacity = chosen_ref.shape[1] // experts
    for block in range(chosen_ref.shape[0]):
        picked = plain_dot(chosen_ref[block], whole_ref[block * length : (block + 1) * length, :])
        picked = picked.astype(jnp.bfloat16)
        for expert in range(experts):
            rows_ref[expert, block * capacity : (block + 1) * capacity, :] = picked[
                expert * capacity : (expert + 1) * capacity
            ]


def dispatch(pieces, chosen, experts):
    rows = sum(piece.shape[0] for piece in pieces)
    width = pieces[0].shape[1]
    blocks, slots, _ = chosen.shape
    return pl.pallas_call(
        functools.partial(dispatch_kernel, len(pieces), experts),
        out_shape=(
            jax.ShapeDtypeStruct((rows, width), jnp.bfloat16),
            jax.ShapeDtypeStruct((experts, blocks * (slots // experts), width), jnp.bfloat16),
        ),
        in_specs=in_vmem(len(pieces) + 1),
        out_specs=tuple(in_vmem(2)),
        **kernel_options(),
    )(*pieces, chosen)


def hidden_tiles(width, tile):
    return [slice(start, min(start + tile, width)) for start in range(0, width, tile)]


def slopes(pre_gate, pre_up):
    sigmoid = 1.0 / (1.0 + jnp.exp(-pre_gate))
    silu = pre_gate * sigmoid
    return silu * pre_up, pre_up * sigmoid * (1.0 + pre_gate * (1.0 - sigmoid)), silu


def expert_forward_kernel(rows_ref, weight_gate_ref, weight_up_ref, act_ref, by_gate_ref, by_up_ref):
    for here in hidden_tiles(act_ref.shape[2], 256):
        pre_gate = plain_dot(rows_ref[0], weight_gate_ref[0, :, here])
        pre_up = plain_dot(rows_ref[0], weight_up_ref[0, :, here])
        act, by_gate, by_up = slopes(pre_gate, pre_up)
        act_ref[0, :, here] = act.astype(jnp.bfloat16)
        by_gate_ref[0, :, here] = by_gate.astype(jnp.bfloat16)
        by_up_ref[0, :, here] = by_up.astype(jnp.bfloat16)


def one_expert(*shape):
    return pl.BlockSpec((1,) + shape, lambda expert: (expert, 0, 0))


def expert_forward(rows, weight_gate, weight_up):
    experts, count, width = rows.shape
    hidden = weight_gate.shape[2]
    return pl.pallas_call(
        expert_forward_kernel,
        grid=(experts,),
        out_shape=(jax.ShapeDtypeStruct((experts, count, hidden), jnp.bfloat16),) * 3,
        in_specs=[one_expert(count, width), one_expert(width, hidden), one_expert(width, hidden)],
        out_specs=(one_expert(count, hidden),) * 3,
        **kernel_options(),
    )(rows, weight_gate, weight_up)


def expert_backward_kernel(
    first_ref,
    grad_ref,
    gate_ref,
    act_ref,
    by_gate_ref,
    by_up_ref,
    weight_gate_ref,
    weight_up_ref,
    weight_down_ref,
    gate_grad_ref,
    up_grad_ref,
    row_grad_ref,
):
    width = weight_gate_ref.shape[1]
    count = grad_ref.shape[1]
    score = jnp.zeros((count, 1), jnp.float32)
    for here in hidden_tiles(act_ref.shape[2], 256):
        act_grad = last_dims(grad_ref[0], weight_down_ref[0, here, :])
        score = score + jnp.sum(
            act_ref[0, :, here].astype(jnp.float32) * act_grad, axis=1, keepdims=True
        )
        act_grad = act_grad * gate_ref[0]
        gate_grad_ref[0, :, here] = (act_grad * by_gate_ref[0, :, here].astype(jnp.float32)).astype(
            jnp.bfloat16
        )
        up_grad_ref[0, :, here] = (act_grad * by_up_ref[0, :, here].astype(jnp.float32)).astype(
            jnp.bfloat16
        )

    for here in hidden_tiles(width, 512):
        row_grad_ref[0, :, here] = (
            last_dims(gate_grad_ref[0], weight_gate_ref[0, here, :])
            + last_dims(up_grad_ref[0], weight_up_ref[0, here, :])
        ).astype(jnp.bfloat16)

    lane = lax.broadcasted_iota(jnp.int32, (count, HEAD_DIM), 1)
    own = first_ref[0] + pl.program_id(0)
    row_grad_ref[0, :, width:] = jnp.where(lane == own, score, 0.0).astype(jnp.bfloat16)


def expert_backward(first_expert, grads, gates, act, by_gate, by_up, weight_gate, weight_up, weight_down):
    experts, count, width = grads.shape
    hidden = act.shape[2]
    low = one_expert(count, hidden)
    return pl.pallas_call(
        expert_backward_kernel,
        grid=(experts,),
        out_shape=(
            jax.ShapeDtypeStruct((experts, count, hidden), jnp.bfloat16),
            jax.ShapeDtypeStruct((experts, count, hidden), jnp.bfloat16),
            jax.ShapeDtypeStruct((experts, count, width + HEAD_DIM), jnp.bfloat16),
        ),
        in_specs=in_smem(1)
        + [
            one_expert(count, width),
            one_expert(count, 1),
            low,
            low,
            low,
            one_expert(width, hidden),
            one_expert(width, hidden),
            one_expert(hidden, width),
        ],
        out_specs=(low, low, one_expert(count, width + HEAD_DIM)),
        **kernel_options(),
    )(first_expert.reshape(1), grads, gates, act, by_gate, by_up, weight_gate, weight_up, weight_down)


def result_kernel(act_ref, gate_ref, weight_ref, out_ref):
    for here in hidden_tiles(out_ref.shape[2], 512):
        result = plain_dot(act_ref[0], weight_ref[0, :, here]).astype(jnp.bfloat16)
        out_ref[0, :, here] = (result.astype(jnp.float32) * gate_ref[0]).astype(jnp.bfloat16)


def expert_results(act, gates, weight_down):
    experts, count, hidden = act.shape
    width = weight_down.shape[2]

    def one(*shape):
        return pl.BlockSpec((1,) + shape, lambda expert: (expert, 0, 0))

    return pl.pallas_call(
        result_kernel,
        grid=(experts,),
        out_shape=jax.ShapeDtypeStruct((experts, count, width), jnp.bfloat16),
        in_specs=[one(count, hidden), one(count, 1), one(hidden, width)],
        out_specs=one(count, width),
        **kernel_options(),
    )(act, gates, weight_down)


def combine_kernel(turned, chosen_ref, values_ref, left_ref, right_ref, out_ref):
    width = right_ref.shape[0] if turned else right_ref.shape[1]
    experts = values_ref.shape[0]
    length = chosen_ref.shape[1]
    capacity = chosen_ref.shape[2] // experts
    blocks = chosen_ref.shape[0]

    def slots(block, here):
        values = [
            values_ref[expert, block * capacity : (block + 1) * capacity, here]
            for expert in range(experts)
        ]
        return plain_dot(chosen_ref[block], jnp.concatenate(values, axis=0))

    for here in hidden_tiles(width, 512):
        shared = (
            last_dims(left_ref[...], right_ref[here, :])
            if turned
            else plain_dot(left_ref[...], right_ref[:, here])
        )
        for block in range(blocks):
            rows = slice(block * length, (block + 1) * length)
            out_ref[rows, here] = (shared[rows] + slots(block, here)).astype(jnp.bfloat16)

    if out_ref.shape[1] > width:
        for block in range(blocks):
            out_ref[block * length : (block + 1) * length, width:] = slots(
                block, slice(width, out_ref.shape[1])
            ).astype(jnp.bfloat16)


def combine(chosen, values, left, right, turned):
    blocks, length, slots = chosen.shape
    experts, _, wide = values.shape
    capacity = slots // experts
    some = math.gcd(blocks, 2)
    return pl.pallas_call(
        functools.partial(combine_kernel, turned),
        grid=(blocks // some,),
        out_shape=jax.ShapeDtypeStruct((blocks * length, wide), jnp.bfloat16),
        in_specs=[
            pl.BlockSpec((some, length, slots), lambda i: (i, 0, 0)),
            pl.BlockSpec((experts, some * capacity, wide), lambda i: (0, i, 0)),
            pl.BlockSpec((some * length, left.shape[1]), lambda i: (i, 0)),
            pl.BlockSpec(right.shape, lambda i: (0, 0)),
        ],
        out_specs=pl.BlockSpec((some * length, wide), lambda i: (i, 0)),
        **kernel_options(32),
    )(chosen, values, left, right)


def shared_kernel(normed_ref, grad_ref, weight_ref, down_ref, act_ref, both_ref):
    hidden = act_ref.shape[1]
    pre_gate = plain_dot(normed_ref[...], weight_ref[:, :hidden])
    pre_up = plain_dot(normed_ref[...], weight_ref[:, hidden:])
    act_grad = last_dims(grad_ref[...], down_ref[...])
    act, by_gate, by_up = slopes(pre_gate, pre_up)
    act_ref[...] = act.astype(jnp.bfloat16)
    both_ref[:, :hidden] = (act_grad * by_gate).astype(jnp.bfloat16)
    both_ref[:, hidden:] = (act_grad * by_up).astype(jnp.bfloat16)


def shared_pass(normed, grads, weight, down):
    rows, width = normed.shape
    hidden = down.shape[0]
    some = math.gcd(rows, 256)

    def part(columns):
        return pl.BlockSpec((some, columns), lambda i: (i, 0))

    return pl.pallas_call(
        shared_kernel,
        grid=(rows // some,),
        out_shape=(
            jax.ShapeDtypeStruct((rows, hidden), jnp.bfloat16),
            jax.ShapeDtypeStruct((rows, 2 * hidden), jnp.bfloat16),
        ),
        in_specs=[
            part(width),
            part(width),
            pl.BlockSpec(weight.shape, lambda i: (0, 0)),
            pl.BlockSpec(down.shape, lambda i: (0, 0)),
        ],
        out_specs=(part(hidden), part(2 * hidden)),
        **kernel_options(32),
    )(normed, grads, weight, down)


def part_kernel(scaled, added, core_ref, left_ref, right_ref, *refs):
    right = right_ref[0]
    if scaled:
        right = (right.astype(jnp.float32) * refs[0][0]).astype(jnp.bfloat16)
    total = first_dims(left_ref[0], right)
    if added:
        total = total + refs[-2][0, 0].astype(jnp.float32)
    refs[-1][0, 0] = total.astype(jnp.bfloat16)


def weight_parts(core, left, right, cut_left, gates=None, received=None, slices=1, number=0, wide=False):
    chips = lax.axis_size("far")
    parts = 2 * chips * slices
    experts, count, left_width = left.shape
    right_width = right.shape[2]
    left_width, right_width = (
        (left_width // parts, right_width) if cut_left else (left_width, right_width // parts)
    )

    def spec(columns, cut):
        if cut:
            return pl.BlockSpec(
                (1, count, columns), lambda f, e, c: (e, 0, (2 * f + c[0]) * slices + number)
            )
        return pl.BlockSpec((1, count, columns), lambda f, e, c: (e, 0, 0))

    whole = pl.BlockSpec((1, 1, left_width, right_width), lambda f, e, c: (f, e, 0, 0))
    operands = [left, right]
    specs = [spec(left_width, cut_left), spec(right_width, not cut_left)]
    if gates is not None:
        operands.append(gates)
        specs.append(pl.BlockSpec((1, count, 1), lambda f, e, c: (e, 0, 0)))
    if received is not None:
        operands.append(received)
        place = (lambda f, e, c: (f, e, number, 0)) if cut_left else (lambda f, e, c: (f, e, 0, number))
        specs.append(pl.BlockSpec((1, 1, left_width, right_width), place))
    return pl.pallas_call(
        functools.partial(part_kernel, gates is not None, received is not None),
        grid_spec=pltpu.PrefetchScalarGridSpec(
            num_scalar_prefetch=1, grid=(chips, experts), in_specs=specs, out_specs=whole
        ),
        out_shape=jax.ShapeDtypeStruct((chips, experts, left_width, right_width), jnp.bfloat16),
        **kernel_options(60 if wide else 24),
    )(core.reshape(1), *operands)


def output_weight_kernel(piece_count, index_ref, core_ref, grad_ref, *refs):
    pieces = refs[:piece_count]
    keep_ref, send_ref = refs[piece_count:]
    wide = pieces[0].shape[1]
    half = piece_count // 2
    length = keep_ref.shape[1]
    some = min(wide, length)

    def part(piece, start):
        return first_dims(piece[...], grad_ref[start : start + piece.shape[0], :])

    def place(total, first):
        target = lax.div(first, length)
        chip = lax.div(target, 2)
        offset = pl.multiple_of(lax.rem(first, length), some)
        mine = lax.rem(target, 2) == core_ref[0]

        @pl.when(mine)
        def _():
            keep_ref[chip, pl.ds(offset, some), :] = total

        @pl.when(jnp.logical_not(mine))
        def _():
            send_ref[chip, pl.ds(offset, some), :] = total

    for block in range(index_ref.shape[0]):
        if block < half:
            total = part(pieces[block], 0)
        elif block == half:
            total = part(pieces[half], 0) + part(pieces[half + 1], pieces[half].shape[0])
        else:
            total = part(pieces[block + 1], 0)
        total = total.astype(jnp.bfloat16)
        for start in range(0, wide, some):
            place(total[start : start + some], index_ref[block] * wide + start)


def output_weight(index, core, grads, pieces):
    chips = lax.axis_size("far")
    length = index.shape[0] * pieces[0].shape[1] // (2 * chips)
    return pl.pallas_call(
        functools.partial(output_weight_kernel, len(pieces)),
        out_shape=(jax.ShapeDtypeStruct((chips, length, grads.shape[1]), jnp.bfloat16),) * 2,
        in_specs=in_smem(2) + in_vmem(len(pieces) + 1),
        out_specs=tuple(in_vmem(2)),
        **kernel_options(),
    )(index, core.reshape(1), grads, *pieces)


def hidden_send_kernel(own, chips, gate_ref, up_ref, out_ref):
    spread = out_ref.shape[0]
    wide = out_ref.shape[2] // 2
    piece = own // chips
    blank = [jnp.zeros((gate_ref.shape[0], wide - own), jnp.float32)] if wide > own else []
    for start, weight_ref in ((0, gate_ref), (wide, up_ref)):
        weight = weight_ref[...].astype(jnp.float32)
        for device in range(spread):
            columns = [
                weight[:, (chip * spread + device) * piece : (chip * spread + device + 1) * piece]
                for chip in range(chips)
            ]
            out_ref[device, :, start : start + wide] = jnp.concatenate(
                columns + blank, axis=1
            ).astype(jnp.bfloat16)


def hidden_send(gate, up, own, wide, chips, spread):
    return pl.pallas_call(
        functools.partial(hidden_send_kernel, own, chips),
        out_shape=jax.ShapeDtypeStruct((spread, gate.shape[0], 2 * wide), jnp.bfloat16),
        in_specs=in_vmem(2),
        out_specs=pl.BlockSpec(memory_space=pltpu.VMEM),
        **kernel_options(),
    )(gate, up)


def hidden_home_kernel(own, chips, back_ref, gate_ref, up_ref):
    spread = back_ref.shape[0]
    wide = back_ref.shape[2] // 2
    piece = own // chips
    for start, out_ref in ((0, gate_ref), (wide, up_ref)):
        values = [
            back_ref[device, :, start : start + wide].astype(jnp.float32)
            for device in range(spread)
        ]
        out_ref[...] = jnp.concatenate(
            [
                values[device][:, chip * piece : (chip + 1) * piece]
                for chip in range(chips)
                for device in range(spread)
            ],
            axis=1,
        )


def hidden_home(back, own, chips):
    spread, rows, _ = back.shape
    return pl.pallas_call(
        functools.partial(hidden_home_kernel, own, chips),
        out_shape=(jax.ShapeDtypeStruct((rows, own * spread), jnp.float32),) * 2,
        in_specs=in_vmem(1),
        out_specs=tuple(in_vmem(2)),
        **kernel_options(12),
    )(back)


def dense_home_kernel(back_ref, weight_ref, gain_ref, qkv_ref, out_ref, small_ref, gain_grad_ref):
    spread, _, wide = back_ref.shape
    own = QUERY_HEADS * HEAD_DIM // spread
    repeat = spread // KEY_VALUE_HEADS
    out_wide = out_ref.shape[1] // spread
    score = jnp.zeros(gain_ref.shape, jnp.float32)

    def keep(score, start, values):
        columns = slice(start, start + values.shape[1])
        qkv_ref[:, columns] = values * gain_ref[...]
        weight = weight_ref[:, columns].astype(jnp.float32)
        return score + jnp.sum(weight * values, axis=1, keepdims=True)

    small = jnp.zeros(small_ref.shape, jnp.float32)
    for device in range(spread):
        score = keep(score, device * own, back_ref[device, :, :own].astype(jnp.float32))
        start = own + 2 * HEAD_DIM
        out_ref[:, device * out_wide : (device + 1) * out_wide] = back_ref[
            device, :, start : start + out_wide
        ].astype(jnp.float32)
        small = small + back_ref[device, :, start + out_wide :].astype(jnp.float32)
    for part in range(2):
        for head in range(KEY_VALUE_HEADS):
            start = own + part * HEAD_DIM
            values = sum(
                back_ref[head * repeat + i, :, start : start + HEAD_DIM].astype(jnp.float32)
                for i in range(repeat)
            )
            place = QUERY_HEADS * HEAD_DIM + (part * KEY_VALUE_HEADS + head) * HEAD_DIM
            score = keep(score, place, values)
    small_ref[...] = small
    gain_grad_ref[...] = score


def dense_home(back, weight, gain, width):
    rows, qkv_width = weight.shape
    return pl.pallas_call(
        dense_home_kernel,
        out_shape=(
            jax.ShapeDtypeStruct((rows, qkv_width), jnp.float32),
            jax.ShapeDtypeStruct((rows, width), jnp.float32),
            jax.ShapeDtypeStruct((rows, HEAD_DIM), jnp.float32),
            jax.ShapeDtypeStruct((rows, 1), jnp.float32),
        ),
        in_specs=in_vmem(3),
        out_specs=tuple(in_vmem(4)),
        **kernel_options(12),
    )(back, weight, gain)


def product_kernel(left_ref, right_ref, out_ref):
    for here in hidden_tiles(out_ref.shape[0], 512):
        out_ref[here, :] = first_dims(left_ref[:, here], right_ref[...]).astype(jnp.bfloat16)


def row_product(left, right, columns):
    return pl.pallas_call(
        product_kernel,
        out_shape=jax.ShapeDtypeStruct((columns, right.shape[1]), jnp.bfloat16),
        in_specs=in_vmem(2),
        out_specs=pl.BlockSpec(memory_space=pltpu.VMEM),
        **kernel_options(24),
    )(left, right)


def widen_kernel(*refs):
    out_ref = refs[-1]
    start = 0
    for part_ref in refs[:-1]:
        rows = part_ref.shape[1]
        out_ref[0, start : start + rows, :] = part_ref[0].astype(jnp.float32)
        start += rows


def widen(*parts):
    experts, _, columns = parts[0].shape
    rows = sum(part.shape[1] for part in parts)
    return pl.pallas_call(
        widen_kernel,
        grid=(experts,),
        out_shape=jax.ShapeDtypeStruct((experts, rows, columns), jnp.float32),
        in_specs=[one_expert(part.shape[1], columns) for part in parts],
        out_specs=one_expert(rows, columns),
        **kernel_options(28),
    )(*parts)


def project_back_kernel(
    query_ref, own_ref, last_ref, cosine_ref, sine_ref, weight_ref, projected_ref, out_ref
):
    wide = query_ref.shape[1]
    projected_ref[:, :wide] = query_ref[...]
    total = own_ref[...] + last_ref[...].astype(jnp.float32)
    keys = total[:, :HEAD_DIM]
    turned = keys * cosine_ref[...] - pltpu.roll(keys, HEAD_DIM // 2, 1) * sine_ref[...]
    projected_ref[:, wide : wide + HEAD_DIM] = turned.astype(jnp.bfloat16)
    projected_ref[:, wide + HEAD_DIM :] = total[:, HEAD_DIM:].astype(jnp.bfloat16)
    for here in hidden_tiles(out_ref.shape[1], 512):
        out_ref[:, here] = last_dims(projected_ref[...], weight_ref[here, :]).astype(jnp.bfloat16)


def project_back(queries, own, last, cosine, sine, weight):
    rows = queries.shape[0]
    return pl.pallas_call(
        project_back_kernel,
        out_shape=(
            jax.ShapeDtypeStruct((rows, weight.shape[1]), jnp.bfloat16),
            jax.ShapeDtypeStruct((rows, weight.shape[0]), jnp.bfloat16),
        ),
        in_specs=in_vmem(6),
        out_specs=tuple(in_vmem(2)),
        **kernel_options(24),
    )(queries, own, last, cosine, sine, weight)


def finish_kernel(first_ref, second_ref, own_ref, tokens_ref, grad_ref, out_ref):
    weighted = (
        first_ref[...].astype(jnp.float32)
        + second_ref[...].astype(jnp.float32)
        + own_ref[...].astype(jnp.float32)
    )
    inputs = tokens_ref[...].astype(jnp.float32)
    scale = lax.rsqrt(jnp.mean(inputs * inputs, axis=-1, keepdims=True) + EPSILON)
    inner_mean = jnp.mean(weighted * inputs, axis=-1, keepdims=True)
    out_ref[...] = grad_ref[...] + scale * weighted - inputs * (scale * scale * scale * inner_mean)


def finish(first, second, own, tokens, grads):
    return pl.pallas_call(
        finish_kernel,
        out_shape=jax.ShapeDtypeStruct(grads.shape, jnp.float32),
        in_specs=in_vmem(5),
        out_specs=pl.BlockSpec(memory_space=pltpu.VMEM),
        **kernel_options(16),
    )(first, second, own, tokens, grads)


def body(
    tokens,
    attn_gain,
    query_key_value_weight,
    out_weight,
    ffn_gain,
    router_weight,
    shared_gate,
    shared_up,
    shared_down,
    routed_gate_weight,
    routed_up_weight,
    routed_down_weight,
    routes,
    cotangent,
):
    f32 = jnp.float32
    bf16 = jnp.bfloat16
    both = CONTEXT + ("experts",)
    context_count = context_size()
    spread = lax.axis_size("experts")
    context_index = lax.axis_index(CONTEXT)
    expert_index = lax.axis_index("experts")
    token_count, width = tokens.shape
    local_experts = routed_gate_weight.shape[0]
    experts_all = local_experts * spread
    rows = token_count * spread
    weight_rows = query_key_value_weight.shape[0]
    query_width = QUERY_HEADS * HEAD_DIM
    key_width = KEY_VALUE_HEADS * HEAD_DIM
    repeat_times = spread // KEY_VALUE_HEADS
    head_share = QUERY_HEADS // spread
    own_width = head_share * HEAD_DIM
    block_width = width // context_count

    def key_columns(weight):
        heads = weight.reshape(weight_rows, KEY_VALUE_HEADS, HEAD_DIM)
        return jnp.repeat(heads, repeat_times, axis=1)

    own_gain = attn_gain.astype(f32)[:, None]
    qkv_scaled = (query_key_value_weight.astype(f32) * own_gain).astype(bf16)
    qkv_send = jnp.concatenate(
        [
            qkv_scaled[:, :query_width].reshape(weight_rows, spread, own_width),
            key_columns(qkv_scaled[:, query_width : query_width + key_width]),
            key_columns(qkv_scaled[:, query_width + key_width :]),
        ],
        axis=2,
    ).transpose(1, 0, 2)
    hidden_piece = shared_down.shape[0]
    hidden_own = hidden_piece * context_count
    hidden_wide = -(-hidden_own // HEAD_DIM) * HEAD_DIM

    shared_send = hidden_send(
        shared_gate, shared_up, hidden_own, hidden_wide, context_count, spread
    )

    token_ring = RingGather(tokens)
    token_ring.step()
    position = context_index * rows + jnp.arange(rows, dtype=jnp.int32)
    position = ring_order(position.reshape(spread, token_count)).reshape(rows).astype(f32)
    half_width = HEAD_DIM // 2
    frequency = THETA ** (-jnp.arange(half_width, dtype=f32) * 2.0 / HEAD_DIM)
    angles = position[:, None] * frequency[None, :]
    cosine = jnp.cos(angles)
    sine = jnp.sin(angles)
    cosine = jnp.concatenate([cosine, cosine], axis=1)
    sine = jnp.concatenate([-sine, sine], axis=1)
    small = jnp.concatenate([ffn_gain[None], router_weight.T], axis=0)
    small = flip_double(small[None], CONTEXT)
    qkv_send = after(small, qkv_send)
    qkv_rows = to_experts(qkv_send).reshape(spread * weight_rows, -1)
    while small.shape[0] < context_count:
        small = flip_double(small, CONTEXT)
    small = jnp.concatenate([small.reshape(1, -1), routes.astype(bf16).reshape(1, -1)], axis=1)
    small, cosine, sine = meet([token_ring], small, cosine, sine)
    token_ring.step()
    (qkv_rows,) = meet([token_ring], qkv_rows)
    token_ring.step()
    qkv_far = far_gather(qkv_rows)
    qkv_far, out_weight = meet([token_ring], qkv_far, out_weight)
    token_ring.step()
    qkv_own = core_gather(qkv_far)
    (qkv_own,) = meet([token_ring], qkv_own)
    small = after(token_ring.latest(), small)

    out_full = lax.all_gather(out_weight, both, axis=0, tiled=True)
    normed_one, query_rows, key_value = project(
        token_ring.pieces(), qkv_own, cosine, sine, own_width
    )
    key_value = far_gather(key_value)
    small = flip_double(small, "experts")
    key_value, small = lax.optimization_barrier((key_value, small))
    key_value = core_gather(key_value)
    small = flip_double(small, "experts")
    place = ring_place(expert_index, spread)
    order = (ring_place(jnp.arange(spread, dtype=jnp.int32), spread) - place + spread) % spread
    attended, attended_low, log_total = attention_forward(
        context_index, order, query_rows, key_value
    )
    attended_low, small = lax.optimization_barrier((attended_low, small))
    attended_tok = (
        to_experts(attended_low.reshape(spread, token_count, own_width))
        .transpose(1, 0, 2)
        .reshape(token_count, query_width)
    )
    while small.shape[0] < spread:
        small = flip_double(small, "experts")
    attended_tok, small = lax.optimization_barrier((attended_tok, small))
    routes_block = small[:, -token_count * TOP :].reshape(spread, token_count, TOP)
    routes_block = routes_block.astype(jnp.int32).transpose(0, 2, 1)
    small = small[:, : -token_count * TOP].reshape(spread, context_count, -1, weight_rows)
    small = small.transpose(2, 1, 0, 3).reshape(-1, width)
    gain_two = small[0].astype(f32)
    router_full = small[1:]

    inputs = tokens.astype(f32)
    middle = inputs + jnp.dot(attended_tok, out_full, preferred_element_type=f32)
    scale_two = rms_scale(middle)
    normed_two = (middle * scale_two * gain_two).astype(bf16)
    normed_ring = RingGather(normed_two)
    normed_ring.step()
    routes_block, router_full, shared_down = meet(
        [normed_ring], routes_block, router_full, shared_down
    )

    normed_ring.step()
    down_far = far_gather(shared_down)
    first_expert = expert_index * local_experts
    own_ids = first_expert + jnp.arange(local_experts, dtype=jnp.int32)
    routes_block = ring_order(routes_block)
    member = jnp.any(routes_block[:, None] == own_ids[None, :, None, None], axis=2)
    counted = member.astype(jnp.int32)
    slot_index = jnp.cumsum(counted, axis=2) - counted
    capacity = token_count * TOP * 4 // (3 * experts_all)
    slot = jnp.arange(capacity, dtype=jnp.int32)
    chosen = member[:, :, None, :] & (slot_index[:, :, None, :] == slot[None, None, :, None])
    chosen_wide = chosen.astype(f32)
    slots = local_experts * capacity
    chosen_low = chosen.astype(bf16).reshape(spread, slots, token_count)
    chosen_back = chosen_low.transpose(0, 2, 1)
    down_far, chosen_low, chosen_wide, chosen_back = meet(
        [normed_ring], down_far, chosen_low, chosen_wide, chosen_back
    )
    normed_ring.step()
    down_own = jnp.pad(core_gather(down_far), ((0, hidden_wide - hidden_own), (0, 0)))
    (down_own,) = meet([normed_ring], down_own)
    normed_ring.step()
    (cotangent_late,) = meet([normed_ring], cotangent)
    grad_ring = RingGather(cotangent_late)
    grad_ring.step()
    normed_block, expert_rows = dispatch(normed_ring.pieces(), chosen_low, local_experts)

    (normed_block,) = meet([grad_ring], normed_block)
    grad_ring.step()
    router_probs = jax.nn.softmax(dot_last(normed_block, router_full), axis=-1)
    gate_tokens = (
        lax.dynamic_slice_in_dim(router_probs, first_expert, local_experts, 1)
        .reshape(spread, token_count, local_experts)
        .transpose(0, 2, 1)
    )
    gates = jnp.sum(chosen_wide * gate_tokens[:, :, None, :], axis=3)
    gates = gates.transpose(1, 0, 2).reshape(local_experts, spread * capacity, 1)
    expert_rows = after(gates, expert_rows)
    act, by_gate, by_up = expert_forward(expert_rows, routed_gate_weight, routed_up_weight)
    act, gates = meet([grad_ring], act, gates)
    grad_ring.step()
    weighted_y = expert_results(act, gates, routed_down_weight)
    (weighted_y,) = meet([grad_ring], weighted_y)
    grad_ring.step()
    chosen_low, shared_send = meet([grad_ring], chosen_low, shared_send)
    grad_block, grad_rows = dispatch(grad_ring.pieces(), chosen_low, local_experts)

    own_core = lax.axis_index("core")
    other_core = 1 - own_core
    shared_rows = to_experts(shared_send).reshape(spread * weight_rows, -1)
    down_parts = weight_parts(other_core, act, grad_rows, False, gates, wide=True)
    down_parts, shared_rows, attended_late = lax.optimization_barrier(
        (down_parts, shared_rows, attended_low)
    )
    shared_far = far_gather(shared_rows)
    down_received = core_swap(down_parts)
    heads_ring = RingGather(attended_late)
    heads_ring.step()
    grad_rows, gates = after(down_parts, grad_rows, gates)
    expert_dg, expert_du, row_grad = expert_backward(
        first_expert,
        grad_rows,
        gates,
        act,
        by_gate,
        by_up,
        routed_gate_weight,
        routed_up_weight,
        routed_down_weight,
    )
    row_grad, shared_far, down_received = meet(
        [heads_ring], row_grad, shared_far, down_received
    )
    heads_ring.step()
    shared_own = core_gather(shared_far)
    shared_act, shared_both = shared_pass(normed_block, grad_block, shared_own, down_own)
    shared_act, shared_both = meet([heads_ring], shared_act, shared_both)
    heads_ring.step()
    grad_part = combine(chosen_back, row_grad, shared_both, shared_own, True)
    grad_scatter = RingScatter(grad_part)
    grad_scatter.step()
    expert_dg, expert_du, weighted_y, act = after(
        grad_part, expert_dg, expert_du, weighted_y, act
    )
    down_parts = weight_parts(own_core, act, grad_rows, False, gates, down_received)
    (down_parts,) = meet([grad_scatter, heads_ring], down_parts)
    down_sum = chips_sum(down_parts)
    grad_scatter.step()
    heads_ring.step()
    expert_dg = after(down_parts, expert_dg)
    gate_parts = weight_parts(other_core, expert_rows, expert_dg, True)
    shared_parts = weight_parts(
        other_core, after(gate_parts, normed_block)[None], shared_both[None], True
    )
    gate_parts, shared_parts = meet([grad_scatter, heads_ring], gate_parts, shared_parts)
    grad_scatter.step()
    gate_received = core_swap(gate_parts)
    shared_received = core_swap(shared_parts)
    weighted_y = after(shared_parts, weighted_y)
    out_part = combine(chosen_back, weighted_y, shared_act, down_own, False)
    out_part, gate_received = lax.optimization_barrier((out_part, gate_received))
    gate_parts = weight_parts(own_core, expert_rows, expert_dg, True, None, gate_received)
    gate_parts, shared_received, out_part = meet(
        [grad_scatter], gate_parts, shared_received, out_part
    )
    grad_scatter.step()
    expert_du = after(gate_parts, expert_du)
    up_parts = weight_parts(other_core, expert_rows, expert_du, True)
    shared_parts = weight_parts(
        own_core,
        after(up_parts, normed_block)[None],
        shared_both[None],
        True,
        None,
        shared_received,
    )
    up_parts, shared_parts, out_part = meet([grad_scatter], up_parts, shared_parts, out_part)
    gathered = grad_scatter.total()
    out_scatter = RingScatter(out_part)
    out_scatter.step()
    shared_pair = chips_exchange(shared_parts)

    prob_grad = gathered[:, width : width + experts_all]
    probs_tok = router_probs[:token_count]
    logit_grad = (
        probs_tok * (prob_grad - jnp.sum(probs_tok * prob_grad, axis=-1, keepdims=True))
    ).astype(bf16)
    normed_grad = gathered[:, :width] + jnp.dot(
        logit_grad, router_full, preferred_element_type=f32
    )
    grad_final = cotangent.astype(f32)
    weighted = normed_grad * gain_two
    inner_mean = jnp.mean(weighted * middle, axis=-1, keepdims=True)
    middle_grad = (
        grad_final
        + scale_two * weighted
        - middle * scale_two * scale_two * scale_two * inner_mean
    )
    gain_rows = (normed_grad * middle * scale_two).astype(bf16)
    branch_grad = middle_grad.astype(bf16)
    attended_grad = dot_last(branch_grad, out_full).astype(bf16)
    (attended_grad,) = meet([out_scatter], attended_grad)
    grad_heads = to_experts(
        attended_grad.reshape(token_count, spread, own_width).transpose(1, 0, 2)
    ).reshape(rows, own_width)
    lane = jnp.arange(HEAD_DIM, dtype=jnp.int32)[None, :]
    gain_column = jnp.broadcast_to(lane == experts_all, (token_count, HEAD_DIM)).astype(bf16)
    small_left = jnp.concatenate([normed_two, gain_rows], axis=0)
    small_right = jnp.concatenate(
        [jnp.pad(logit_grad, ((0, 0), (0, HEAD_DIM - experts_all))), gain_column], axis=0
    )
    small_left, small_right, expert_du = after(attended_grad, small_left, small_right, expert_du)
    up_received = core_swap(up_parts)
    slices = 2 if block_width % (2 * HEAD_DIM) == 0 else 1
    up_parts = [
        weight_parts(own_core, expert_rows, expert_du, True, None, up_received, slices, number)
        for number in range(slices)
    ]
    small_parts = weight_parts(other_core, small_left[None], small_right[None], True)
    branch_late, up_parts = after(small_parts, branch_grad, up_parts)
    branch_columns = to_experts(
        branch_late.reshape(token_count, spread, own_width).transpose(1, 0, 2)
    ).reshape(rows, own_width)
    grad_heads, small_parts, up_parts = lax.optimization_barrier((grad_heads, small_parts, up_parts))

    out_scatter.step()
    small_received = core_swap(small_parts)
    query_grad, key_value_all = attention_backward(
        context_index,
        order,
        query_rows,
        key_value,
        attended,
        grad_heads,
        log_total,
        cosine,
        sine,
    )
    key_value_all, branch_columns, small_received, down_sum, shared_last = meet(
        [out_scatter], key_value_all, branch_columns, small_received, down_sum, shared_pair[1]
    )
    gate_sum = chips_sum(gate_parts)
    key_value_all = key_value_all.reshape(context_count, rows, -1)
    key_value_received = core_exchange(block_parts(key_value_all))
    key_value_sums = block_sums(key_value_all, key_value_received)
    (key_value_sums,) = lax.optimization_barrier((key_value_sums,))
    key_value_own, key_value_last = far_exchange(key_value_sums)
    out_scatter.first = after(key_value_sums, out_scatter.first)
    out_scatter.step()
    branch_columns, shared_last, small_left = after(
        key_value_sums, branch_columns, shared_last, small_left
    )
    index = ring_index(place + jnp.arange(spread, dtype=jnp.int32), spread)
    out_keep, out_send = output_weight(index, own_core, branch_columns, heads_ring.pieces())
    small_parts = weight_parts(
        own_core, small_left[None], small_right[None], True, None, small_received
    )
    shared_own_part = both_halves((shared_pair[0].astype(f32), shared_last)).astype(bf16)
    shared_back = to_experts(shared_own_part.reshape(spread, weight_rows, -1))
    key_value_last, out_keep, out_send, small_parts, gate_sum, shared_act = meet(
        [out_scatter], key_value_last, out_keep, out_send, small_parts, gate_sum, shared_act
    )
    up_first = chips_sum(up_parts[0])
    projected_grad, input_part = project_back(
        query_grad, key_value_own, key_value_last, cosine, sine, qkv_own
    )
    input_scatter = RingScatter(input_part)
    input_scatter.step()
    out_received = core_swap(out_send)
    normed_one = after(input_scatter.sent, normed_one)
    qkv_parts = weight_parts(other_core, normed_one[None], projected_grad[None], True)
    qkv_received = core_swap(qkv_parts)
    qkv_parts = weight_parts(
        own_core, normed_one[None], projected_grad[None], True, None, qkv_received
    )
    qkv_parts, out_received, shared_back = meet(
        [input_scatter, out_scatter], qkv_parts, out_received, shared_back
    )
    input_scatter.step()
    qkv_parts, out_received, shared_back, out_scatter.first = after(
        input_scatter.sent, qkv_parts, out_received, shared_back, out_scatter.first
    )
    out_scatter.step()
    out_sums = out_keep.astype(f32) + out_received.astype(f32)
    dense_parts = jnp.concatenate(
        [qkv_parts[:, 0], out_sums.astype(bf16), small_parts[:, 0]], axis=2
    )
    dense_pair = chips_exchange(dense_parts)
    down_sum, shared_act, shared_back = after(dense_parts, down_sum, shared_act, shared_back)
    shared_gate_grad, shared_up_grad = hidden_home(shared_back, hidden_own, context_count)
    expert_down_grad = widen(after(shared_gate_grad, down_sum))
    shared_down_sum = row_product(shared_act, after(expert_down_grad, grad_block), hidden_own)
    shared_down_sum = shared_down_sum.reshape(context_count, hidden_piece, width)
    shared_down_sum, shared_gate_grad = meet(
        [input_scatter, out_scatter], shared_down_sum, shared_gate_grad
    )
    input_scatter.step()
    gate_sum, shared_down_sum = after(input_scatter.sent, gate_sum, shared_down_sum)
    shared_down_received = core_exchange(block_parts(shared_down_sum))
    expert_gate_grad = widen(gate_sum)
    expert_gate_grad, dense_last, shared_down_received = meet(
        [input_scatter], expert_gate_grad, dense_pair[1], shared_down_received
    )
    input_scatter.step()
    up_later = [chips_sum(after((dense_last, up_first), part)) for part in up_parts[1:]]
    dense_last, out_scatter.first, shared_down_received = after(
        input_scatter.sent, dense_last, out_scatter.first, shared_down_received
    )
    dense_sum = both_halves((dense_pair[0].astype(f32), dense_last)).astype(bf16)
    dense_back = to_experts(dense_sum.reshape(spread, weight_rows, -1))
    shared_down_pair = far_exchange(block_sums(shared_down_sum, shared_down_received))
    dense_back, shared_down_pair = meet([input_scatter], dense_back, shared_down_pair)
    shared_down_grad = both_halves(shared_down_pair)
    layer_out = (middle + out_scatter.total()).astype(bf16)
    expert_up_grad = widen(up_first, *up_later)
    qkv_weight_grad, out_weight_grad, small_grad, attn_gain_grad = dense_home(
        dense_back, query_key_value_weight, own_gain, width
    )
    attn_gain_grad = attn_gain_grad[:, 0]
    router_weight_grad = small_grad[:, :experts_all]
    ffn_gain_grad = small_grad[:, experts_all]
    tokens_grad = finish(
        input_scatter.first, input_scatter.second, input_part[:token_count], tokens, middle_grad
    )
    return (
        layer_out,
        tokens_grad,
        attn_gain_grad,
        qkv_weight_grad,
        out_weight_grad,
        ffn_gain_grad,
        router_weight_grad,
        shared_gate_grad,
        shared_up_grad,
        shared_down_grad,
        expert_gate_grad,
        expert_up_grad,
        expert_down_grad,
    )


def solution(mesh):
    context_count, spread = mesh.devices.shape
    split = jax.sharding.Mesh(
        mesh.devices.reshape(context_count // 2, 2, spread), ("far", "core", "experts")
    )
    return jax.shard_map(
        body,
        mesh=split,
        in_specs=(
            P(("far", "core", "experts"), None),
            P(("far", "core", "experts")),
            P(("far", "core", "experts"), None),
            P(("far", "core", "experts"), None),
            P(("far", "core", "experts")),
            P(("far", "core", "experts"), None),
            P(("far", "core", "experts"), None),
            P(("far", "core", "experts"), None),
            P(("far", "core", "experts"), None),
            P("experts", None, None),
            P("experts", None, None),
            P("experts", None, None),
            P(("far", "core", "experts"), None),
            P(("far", "core", "experts"), None),
        ),
        out_specs=(
            P(("far", "core", "experts"), None),
            P(("far", "core", "experts"), None),
            P(("far", "core", "experts")),
            P(("far", "core", "experts"), None),
            P(("far", "core", "experts"), None),
            P(("far", "core", "experts")),
            P(("far", "core", "experts"), None),
            P(("far", "core", "experts"), None),
            P(("far", "core", "experts"), None),
            P(("far", "core", "experts"), None),
            P("experts", CONTEXT, None),
            P("experts", CONTEXT, None),
            P("experts", None, CONTEXT),
        ),
        check_vma=False,
    )
```

```python
import functools
import math

import jax
import jax.numpy as jnp
from jax import lax
from jax.experimental import pallas as pl
from jax.experimental.pallas import tpu as pltpu
from jax.sharding import PartitionSpec as P

QUERY_HEADS = 16
KEY_VALUE_HEADS = 4
HEAD_DIM = 128
TOP = 6


EPSILON = 1e-06
THETA = 10000.0
NEG_LARGE = -1e30
CONTEXT = ("far", "core")


def rms_scale(values):
    return lax.rsqrt(jnp.mean(values * values, axis=-1, keepdims=True) + EPSILON)


def norm_back(values, row_scale, gain_values, grad_out):
    weighted = grad_out * gain_values
    gain_grad = jnp.sum(grad_out * values * row_scale, axis=0)
    inner_mean = jnp.mean(weighted * values, axis=-1, keepdims=True)
    return (
        row_scale * weighted - values * row_scale * row_scale * row_scale * inner_mean,
        gain_grad,
    )


def inner_rows(left, right):
    return lax.dot_general(
        left, right, (((0,), (0,)), ((), ())), preferred_element_type=jnp.float32
    )


def dot_last(left, right):
    return lax.dot_general(
        left, right, (((1,), (1,)), ((), ())), preferred_element_type=jnp.float32
    )


def context_size():
    return lax.axis_size("far") * lax.axis_size("core")


def ring_pairs(count):
    order = [i for i in range(count) if i % 2 == 0] + [i for i in reversed(range(count)) if i % 2 == 1]
    right = [(order[i], order[(i + 1) % count]) for i in range(count)]
    left = [(order[i], order[(i - 1) % count]) for i in range(count)]
    return right, left


def ring_place(index, count):
    return jnp.where(index % 2 == 0, index // 2, count - 1 - index // 2)


def ring_index(place, count):
    place = (place + 2 * count) % count
    return jnp.where(place < count // 2, 2 * place, 2 * (count - 1 - place) + 1)


class RingGather:
    def __init__(self, block):
        self.count = lax.axis_size("experts")
        self.right, self.left = ring_pairs(self.count)
        self.half = block.shape[0] // 2
        self.block = block
        self.ahead = [block]
        self.behind = [block]
        self.far = None

    def step(self):
        if len(self.ahead) < self.count // 2:
            self.behind.append(lax.ppermute(self.behind[-1], "experts", self.right))
            self.ahead.append(lax.ppermute(self.ahead[-1], "experts", self.left))
        else:
            self.far = [
                lax.ppermute(self.behind[-1][: self.half], "experts", self.right),
                lax.ppermute(self.ahead[-1][self.half :], "experts", self.left),
            ]

    def latest(self):
        return self.far if self.far else [self.behind[-1], self.ahead[-1]]

    def replace(self, values):
        if self.far:
            self.far = list(values)
        else:
            self.behind[-1], self.ahead[-1] = values

    def pieces(self):
        return self.ahead + self.far + self.behind[:0:-1]


class RingScatter:
    def __init__(self, whole):
        self.count = lax.axis_size("experts")
        self.right, self.left = ring_pairs(self.count)
        self.whole = whole
        self.rows = whole.shape[0] // self.count
        self.half = self.rows // 2
        self.left_steps = self.count // 2
        self.first = None
        self.second = None

    def own(self, step):
        start = step % self.count * self.rows
        return self.whole[start : start + self.rows].astype(jnp.float32)

    def arrived(self):
        first = self.first.astype(jnp.float32)
        second = self.second.astype(jnp.float32)
        if self.left_steps == self.count // 2 - 1:
            blank = jnp.zeros((self.half, self.whole.shape[1]), jnp.float32)
            first = jnp.concatenate([first, blank], axis=0)
            second = jnp.concatenate([blank, second], axis=0)
        return first, second

    def step(self):
        if self.first is None:
            far = self.own(self.left_steps)
            first, second = far[: self.half], far[self.half :]
        else:
            first, second = self.arrived()
            first = first + self.own(self.left_steps)
            second = second + self.own(-self.left_steps)
        self.sent = (first.astype(jnp.bfloat16), second.astype(jnp.bfloat16))
        self.first = lax.ppermute(self.sent[0], "experts", self.right)
        self.second = lax.ppermute(self.sent[1], "experts", self.left)
        self.left_steps -= 1

    def latest(self):
        return [self.first, self.second]

    def replace(self, values):
        self.first, self.second = values

    def total(self):
        first, second = self.arrived()
        return first + second + self.own(0)


def meet(rings, *values):
    held, values = lax.optimization_barrier(([ring.latest() for ring in rings], values))
    for ring, value in zip(rings, held):
        ring.replace(value)
    return values


def ring_order(values):
    count = lax.axis_size("experts")
    place = ring_place(lax.axis_index("experts"), count)
    return jnp.concatenate(
        [
            lax.dynamic_slice_in_dim(values, ring_index(place + step, count), 1, 0)
            for step in range(count)
        ],
        axis=0,
    )


def flip_pairs(count, bit):
    return [(i, i ^ bit) for i in range(count)]


def flip_double(whole, axis):
    bit = whole.shape[0]
    received = lax.ppermute(whole, axis, flip_pairs(lax.axis_size(axis), bit))
    return jnp.where(
        (lax.axis_index(axis) // bit) % 2 == 0,
        jnp.concatenate([whole, received], axis=0),
        jnp.concatenate([received, whole], axis=0),
    )


def flip_gather(block, axis):
    whole = block[None]
    while whole.shape[0] < lax.axis_size(axis):
        whole = flip_double(whole, axis)
    return whole


def flip_half(values, axis, bit, dimension):
    shape = values.shape
    pairs = values.reshape(shape[:dimension] + (shape[dimension] // 2, 2) + shape[dimension + 1 :])
    mine = (lax.axis_index(axis) // bit) % 2
    sent = lax.dynamic_index_in_dim(pairs, 1 - mine, dimension + 1, keepdims=False)
    kept = lax.dynamic_index_in_dim(pairs, mine, dimension + 1, keepdims=False)
    return kept + lax.ppermute(sent, axis, flip_pairs(lax.axis_size(axis), bit))


def context_double(whole, bit):
    received = lax.ppermute(whole, CONTEXT, flip_pairs(context_size(), bit))
    low = (lax.axis_index(CONTEXT) // bit) % 2 == 0
    return jnp.stack(
        [jnp.where(low, whole, received), jnp.where(low, received, whole)], axis=1
    ).reshape((2 * whole.shape[0],) + whole.shape[1:])


def far_gather(block):
    whole = block[None]
    bit = context_size() // 2
    while bit > 1:
        whole = context_double(whole, bit)
        bit //= 2
    return whole


def core_gather(whole):
    return context_double(whole, 1).reshape(-1, whole.shape[-1])


def context_gather(block):
    return core_gather(far_gather(block))


def after(done, *values):
    values, _ = lax.optimization_barrier((values, done))
    return values[0] if len(values) == 1 else values


def core_parts(piece_of):
    count = context_size()
    index = lax.axis_index(CONTEXT)
    return {place: piece_of(index ^ (place + 1)) for place in range(count - 2, -1, -2)}


def core_exchange(parts):
    pairs = flip_pairs(context_size(), 1)
    return {
        place: lax.ppermute(part.astype(jnp.bfloat16), CONTEXT, pairs)
        for place, part in parts.items()
    }


def core_sums(piece_of, received):
    index = lax.axis_index(CONTEXT)
    return {
        place // 2: piece_of(index ^ place, part) for place, part in received.items()
    }


def far_exchange(pieces):
    count = context_size()
    bit = 2
    while 2 * bit < count:
        merged = {}
        for place in sorted(pieces, reverse=True):
            if place % 2 == 0:
                received = lax.ppermute(
                    pieces[place + 1].astype(jnp.bfloat16), CONTEXT, flip_pairs(count, bit)
                )
                merged[place // 2] = pieces[place] + received.astype(jnp.float32)
        pieces = merged
        bit *= 2
    last = lax.ppermute(pieces[1].astype(jnp.bfloat16), CONTEXT, flip_pairs(count, bit))
    return pieces[0], last


def both_halves(pair):
    return pair[0] + pair[1].astype(jnp.float32)


def core_swap(values):
    return lax.ppermute(values, "core", [(0, 1), (1, 0)])


def chips_sum(values):
    return lax.psum_scatter(values, "far", scatter_dimension=0, tiled=True)[0]


def chips_exchange(values):
    chip = lax.axis_index("far")
    pieces = {
        place: lax.dynamic_index_in_dim(values, chip ^ place, 0, keepdims=False)
        for place in range(values.shape[0])
    }
    return far_exchange(pieces)


def block_sums(values, received):
    def piece_of(target, part):
        return lax.dynamic_index_in_dim(values, target, 0, keepdims=False) + part.astype(jnp.float32)

    return core_sums(piece_of, received)


def block_parts(values):
    return core_parts(lambda target: lax.dynamic_index_in_dim(values, target, 0, keepdims=False))


def to_experts(stacked):
    return lax.all_to_all(stacked, "experts", split_axis=0, concat_axis=0, tiled=True)


def kernel_options(mebibytes=60):
    return dict(
        compiler_params=pltpu.CompilerParams(vmem_limit_bytes=mebibytes * 1024 * 1024),
        cost_estimate=pl.CostEstimate(flops=1024, bytes_accessed=1024, transcendentals=0),
    )


def in_vmem(count):
    return [pl.BlockSpec(memory_space=pltpu.VMEM)] * count


def in_smem(count):
    return [pl.BlockSpec(memory_space=pltpu.SMEM)] * count


def plain_dot(left, right):
    return jnp.dot(left, right, preferred_element_type=jnp.float32)


def last_dims(left, right):
    return lax.dot_general(
        left, right, (((1,), (1,)), ((), ())), preferred_element_type=jnp.float32
    )


def first_dims(left, right):
    return lax.dot_general(
        left, right, (((0,), (0,)), ((), ())), preferred_element_type=jnp.float32
    )


def project_kernel(piece_count, *refs):
    pieces = refs[:piece_count]
    weight_ref, cosine_ref, sine_ref, normed_ref, query_ref, key_value_ref = refs[piece_count:]
    start = 0
    for piece in pieces:
        rows = piece.shape[0]
        values = piece[...].astype(jnp.float32)
        scale = lax.rsqrt(jnp.mean(values * values, axis=-1, keepdims=True) + EPSILON)
        normed_ref[start : start + rows, :] = (values * scale).astype(jnp.bfloat16)
        start += rows
    query_width = query_ref.shape[1]
    heads = plain_dot(normed_ref[...], weight_ref[...])

    def rotated(offset):
        head = heads[:, offset : offset + HEAD_DIM]
        turned = pltpu.roll(head, HEAD_DIM // 2, 1)
        return (head * cosine_ref[...] + turned * sine_ref[...]).astype(jnp.bfloat16)

    for offset in range(0, query_width, HEAD_DIM):
        query_ref[:, offset : offset + HEAD_DIM] = rotated(offset)
    key_value_ref[:, :HEAD_DIM] = rotated(query_width)
    key_value_ref[:, HEAD_DIM:] = heads[:, query_width + HEAD_DIM :].astype(jnp.bfloat16)


def project(pieces, weight, cosine, sine, query_width):
    rows = sum(piece.shape[0] for piece in pieces)
    width = pieces[0].shape[1]
    return pl.pallas_call(
        functools.partial(project_kernel, len(pieces)),
        out_shape=(
            jax.ShapeDtypeStruct((rows, width), jnp.bfloat16),
            jax.ShapeDtypeStruct((rows, query_width), jnp.bfloat16),
            jax.ShapeDtypeStruct((rows, weight.shape[1] - query_width), jnp.bfloat16),
        ),
        in_specs=in_vmem(len(pieces) + 3),
        out_specs=tuple(in_vmem(3)),
        **kernel_options(),
    )(*pieces, weight, cosine, sine)


def stack_heads(values):
    heads = values.shape[1] // HEAD_DIM
    return jnp.concatenate(
        [values[:, i * HEAD_DIM : (i + 1) * HEAD_DIM] for i in range(heads)], axis=0
    )


def spread_heads(values, heads):
    rows = values.shape[0] // heads
    return jnp.concatenate([values[i * rows : (i + 1) * rows] for i in range(heads)], axis=1)


def stack_lanes(values):
    return jnp.concatenate([values[i : i + 1] for i in range(values.shape[0])], axis=1)


def visible_keys(shape, key_start, query_start, query_tile):
    key_pos = key_start + lax.broadcasted_iota(jnp.int32, shape, 0)
    query_pos = query_start + lax.rem(lax.broadcasted_iota(jnp.int32, shape, 1), query_tile)
    return query_pos >= key_pos


def ring_slices(order_ref, rows, first, count):
    spread = order_ref.shape[0]
    length = rows // spread
    found = []
    for i in range(count):
        number = first + i
        base = lax.div(number, spread) * rows
        place = order_ref[lax.rem(number, spread)] * length
        found.append(pl.ds(pl.multiple_of(base + place, length), length))
    return found


def forward_kernel(
    query_tile, key_tile, block_ref, order_ref, query_ref, key_value_ref, out_ref, low_ref, total_ref
):
    rows = query_ref.shape[0]
    length = rows // order_ref.shape[0]
    heads = query_ref.shape[1] // HEAD_DIM
    wide = heads * query_tile
    scale = HEAD_DIM ** (-0.5) * math.log2(math.e)

    @pl.loop(0, rows // query_tile)
    def _(index):
        offset = pl.multiple_of(index * query_tile, query_tile)
        places = ring_slices(order_ref, rows, index * (query_tile // length), query_tile // length)
        queries = stack_heads(jnp.concatenate([query_ref[place, :] for place in places], axis=0))
        start = block_ref[0] * rows + offset

        def step(tile, state, masked):
            top, total, summed = state
            here = ring_slices(order_ref, rows, tile * (key_tile // length), key_tile // length)
            keys = jnp.concatenate([key_value_ref[place, :HEAD_DIM] for place in here], axis=0)
            values = jnp.concatenate([key_value_ref[place, HEAD_DIM:] for place in here], axis=0)
            scores = last_dims(keys, queries) * scale
            if masked:
                seen = visible_keys(scores.shape, tile * key_tile, start, query_tile)
                scores = jnp.where(seen, scores, NEG_LARGE)
            new_top = jnp.maximum(top, jnp.max(scores, axis=0, keepdims=True))
            weights = jnp.exp2(scores - new_top)
            rescale = jnp.exp2(top - new_top)
            total = total * rescale + jnp.sum(weights, axis=0, keepdims=True)
            summed = summed * rescale + first_dims(values, weights.astype(jnp.bfloat16))
            return new_top, total, summed

        state = (
            jnp.full((1, wide), NEG_LARGE, jnp.float32),
            jnp.zeros((1, wide), jnp.float32),
            jnp.zeros((HEAD_DIM, wide), jnp.float32),
        )
        full = lax.div(start, key_tile)
        state = lax.fori_loop(0, full, lambda tile, state: step(tile, state, False), state)
        top, total, summed = step(full, state, True)
        result = spread_heads((summed / total).T, heads)
        out_ref[pl.ds(offset, query_tile), :] = result
        low_ref[pl.ds(offset, query_tile), :] = result.astype(jnp.bfloat16)
        log_total = top + jnp.log2(total)
        for i in range(heads):
            total_ref[i : i + 1, pl.ds(offset, query_tile)] = log_total[
                :, i * query_tile : (i + 1) * query_tile
            ]


def backward_kernel(
    query_tile,
    key_tile,
    block_ref,
    order_ref,
    query_ref,
    key_value_ref,
    out_ref,
    grad_ref,
    total_ref,
    cosine_ref,
    sine_ref,
    query_grad_ref,
    key_value_grad_ref,
):
    rows = query_ref.shape[0]
    length = rows // order_ref.shape[0]
    heads = query_ref.shape[1] // HEAD_DIM
    wide = heads * query_tile
    score_scale = HEAD_DIM ** (-0.5)
    scale = score_scale * math.log2(math.e)

    @pl.loop(0, key_value_ref.shape[0] // key_tile)
    def _(tile):
        key_start = pl.multiple_of(tile * key_tile, key_tile)
        key_value_grad_ref[pl.ds(key_start, key_tile), :] = jnp.zeros(
            (key_tile, 2 * HEAD_DIM), jnp.float32
        )

    @pl.loop(0, rows // query_tile)
    def _(index):
        offset = pl.multiple_of(index * query_tile, query_tile)
        places = ring_slices(order_ref, rows, index * (query_tile // length), query_tile // length)
        queries = stack_heads(jnp.concatenate([query_ref[place, :] for place in places], axis=0))
        grads = stack_heads(grad_ref[pl.ds(offset, query_tile), :])
        outs = stack_heads(out_ref[pl.ds(offset, query_tile), :])
        delta = jnp.sum((grads.astype(jnp.float32) * outs).T, axis=0, keepdims=True)
        log_total = stack_lanes(total_ref[:, pl.ds(offset, query_tile)])
        start = block_ref[0] * rows + offset

        def step(tile, query_grad, masked):
            here = ring_slices(order_ref, rows, tile * (key_tile // length), key_tile // length)
            keys = jnp.concatenate([key_value_ref[place, :HEAD_DIM] for place in here], axis=0)
            values = jnp.concatenate([key_value_ref[place, HEAD_DIM:] for place in here], axis=0)
            weights = jnp.exp2(last_dims(keys, queries) * scale - log_total)
            if masked:
                seen = visible_keys(weights.shape, tile * key_tile, start, query_tile)
                weights = jnp.where(seen, weights, 0.0)
            value_part = plain_dot(weights.astype(jnp.bfloat16), grads)
            score_grad = (weights * (last_dims(values, grads) - delta)).astype(jnp.bfloat16)
            key_part = plain_dot(score_grad, queries) * score_scale
            part = jnp.concatenate([key_part, value_part], axis=1)
            for i, place in enumerate(here):
                key_value_grad_ref[place, :] += part[i * length : (i + 1) * length]
            return query_grad + first_dims(score_grad, keys)

        full = lax.div(start, key_tile)
        query_grad = lax.fori_loop(
            0,
            full,
            lambda tile, state: step(tile, state, False),
            jnp.zeros((wide, HEAD_DIM), jnp.float32),
        )
        query_grad = step(full, query_grad, True) * score_scale
        for i, place in enumerate(places):
            cosine = cosine_ref[place, :]
            sine = sine_ref[place, :]
            for head in range(heads):
                begin = head * query_tile + i * length
                part = query_grad[begin : begin + length]
                turned = part * cosine - pltpu.roll(part, HEAD_DIM // 2, 1) * sine
                query_grad_ref[place, head * HEAD_DIM : (head + 1) * HEAD_DIM] = turned.astype(
                    jnp.bfloat16
                )


def attention_forward(block_index, order, queries, keys):
    rows, wide = queries.shape
    return pl.pallas_call(
        functools.partial(forward_kernel, math.gcd(rows, 1024), math.gcd(rows, 1024)),
        out_shape=(
            jax.ShapeDtypeStruct((rows, wide), jnp.float32),
            jax.ShapeDtypeStruct((rows, wide), jnp.bfloat16),
            jax.ShapeDtypeStruct((wide // HEAD_DIM, rows), jnp.float32),
        ),
        in_specs=in_smem(2) + in_vmem(2),
        out_specs=tuple(in_vmem(3)),
        **kernel_options(50),
    )(block_index.reshape(1), order, queries, keys)


def attention_backward(block_index, order, queries, keys, outs, grads, log_total, cosine, sine):
    rows, wide = queries.shape
    return pl.pallas_call(
        functools.partial(backward_kernel, math.gcd(rows, 512), math.gcd(rows, 512)),
        out_shape=(
            jax.ShapeDtypeStruct((rows, wide), jnp.bfloat16),
            jax.ShapeDtypeStruct((keys.shape[0], 2 * HEAD_DIM), jnp.float32),
        ),
        in_specs=in_smem(2) + in_vmem(7),
        out_specs=tuple(in_vmem(2)),
        **kernel_options(44),
    )(block_index.reshape(1), order, queries, keys, outs, grads, log_total, cosine, sine)


def dispatch_kernel(piece_count, experts, *refs):
    pieces = refs[:piece_count]
    chosen_ref, whole_ref, rows_ref = refs[piece_count:]
    start = 0
    for piece in pieces:
        whole_ref[start : start + piece.shape[0], :] = piece[...]
        start += piece.shape[0]
    length = chosen_ref.shape[2]
    capacity = chosen_ref.shape[1] // experts
    for block in range(chosen_ref.shape[0]):
        picked = plain_dot(chosen_ref[block], whole_ref[block * length : (block + 1) * length, :])
        picked = picked.astype(jnp.bfloat16)
        for expert in range(experts):
            rows_ref[expert, block * capacity : (block + 1) * capacity, :] = picked[
                expert * capacity : (expert + 1) * capacity
            ]


def dispatch(pieces, chosen, experts):
    rows = sum(piece.shape[0] for piece in pieces)
    width = pieces[0].shape[1]
    blocks, slots, _ = chosen.shape
    return pl.pallas_call(
        functools.partial(dispatch_kernel, len(pieces), experts),
        out_shape=(
            jax.ShapeDtypeStruct((rows, width), jnp.bfloat16),
            jax.ShapeDtypeStruct((experts, blocks * (slots // experts), width), jnp.bfloat16),
        ),
        in_specs=in_vmem(len(pieces) + 1),
        out_specs=tuple(in_vmem(2)),
        **kernel_options(),
    )(*pieces, chosen)


def hidden_tiles(width, tile):
    return [slice(start, min(start + tile, width)) for start in range(0, width, tile)]


def slopes(pre_gate, pre_up):
    sigmoid = 1.0 / (1.0 + jnp.exp(-pre_gate))
    silu = pre_gate * sigmoid
    return silu * pre_up, pre_up * sigmoid * (1.0 + pre_gate * (1.0 - sigmoid)), silu


def expert_forward_kernel(rows_ref, weight_gate_ref, weight_up_ref, act_ref, by_gate_ref, by_up_ref):
    for here in hidden_tiles(act_ref.shape[2], 256):
        pre_gate = plain_dot(rows_ref[0], weight_gate_ref[0, :, here])
        pre_up = plain_dot(rows_ref[0], weight_up_ref[0, :, here])
        act, by_gate, by_up = slopes(pre_gate, pre_up)
        act_ref[0, :, here] = act.astype(jnp.bfloat16)
        by_gate_ref[0, :, here] = by_gate.astype(jnp.bfloat16)
        by_up_ref[0, :, here] = by_up.astype(jnp.bfloat16)


def one_expert(*shape):
    return pl.BlockSpec((1,) + shape, lambda expert: (expert, 0, 0))


def expert_forward(rows, weight_gate, weight_up):
    experts, count, width = rows.shape
    hidden = weight_gate.shape[2]
    return pl.pallas_call(
        expert_forward_kernel,
        grid=(experts,),
        out_shape=(jax.ShapeDtypeStruct((experts, count, hidden), jnp.bfloat16),) * 3,
        in_specs=[one_expert(count, width), one_expert(width, hidden), one_expert(width, hidden)],
        out_specs=(one_expert(count, hidden),) * 3,
        **kernel_options(),
    )(rows, weight_gate, weight_up)


def expert_backward_kernel(
    first_ref,
    grad_ref,
    gate_ref,
    act_ref,
    by_gate_ref,
    by_up_ref,
    weight_gate_ref,
    weight_up_ref,
    weight_down_ref,
    gate_grad_ref,
    up_grad_ref,
    row_grad_ref,
):
    width = weight_gate_ref.shape[1]
    count = grad_ref.shape[1]
    score = jnp.zeros((count, 1), jnp.float32)
    for here in hidden_tiles(act_ref.shape[2], 256):
        act_grad = last_dims(grad_ref[0], weight_down_ref[0, here, :])
        score = score + jnp.sum(
            act_ref[0, :, here].astype(jnp.float32) * act_grad, axis=1, keepdims=True
        )
        act_grad = act_grad * gate_ref[0]
        gate_grad_ref[0, :, here] = (act_grad * by_gate_ref[0, :, here].astype(jnp.float32)).astype(
            jnp.bfloat16
        )
        up_grad_ref[0, :, here] = (act_grad * by_up_ref[0, :, here].astype(jnp.float32)).astype(
            jnp.bfloat16
        )

    for here in hidden_tiles(width, 512):
        row_grad_ref[0, :, here] = (
            last_dims(gate_grad_ref[0], weight_gate_ref[0, here, :])
            + last_dims(up_grad_ref[0], weight_up_ref[0, here, :])
        ).astype(jnp.bfloat16)

    lane = lax.broadcasted_iota(jnp.int32, (count, HEAD_DIM), 1)
    own = first_ref[0] + pl.program_id(0)
    row_grad_ref[0, :, width:] = jnp.where(lane == own, score, 0.0).astype(jnp.bfloat16)


def expert_backward(first_expert, grads, gates, act, by_gate, by_up, weight_gate, weight_up, weight_down):
    experts, count, width = grads.shape
    hidden = act.shape[2]
    low = one_expert(count, hidden)
    return pl.pallas_call(
        expert_backward_kernel,
        grid=(experts,),
        out_shape=(
            jax.ShapeDtypeStruct((experts, count, hidden), jnp.bfloat16),
            jax.ShapeDtypeStruct((experts, count, hidden), jnp.bfloat16),
            jax.ShapeDtypeStruct((experts, count, width + HEAD_DIM), jnp.bfloat16),
        ),
        in_specs=in_smem(1)
        + [
            one_expert(count, width),
            one_expert(count, 1),
            low,
            low,
            low,
            one_expert(width, hidden),
            one_expert(width, hidden),
            one_expert(hidden, width),
        ],
        out_specs=(low, low, one_expert(count, width + HEAD_DIM)),
        **kernel_options(),
    )(first_expert.reshape(1), grads, gates, act, by_gate, by_up, weight_gate, weight_up, weight_down)


def result_kernel(act_ref, gate_ref, weight_ref, out_ref):
    for here in hidden_tiles(out_ref.shape[2], 512):
        result = plain_dot(act_ref[0], weight_ref[0, :, here]).astype(jnp.bfloat16)
        out_ref[0, :, here] = (result.astype(jnp.float32) * gate_ref[0]).astype(jnp.bfloat16)


def expert_results(act, gates, weight_down):
    experts, count, hidden = act.shape
    width = weight_down.shape[2]

    def one(*shape):
        return pl.BlockSpec((1,) + shape, lambda expert: (expert, 0, 0))

    return pl.pallas_call(
        result_kernel,
        grid=(experts,),
        out_shape=jax.ShapeDtypeStruct((experts, count, width), jnp.bfloat16),
        in_specs=[one(count, hidden), one(count, 1), one(hidden, width)],
        out_specs=one(count, width),
        **kernel_options(),
    )(act, gates, weight_down)


def combine_kernel(turned, chosen_ref, values_ref, left_ref, right_ref, out_ref):
    width = right_ref.shape[0] if turned else right_ref.shape[1]
    experts = values_ref.shape[0]
    length = chosen_ref.shape[1]
    capacity = chosen_ref.shape[2] // experts
    blocks = chosen_ref.shape[0]

    def slots(block, here):
        values = [
            values_ref[expert, block * capacity : (block + 1) * capacity, here]
            for expert in range(experts)
        ]
        return plain_dot(chosen_ref[block], jnp.concatenate(values, axis=0))

    for here in hidden_tiles(width, 512):
        shared = (
            last_dims(left_ref[...], right_ref[here, :])
            if turned
            else plain_dot(left_ref[...], right_ref[:, here])
        )
        for block in range(blocks):
            rows = slice(block * length, (block + 1) * length)
            out_ref[rows, here] = (shared[rows] + slots(block, here)).astype(jnp.bfloat16)

    if out_ref.shape[1] > width:
        for block in range(blocks):
            out_ref[block * length : (block + 1) * length, width:] = slots(
                block, slice(width, out_ref.shape[1])
            ).astype(jnp.bfloat16)


def combine(chosen, values, left, right, turned):
    blocks, length, slots = chosen.shape
    experts, _, wide = values.shape
    capacity = slots // experts
    some = math.gcd(blocks, 2)
    return pl.pallas_call(
        functools.partial(combine_kernel, turned),
        grid=(blocks // some,),
        out_shape=jax.ShapeDtypeStruct((blocks * length, wide), jnp.bfloat16),
        in_specs=[
            pl.BlockSpec((some, length, slots), lambda i: (i, 0, 0)),
            pl.BlockSpec((experts, some * capacity, wide), lambda i: (0, i, 0)),
            pl.BlockSpec((some * length, left.shape[1]), lambda i: (i, 0)),
            pl.BlockSpec(right.shape, lambda i: (0, 0)),
        ],
        out_specs=pl.BlockSpec((some * length, wide), lambda i: (i, 0)),
        **kernel_options(32),
    )(chosen, values, left, right)


def shared_kernel(normed_ref, grad_ref, weight_ref, down_ref, act_ref, both_ref):
    hidden = act_ref.shape[1]
    pre_gate = plain_dot(normed_ref[...], weight_ref[:, :hidden])
    pre_up = plain_dot(normed_ref[...], weight_ref[:, hidden:])
    act_grad = last_dims(grad_ref[...], down_ref[...])
    act, by_gate, by_up = slopes(pre_gate, pre_up)
    act_ref[...] = act.astype(jnp.bfloat16)
    both_ref[:, :hidden] = (act_grad * by_gate).astype(jnp.bfloat16)
    both_ref[:, hidden:] = (act_grad * by_up).astype(jnp.bfloat16)


def shared_pass(normed, grads, weight, down):
    rows, width = normed.shape
    hidden = down.shape[0]
    some = math.gcd(rows, 256)

    def part(columns):
        return pl.BlockSpec((some, columns), lambda i: (i, 0))

    return pl.pallas_call(
        shared_kernel,
        grid=(rows // some,),
        out_shape=(
            jax.ShapeDtypeStruct((rows, hidden), jnp.bfloat16),
            jax.ShapeDtypeStruct((rows, 2 * hidden), jnp.bfloat16),
        ),
        in_specs=[
            part(width),
            part(width),
            pl.BlockSpec(weight.shape, lambda i: (0, 0)),
            pl.BlockSpec(down.shape, lambda i: (0, 0)),
        ],
        out_specs=(part(hidden), part(2 * hidden)),
        **kernel_options(32),
    )(normed, grads, weight, down)


def part_kernel(scaled, added, core_ref, left_ref, right_ref, *refs):
    right = right_ref[0]
    if scaled:
        right = (right.astype(jnp.float32) * refs[0][0]).astype(jnp.bfloat16)
    total = first_dims(left_ref[0], right)
    if added:
        total = total + refs[-2][0, 0].astype(jnp.float32)
    refs[-1][0, 0] = total.astype(jnp.bfloat16)


def weight_parts(core, left, right, cut_left, gates=None, received=None, slices=1, number=0, wide=False):
    chips = lax.axis_size("far")
    parts = 2 * chips * slices
    experts, count, left_width = left.shape
    right_width = right.shape[2]
    left_width, right_width = (
        (left_width // parts, right_width) if cut_left else (left_width, right_width // parts)
    )

    def spec(columns, cut):
        if cut:
            return pl.BlockSpec(
                (1, count, columns), lambda f, e, c: (e, 0, (2 * f + c[0]) * slices + number)
            )
        return pl.BlockSpec((1, count, columns), lambda f, e, c: (e, 0, 0))

    whole = pl.BlockSpec((1, 1, left_width, right_width), lambda f, e, c: (f, e, 0, 0))
    operands = [left, right]
    specs = [spec(left_width, cut_left), spec(right_width, not cut_left)]
    if gates is not None:
        operands.append(gates)
        specs.append(pl.BlockSpec((1, count, 1), lambda f, e, c: (e, 0, 0)))
    if received is not None:
        operands.append(received)
        place = (lambda f, e, c: (f, e, number, 0)) if cut_left else (lambda f, e, c: (f, e, 0, number))
        specs.append(pl.BlockSpec((1, 1, left_width, right_width), place))
    return pl.pallas_call(
        functools.partial(part_kernel, gates is not None, received is not None),
        grid_spec=pltpu.PrefetchScalarGridSpec(
            num_scalar_prefetch=1, grid=(chips, experts), in_specs=specs, out_specs=whole
        ),
        out_shape=jax.ShapeDtypeStruct((chips, experts, left_width, right_width), jnp.bfloat16),
        **kernel_options(60 if wide else 24),
    )(core.reshape(1), *operands)


def output_weight_kernel(piece_count, index_ref, core_ref, grad_ref, *refs):
    pieces = refs[:piece_count]
    keep_ref, send_ref = refs[piece_count:]
    wide = pieces[0].shape[1]
    half = piece_count // 2
    length = keep_ref.shape[1]
    some = min(wide, length)

    def part(piece, start):
        return first_dims(piece[...], grad_ref[start : start + piece.shape[0], :])

    def place(total, first):
        target = lax.div(first, length)
        chip = lax.div(target, 2)
        offset = pl.multiple_of(lax.rem(first, length), some)
        mine = lax.rem(target, 2) == core_ref[0]

        @pl.when(mine)
        def _():
            keep_ref[chip, pl.ds(offset, some), :] = total

        @pl.when(jnp.logical_not(mine))
        def _():
            send_ref[chip, pl.ds(offset, some), :] = total

    for block in range(index_ref.shape[0]):
        if block < half:
            total = part(pieces[block], 0)
        elif block == half:
            total = part(pieces[half], 0) + part(pieces[half + 1], pieces[half].shape[0])
        else:
            total = part(pieces[block + 1], 0)
        total = total.astype(jnp.bfloat16)
        for start in range(0, wide, some):
            place(total[start : start + some], index_ref[block] * wide + start)


def output_weight(index, core, grads, pieces):
    chips = lax.axis_size("far")
    length = index.shape[0] * pieces[0].shape[1] // (2 * chips)
    return pl.pallas_call(
        functools.partial(output_weight_kernel, len(pieces)),
        out_shape=(jax.ShapeDtypeStruct((chips, length, grads.shape[1]), jnp.bfloat16),) * 2,
        in_specs=in_smem(2) + in_vmem(len(pieces) + 1),
        out_specs=tuple(in_vmem(2)),
        **kernel_options(),
    )(index, core.reshape(1), grads, *pieces)


def hidden_send_kernel(own, chips, gate_ref, up_ref, out_ref):
    spread = out_ref.shape[0]
    wide = out_ref.shape[2] // 2
    piece = own // chips
    blank = [jnp.zeros((gate_ref.shape[0], wide - own), jnp.float32)] if wide > own else []
    for start, weight_ref in ((0, gate_ref), (wide, up_ref)):
        weight = weight_ref[...].astype(jnp.float32)
        for device in range(spread):
            columns = [
                weight[:, (chip * spread + device) * piece : (chip * spread + device + 1) * piece]
                for chip in range(chips)
            ]
            out_ref[device, :, start : start + wide] = jnp.concatenate(
                columns + blank, axis=1
            ).astype(jnp.bfloat16)


def hidden_send(gate, up, own, wide, chips, spread):
    return pl.pallas_call(
        functools.partial(hidden_send_kernel, own, chips),
        out_shape=jax.ShapeDtypeStruct((spread, gate.shape[0], 2 * wide), jnp.bfloat16),
        in_specs=in_vmem(2),
        out_specs=pl.BlockSpec(memory_space=pltpu.VMEM),
        **kernel_options(),
    )(gate, up)


def hidden_home_kernel(own, chips, back_ref, gate_ref, up_ref):
    spread = back_ref.shape[0]
    wide = back_ref.shape[2] // 2
    piece = own // chips
    for start, out_ref in ((0, gate_ref), (wide, up_ref)):
        values = [
            back_ref[device, :, start : start + wide].astype(jnp.float32)
            for device in range(spread)
        ]
        out_ref[...] = jnp.concatenate(
            [
                values[device][:, chip * piece : (chip + 1) * piece]
                for chip in range(chips)
                for device in range(spread)
            ],
            axis=1,
        )


def hidden_home(back, own, chips):
    spread, rows, _ = back.shape
    return pl.pallas_call(
        functools.partial(hidden_home_kernel, own, chips),
        out_shape=(jax.ShapeDtypeStruct((rows, own * spread), jnp.float32),) * 2,
        in_specs=in_vmem(1),
        out_specs=tuple(in_vmem(2)),
        **kernel_options(12),
    )(back)


def dense_home_kernel(back_ref, weight_ref, gain_ref, qkv_ref, out_ref, small_ref, gain_grad_ref):
    spread, _, wide = back_ref.shape
    own = QUERY_HEADS * HEAD_DIM // spread
    repeat = spread // KEY_VALUE_HEADS
    out_wide = out_ref.shape[1] // spread
    score = jnp.zeros(gain_ref.shape, jnp.float32)

    def keep(score, start, values):
        columns = slice(start, start + values.shape[1])
        qkv_ref[:, columns] = values * gain_ref[...]
        weight = weight_ref[:, columns].astype(jnp.float32)
        return score + jnp.sum(weight * values, axis=1, keepdims=True)

    small = jnp.zeros(small_ref.shape, jnp.float32)
    for device in range(spread):
        score = keep(score, device * own, back_ref[device, :, :own].astype(jnp.float32))
        start = own + 2 * HEAD_DIM
        out_ref[:, device * out_wide : (device + 1) * out_wide] = back_ref[
            device, :, start : start + out_wide
        ].astype(jnp.float32)
        small = small + back_ref[device, :, start + out_wide :].astype(jnp.float32)
    for part in range(2):
        for head in range(KEY_VALUE_HEADS):
            start = own + part * HEAD_DIM
            values = sum(
                back_ref[head * repeat + i, :, start : start + HEAD_DIM].astype(jnp.float32)
                for i in range(repeat)
            )
            place = QUERY_HEADS * HEAD_DIM + (part * KEY_VALUE_HEADS + head) * HEAD_DIM
            score = keep(score, place, values)
    small_ref[...] = small
    gain_grad_ref[...] = score


def dense_home(back, weight, gain, width):
    rows, qkv_width = weight.shape
    return pl.pallas_call(
        dense_home_kernel,
        out_shape=(
            jax.ShapeDtypeStruct((rows, qkv_width), jnp.float32),
            jax.ShapeDtypeStruct((rows, width), jnp.float32),
            jax.ShapeDtypeStruct((rows, HEAD_DIM), jnp.float32),
            jax.ShapeDtypeStruct((rows, 1), jnp.float32),
        ),
        in_specs=in_vmem(3),
        out_specs=tuple(in_vmem(4)),
        **kernel_options(12),
    )(back, weight, gain)


def product_kernel(left_ref, right_ref, out_ref):
    for here in hidden_tiles(out_ref.shape[0], 512):
        out_ref[here, :] = first_dims(left_ref[:, here], right_ref[...]).astype(jnp.bfloat16)


def row_product(left, right, columns):
    return pl.pallas_call(
        product_kernel,
        out_shape=jax.ShapeDtypeStruct((columns, right.shape[1]), jnp.bfloat16),
        in_specs=in_vmem(2),
        out_specs=pl.BlockSpec(memory_space=pltpu.VMEM),
        **kernel_options(24),
    )(left, right)


def widen_kernel(*refs):
    out_ref = refs[-1]
    start = 0
    for part_ref in refs[:-1]:
        rows = part_ref.shape[1]
        out_ref[0, start : start + rows, :] = part_ref[0].astype(jnp.float32)
        start += rows


def widen(*parts):
    experts, _, columns = parts[0].shape
    rows = sum(part.shape[1] for part in parts)
    return pl.pallas_call(
        widen_kernel,
        grid=(experts,),
        out_shape=jax.ShapeDtypeStruct((experts, rows, columns), jnp.float32),
        in_specs=[one_expert(part.shape[1], columns) for part in parts],
        out_specs=one_expert(rows, columns),
        **kernel_options(28),
    )(*parts)


def project_back_kernel(
    query_ref, own_ref, last_ref, cosine_ref, sine_ref, weight_ref, projected_ref, out_ref
):
    wide = query_ref.shape[1]
    projected_ref[:, :wide] = query_ref[...]
    total = own_ref[...] + last_ref[...].astype(jnp.float32)
    keys = total[:, :HEAD_DIM]
    turned = keys * cosine_ref[...] - pltpu.roll(keys, HEAD_DIM // 2, 1) * sine_ref[...]
    projected_ref[:, wide : wide + HEAD_DIM] = turned.astype(jnp.bfloat16)
    projected_ref[:, wide + HEAD_DIM :] = total[:, HEAD_DIM:].astype(jnp.bfloat16)
    for here in hidden_tiles(out_ref.shape[1], 512):
        out_ref[:, here] = last_dims(projected_ref[...], weight_ref[here, :]).astype(jnp.bfloat16)


def project_back(queries, own, last, cosine, sine, weight):
    rows = queries.shape[0]
    return pl.pallas_call(
        project_back_kernel,
        out_shape=(
            jax.ShapeDtypeStruct((rows, weight.shape[1]), jnp.bfloat16),
            jax.ShapeDtypeStruct((rows, weight.shape[0]), jnp.bfloat16),
        ),
        in_specs=in_vmem(6),
        out_specs=tuple(in_vmem(2)),
        **kernel_options(24),
    )(queries, own, last, cosine, sine, weight)


def finish_kernel(first_ref, second_ref, own_ref, tokens_ref, grad_ref, out_ref):
    weighted = (
        first_ref[...].astype(jnp.float32)
        + second_ref[...].astype(jnp.float32)
        + own_ref[...].astype(jnp.float32)
    )
    inputs = tokens_ref[...].astype(jnp.float32)
    scale = lax.rsqrt(jnp.mean(inputs * inputs, axis=-1, keepdims=True) + EPSILON)
    inner_mean = jnp.mean(weighted * inputs, axis=-1, keepdims=True)
    out_ref[...] = grad_ref[...] + scale * weighted - inputs * (scale * scale * scale * inner_mean)


def finish(first, second, own, tokens, grads):
    return pl.pallas_call(
        finish_kernel,
        out_shape=jax.ShapeDtypeStruct(grads.shape, jnp.float32),
        in_specs=in_vmem(5),
        out_specs=pl.BlockSpec(memory_space=pltpu.VMEM),
        **kernel_options(16),
    )(first, second, own, tokens, grads)


def slot_kernel(experts, index_ref, first_ref, routes_ref, chosen_ref, back_ref):
    length = routes_ref.shape[2]
    capacity = chosen_ref.shape[1] // experts
    earlier = lax.broadcasted_iota(jnp.int32, (length, length), 0)
    earlier = earlier < lax.broadcasted_iota(jnp.int32, (length, length), 1)
    earlier = jnp.where(earlier, 1.0, 0.0).astype(jnp.bfloat16)
    slot = lax.broadcasted_iota(jnp.int32, (capacity, length), 0).astype(jnp.float32)
    for block in range(chosen_ref.shape[0]):
        routes = routes_ref[index_ref[block]]
        for expert in range(experts):
            same = jnp.where(routes == first_ref[0] + expert, 1.0, 0.0)
            member = jnp.sum(same, axis=0, keepdims=True)
            wide = jnp.broadcast_to(member, (16, length)).astype(jnp.bfloat16)
            place = plain_dot(wide, earlier)[:1]
            chosen = jnp.where(place == slot, member, 0.0)
            rows = slice(expert * capacity, (expert + 1) * capacity)
            chosen_ref[block, rows, :] = chosen.astype(jnp.bfloat16)
            back_ref[block, :, rows] = chosen.T.astype(jnp.bfloat16)


def slots_of(index, first_expert, routes, experts, capacity):
    blocks, _, length = routes.shape
    return pl.pallas_call(
        functools.partial(slot_kernel, experts),
        out_shape=(
            jax.ShapeDtypeStruct((blocks, experts * capacity, length), jnp.bfloat16),
            jax.ShapeDtypeStruct((blocks, length, experts * capacity), jnp.bfloat16),
        ),
        in_specs=in_smem(2) + in_vmem(1),
        out_specs=tuple(in_vmem(2)),
        **kernel_options(20),
    )(index, first_expert.reshape(1), routes)


def router_kernel(experts, first_ref, normed_ref, router_ref, chosen_ref, probs_ref, gate_ref):
    logits = last_dims(normed_ref[...], router_ref[...])
    powers = jnp.exp(logits - jnp.max(logits, axis=-1, keepdims=True))
    probs = powers / jnp.sum(powers, axis=-1, keepdims=True)
    probs_ref[...] = probs
    length = chosen_ref.shape[2]
    capacity = chosen_ref.shape[1] // experts
    lane = lax.broadcasted_iota(jnp.int32, (capacity, probs.shape[1]), 1)
    for block in range(chosen_ref.shape[0]):
        taken = jnp.dot(
            chosen_ref[block].astype(jnp.float32),
            probs[block * length : (block + 1) * length],
            precision=lax.Precision.HIGHEST,
            preferred_element_type=jnp.float32,
        )
        for expert in range(experts):
            own = taken[expert * capacity : (expert + 1) * capacity]
            own = jnp.where(lane == first_ref[0] + expert, own, 0.0)
            gate_ref[expert, block * capacity : (block + 1) * capacity, :] = jnp.sum(
                own, axis=1, keepdims=True
            )


def route(first_expert, normed, router, chosen, experts):
    blocks, slots, _ = chosen.shape
    return pl.pallas_call(
        functools.partial(router_kernel, experts),
        out_shape=(
            jax.ShapeDtypeStruct((normed.shape[0], router.shape[0]), jnp.float32),
            jax.ShapeDtypeStruct((experts, blocks * (slots // experts), 1), jnp.float32),
        ),
        in_specs=in_smem(1) + in_vmem(3),
        out_specs=tuple(in_vmem(2)),
        **kernel_options(20),
    )(first_expert.reshape(1), normed, router, chosen)


def body(
    tokens,
    attn_gain,
    query_key_value_weight,
    out_weight,
    ffn_gain,
    router_weight,
    shared_gate,
    shared_up,
    shared_down,
    routed_gate_weight,
    routed_up_weight,
    routed_down_weight,
    routes,
    cotangent,
):
    f32 = jnp.float32
    bf16 = jnp.bfloat16
    both = CONTEXT + ("experts",)
    context_count = context_size()
    spread = lax.axis_size("experts")
    context_index = lax.axis_index(CONTEXT)
    expert_index = lax.axis_index("experts")
    token_count, width = tokens.shape
    local_experts = routed_gate_weight.shape[0]
    experts_all = local_experts * spread
    rows = token_count * spread
    weight_rows = query_key_value_weight.shape[0]
    query_width = QUERY_HEADS * HEAD_DIM
    key_width = KEY_VALUE_HEADS * HEAD_DIM
    repeat_times = spread // KEY_VALUE_HEADS
    head_share = QUERY_HEADS // spread
    own_width = head_share * HEAD_DIM
    block_width = width // context_count

    def key_columns(weight):
        heads = weight.reshape(weight_rows, KEY_VALUE_HEADS, HEAD_DIM)
        return jnp.repeat(heads, repeat_times, axis=1)

    own_gain = attn_gain.astype(f32)[:, None]
    qkv_scaled = (query_key_value_weight.astype(f32) * own_gain).astype(bf16)
    qkv_send = jnp.concatenate(
        [
            qkv_scaled[:, :query_width].reshape(weight_rows, spread, own_width),
            key_columns(qkv_scaled[:, query_width : query_width + key_width]),
            key_columns(qkv_scaled[:, query_width + key_width :]),
        ],
        axis=2,
    ).transpose(1, 0, 2)
    hidden_piece = shared_down.shape[0]
    hidden_own = hidden_piece * context_count
    hidden_wide = -(-hidden_own // HEAD_DIM) * HEAD_DIM

    shared_send = hidden_send(
        shared_gate, shared_up, hidden_own, hidden_wide, context_count, spread
    )

    token_ring = RingGather(tokens)
    token_ring.step()
    position = context_index * rows + jnp.arange(rows, dtype=jnp.int32)
    position = ring_order(position.reshape(spread, token_count)).reshape(rows).astype(f32)
    half_width = HEAD_DIM // 2
    frequency = THETA ** (-jnp.arange(half_width, dtype=f32) * 2.0 / HEAD_DIM)
    angles = position[:, None] * frequency[None, :]
    cosine = jnp.cos(angles)
    sine = jnp.sin(angles)
    cosine = jnp.concatenate([cosine, cosine], axis=1)
    sine = jnp.concatenate([-sine, sine], axis=1)
    small = jnp.concatenate([ffn_gain[None], router_weight.T], axis=0)
    small = flip_double(small[None], CONTEXT)
    qkv_send = after(small, qkv_send)
    qkv_rows = to_experts(qkv_send).reshape(spread * weight_rows, -1)
    while small.shape[0] < context_count:
        small = flip_double(small, CONTEXT)
    small = jnp.concatenate([small.reshape(1, -1), routes.astype(bf16).reshape(1, -1)], axis=1)
    small, cosine, sine = meet([token_ring], small, cosine, sine)
    token_ring.step()
    (qkv_rows,) = meet([token_ring], qkv_rows)
    token_ring.step()
    qkv_far = far_gather(qkv_rows)
    qkv_far, out_weight = meet([token_ring], qkv_far, out_weight)
    token_ring.step()
    qkv_own = core_gather(qkv_far)
    (qkv_own,) = meet([token_ring], qkv_own)
    small = after(token_ring.latest(), small)

    out_full = lax.all_gather(out_weight, both, axis=0, tiled=True)
    normed_one, query_rows, key_value = project(
        token_ring.pieces(), qkv_own, cosine, sine, own_width
    )
    key_value = far_gather(key_value)
    small = flip_double(small, "experts")
    key_value, small = lax.optimization_barrier((key_value, small))
    key_value = core_gather(key_value)
    small = flip_double(small, "experts")
    place = ring_place(expert_index, spread)
    order = (ring_place(jnp.arange(spread, dtype=jnp.int32), spread) - place + spread) % spread
    attended, attended_low, log_total = attention_forward(
        context_index, order, query_rows, key_value
    )
    attended_low, small = lax.optimization_barrier((attended_low, small))
    attended_tok = (
        to_experts(attended_low.reshape(spread, token_count, own_width))
        .transpose(1, 0, 2)
        .reshape(token_count, query_width)
    )
    while small.shape[0] < spread:
        small = flip_double(small, "experts")
    attended_tok, small = lax.optimization_barrier((attended_tok, small))
    routes_block = small[:, -token_count * TOP :].reshape(spread, token_count, TOP)
    routes_block = routes_block.astype(jnp.int32).transpose(0, 2, 1)
    small = small[:, : -token_count * TOP].reshape(spread, context_count, -1, weight_rows)
    small = small.transpose(2, 1, 0, 3).reshape(-1, width)
    gain_two = small[0].astype(f32)
    router_full = small[1:]

    inputs = tokens.astype(f32)
    middle = inputs + jnp.dot(attended_tok, out_full, preferred_element_type=f32)
    scale_two = rms_scale(middle)
    normed_two = (middle * scale_two * gain_two).astype(bf16)
    normed_ring = RingGather(normed_two)
    normed_ring.step()
    routes_block, router_full, shared_down = meet(
        [normed_ring], routes_block, router_full, shared_down
    )

    normed_ring.step()
    down_far = far_gather(shared_down)
    first_expert = expert_index * local_experts
    capacity = token_count * TOP * 4 // (3 * experts_all)
    ring_blocks = ring_index(place + jnp.arange(spread, dtype=jnp.int32), spread)
    chosen_low, chosen_back = slots_of(
        ring_blocks, first_expert, routes_block, local_experts, capacity
    )
    down_far, chosen_low, chosen_back = meet([normed_ring], down_far, chosen_low, chosen_back)
    normed_ring.step()
    down_own = jnp.pad(core_gather(down_far), ((0, hidden_wide - hidden_own), (0, 0)))
    (down_own,) = meet([normed_ring], down_own)
    normed_ring.step()
    (cotangent_late,) = meet([normed_ring], cotangent)
    grad_ring = RingGather(cotangent_late)
    grad_ring.step()
    normed_block, expert_rows = dispatch(normed_ring.pieces(), chosen_low, local_experts)

    (normed_block,) = meet([grad_ring], normed_block)
    grad_ring.step()
    router_probs, gates = route(
        first_expert, normed_block, router_full, chosen_low, local_experts
    )
    expert_rows = after(gates, expert_rows)
    act, by_gate, by_up = expert_forward(expert_rows, routed_gate_weight, routed_up_weight)
    act, gates = meet([grad_ring], act, gates)
    grad_ring.step()
    weighted_y = expert_results(act, gates, routed_down_weight)
    (weighted_y,) = meet([grad_ring], weighted_y)
    grad_ring.step()
    chosen_low, shared_send = meet([grad_ring], chosen_low, shared_send)
    grad_block, grad_rows = dispatch(grad_ring.pieces(), chosen_low, local_experts)

    own_core = lax.axis_index("core")
    other_core = 1 - own_core
    shared_rows = to_experts(shared_send).reshape(spread * weight_rows, -1)
    down_parts = weight_parts(other_core, act, grad_rows, False, gates, wide=True)
    down_parts, shared_rows, attended_late = lax.optimization_barrier(
        (down_parts, shared_rows, attended_low)
    )
    shared_far = far_gather(shared_rows)
    down_received = core_swap(down_parts)
    heads_ring = RingGather(attended_late)
    heads_ring.step()
    grad_rows, gates = after(down_parts, grad_rows, gates)
    expert_dg, expert_du, row_grad = expert_backward(
        first_expert,
        grad_rows,
        gates,
        act,
        by_gate,
        by_up,
        routed_gate_weight,
        routed_up_weight,
        routed_down_weight,
    )
    row_grad, shared_far, down_received = meet(
        [heads_ring], row_grad, shared_far, down_received
    )
    heads_ring.step()
    shared_own = core_gather(shared_far)
    shared_act, shared_both = shared_pass(normed_block, grad_block, shared_own, down_own)
    shared_act, shared_both = meet([heads_ring], shared_act, shared_both)
    heads_ring.step()
    grad_part = combine(chosen_back, row_grad, shared_both, shared_own, True)
    grad_scatter = RingScatter(grad_part)
    grad_scatter.step()
    expert_dg, expert_du, weighted_y, act = after(
        grad_part, expert_dg, expert_du, weighted_y, act
    )
    down_parts = weight_parts(own_core, act, grad_rows, False, gates, down_received)
    (down_parts,) = meet([grad_scatter, heads_ring], down_parts)
    down_sum = chips_sum(down_parts)
    grad_scatter.step()
    heads_ring.step()
    expert_dg = after(down_parts, expert_dg)
    gate_parts = weight_parts(other_core, expert_rows, expert_dg, True)
    shared_parts = weight_parts(
        other_core, after(gate_parts, normed_block)[None], shared_both[None], True
    )
    gate_parts, shared_parts = meet([grad_scatter, heads_ring], gate_parts, shared_parts)
    grad_scatter.step()
    gate_received = core_swap(gate_parts)
    shared_received = core_swap(shared_parts)
    weighted_y = after(shared_parts, weighted_y)
    out_part = combine(chosen_back, weighted_y, shared_act, down_own, False)
    out_part, gate_received = lax.optimization_barrier((out_part, gate_received))
    gate_parts = weight_parts(own_core, expert_rows, expert_dg, True, None, gate_received)
    gate_parts, shared_received, out_part = meet(
        [grad_scatter], gate_parts, shared_received, out_part
    )
    grad_scatter.step()
    expert_du = after(gate_parts, expert_du)
    up_parts = weight_parts(other_core, expert_rows, expert_du, True)
    shared_parts = weight_parts(
        own_core,
        after(up_parts, normed_block)[None],
        shared_both[None],
        True,
        None,
        shared_received,
    )
    up_parts, shared_parts, out_part = meet([grad_scatter], up_parts, shared_parts, out_part)
    gathered = grad_scatter.total()
    out_scatter = RingScatter(out_part)
    out_scatter.step()
    shared_pair = chips_exchange(shared_parts)

    prob_grad = gathered[:, width : width + experts_all]
    probs_tok = router_probs[:token_count]
    logit_grad = (
        probs_tok * (prob_grad - jnp.sum(probs_tok * prob_grad, axis=-1, keepdims=True))
    ).astype(bf16)
    normed_grad = gathered[:, :width] + jnp.dot(
        logit_grad, router_full, preferred_element_type=f32
    )
    grad_final = cotangent.astype(f32)
    weighted = normed_grad * gain_two
    inner_mean = jnp.mean(weighted * middle, axis=-1, keepdims=True)
    middle_grad = (
        grad_final
        + scale_two * weighted
        - middle * scale_two * scale_two * scale_two * inner_mean
    )
    gain_rows = (normed_grad * middle * scale_two).astype(bf16)
    branch_grad = middle_grad.astype(bf16)
    attended_grad = dot_last(branch_grad, out_full).astype(bf16)
    (attended_grad,) = meet([out_scatter], attended_grad)
    grad_heads = to_experts(
        attended_grad.reshape(token_count, spread, own_width).transpose(1, 0, 2)
    ).reshape(rows, own_width)
    lane = jnp.arange(HEAD_DIM, dtype=jnp.int32)[None, :]
    gain_column = jnp.broadcast_to(lane == experts_all, (token_count, HEAD_DIM)).astype(bf16)
    small_left = jnp.concatenate([normed_two, gain_rows], axis=0)
    small_right = jnp.concatenate(
        [jnp.pad(logit_grad, ((0, 0), (0, HEAD_DIM - experts_all))), gain_column], axis=0
    )
    small_left, small_right, expert_du = after(attended_grad, small_left, small_right, expert_du)
    up_received = core_swap(up_parts)
    slices = 2 if block_width % (2 * HEAD_DIM) == 0 else 1
    up_parts = [
        weight_parts(own_core, expert_rows, expert_du, True, None, up_received, slices, number)
        for number in range(slices)
    ]
    small_parts = weight_parts(other_core, small_left[None], small_right[None], True)
    branch_late, up_parts = after(small_parts, branch_grad, up_parts)
    branch_columns = to_experts(
        branch_late.reshape(token_count, spread, own_width).transpose(1, 0, 2)
    ).reshape(rows, own_width)
    grad_heads, small_parts, up_parts = lax.optimization_barrier((grad_heads, small_parts, up_parts))

    out_scatter.step()
    small_received = core_swap(small_parts)
    query_grad, key_value_all = attention_backward(
        context_index,
        order,
        query_rows,
        key_value,
        attended,
        grad_heads,
        log_total,
        cosine,
        sine,
    )
    key_value_all, branch_columns, small_received, down_sum, shared_last = meet(
        [out_scatter], key_value_all, branch_columns, small_received, down_sum, shared_pair[1]
    )
    gate_sum = chips_sum(gate_parts)
    key_value_all = key_value_all.reshape(context_count, rows, -1)
    key_value_received = core_exchange(block_parts(key_value_all))
    key_value_sums = block_sums(key_value_all, key_value_received)
    (key_value_sums,) = lax.optimization_barrier((key_value_sums,))
    key_value_own, key_value_last = far_exchange(key_value_sums)
    out_scatter.first = after(key_value_sums, out_scatter.first)
    out_scatter.step()
    branch_columns, shared_last, small_left = after(
        key_value_sums, branch_columns, shared_last, small_left
    )
    index = ring_index(place + jnp.arange(spread, dtype=jnp.int32), spread)
    out_keep, out_send = output_weight(index, own_core, branch_columns, heads_ring.pieces())
    small_parts = weight_parts(
        own_core, small_left[None], small_right[None], True, None, small_received
    )
    shared_own_part = both_halves((shared_pair[0].astype(f32), shared_last)).astype(bf16)
    shared_back = to_experts(shared_own_part.reshape(spread, weight_rows, -1))
    key_value_last, out_keep, out_send, small_parts, gate_sum, shared_act = meet(
        [out_scatter], key_value_last, out_keep, out_send, small_parts, gate_sum, shared_act
    )
    up_first = chips_sum(up_parts[0])
    projected_grad, input_part = project_back(
        query_grad, key_value_own, key_value_last, cosine, sine, qkv_own
    )
    input_scatter = RingScatter(input_part)
    input_scatter.step()
    out_received = core_swap(out_send)
    normed_one = after(input_scatter.sent, normed_one)
    qkv_parts = weight_parts(other_core, normed_one[None], projected_grad[None], True)
    qkv_received = core_swap(qkv_parts)
    qkv_parts = weight_parts(
        own_core, normed_one[None], projected_grad[None], True, None, qkv_received
    )
    qkv_parts, out_received, shared_back = meet(
        [input_scatter, out_scatter], qkv_parts, out_received, shared_back
    )
    input_scatter.step()
    qkv_parts, out_received, shared_back, out_scatter.first = after(
        input_scatter.sent, qkv_parts, out_received, shared_back, out_scatter.first
    )
    out_scatter.step()
    out_sums = out_keep.astype(f32) + out_received.astype(f32)
    dense_parts = jnp.concatenate(
        [qkv_parts[:, 0], out_sums.astype(bf16), small_parts[:, 0]], axis=2
    )
    dense_pair = chips_exchange(dense_parts)
    down_sum, shared_act, shared_back = after(dense_parts, down_sum, shared_act, shared_back)
    shared_gate_grad, shared_up_grad = hidden_home(shared_back, hidden_own, context_count)
    expert_down_grad = widen(after(shared_gate_grad, down_sum))
    shared_down_sum = row_product(shared_act, after(expert_down_grad, grad_block), hidden_own)
    shared_down_sum = shared_down_sum.reshape(context_count, hidden_piece, width)
    shared_down_sum, shared_gate_grad = meet(
        [input_scatter, out_scatter], shared_down_sum, shared_gate_grad
    )
    input_scatter.step()
    gate_sum, shared_down_sum = after(input_scatter.sent, gate_sum, shared_down_sum)
    shared_down_received = core_exchange(block_parts(shared_down_sum))
    expert_gate_grad = widen(gate_sum)
    expert_gate_grad, dense_last, shared_down_received = meet(
        [input_scatter], expert_gate_grad, dense_pair[1], shared_down_received
    )
    input_scatter.step()
    up_later = [chips_sum(after((dense_last, up_first), part)) for part in up_parts[1:]]
    dense_last, out_scatter.first, shared_down_received = after(
        input_scatter.sent, dense_last, out_scatter.first, shared_down_received
    )
    dense_sum = both_halves((dense_pair[0].astype(f32), dense_last)).astype(bf16)
    dense_back = to_experts(dense_sum.reshape(spread, weight_rows, -1))
    shared_down_pair = far_exchange(block_sums(shared_down_sum, shared_down_received))
    dense_back, shared_down_pair = meet([input_scatter], dense_back, shared_down_pair)
    shared_down_grad = both_halves(shared_down_pair)
    layer_out = (middle + out_scatter.total()).astype(bf16)
    expert_up_grad = widen(up_first, *up_later)
    qkv_weight_grad, out_weight_grad, small_grad, attn_gain_grad = dense_home(
        dense_back, query_key_value_weight, own_gain, width
    )
    attn_gain_grad = attn_gain_grad[:, 0]
    router_weight_grad = small_grad[:, :experts_all]
    ffn_gain_grad = small_grad[:, experts_all]
    tokens_grad = finish(
        input_scatter.first, input_scatter.second, input_part[:token_count], tokens, middle_grad
    )
    return (
        layer_out,
        tokens_grad,
        attn_gain_grad,
        qkv_weight_grad,
        out_weight_grad,
        ffn_gain_grad,
        router_weight_grad,
        shared_gate_grad,
        shared_up_grad,
        shared_down_grad,
        expert_gate_grad,
        expert_up_grad,
        expert_down_grad,
    )


def solution(mesh):
    context_count, spread = mesh.devices.shape
    split = jax.sharding.Mesh(
        mesh.devices.reshape(context_count // 2, 2, spread), ("far", "core", "experts")
    )
    return jax.shard_map(
        body,
        mesh=split,
        in_specs=(
            P(("far", "core", "experts"), None),
            P(("far", "core", "experts")),
            P(("far", "core", "experts"), None),
            P(("far", "core", "experts"), None),
            P(("far", "core", "experts")),
            P(("far", "core", "experts"), None),
            P(("far", "core", "experts"), None),
            P(("far", "core", "experts"), None),
            P(("far", "core", "experts"), None),
            P("experts", None, None),
            P("experts", None, None),
            P("experts", None, None),
            P(("far", "core", "experts"), None),
            P(("far", "core", "experts"), None),
        ),
        out_specs=(
            P(("far", "core", "experts"), None),
            P(("far", "core", "experts"), None),
            P(("far", "core", "experts")),
            P(("far", "core", "experts"), None),
            P(("far", "core", "experts"), None),
            P(("far", "core", "experts")),
            P(("far", "core", "experts"), None),
            P(("far", "core", "experts"), None),
            P(("far", "core", "experts"), None),
            P(("far", "core", "experts"), None),
            P("experts", CONTEXT, None),
            P("experts", CONTEXT, None),
            P("experts", None, CONTEXT),
        ),
        check_vma=False,
    )
```
